32 devices in a mesh: dp: 32 (over z, y, x, core).
Axes of the slice: x: 2, y: 2, z: 4, core: 2. Of those that a mesh axis runs over, the one named last changes fastest.
Arguments:
- inputs: bfloat16 [64, 1024, 512], P('dp'), may hold values from -6 to 6
- lengths: int32 [64], P('dp'), may hold values from 128 to 1024, as said below
- memory: bfloat16 [20, 512], P(None, 'dp'), may hold values from -6 to 6
- query_weight: bfloat16 [512, 512], P('dp'), may hold values from -0.25 to 0.25
- query_bias: bfloat16 [512], P('dp'), may hold values from -3 to 3
- key_weight: bfloat16 [512, 512], P('dp'), may hold values from -0.25 to 0.25
- value_weight: bfloat16 [512, 512], P('dp'), may hold values from -0.25 to 0.25
- value_bias: bfloat16 [512], P('dp'), may hold values from -3 to 3
- output_weight: bfloat16 [512, 512], P('dp'), may hold values from -0.5 to 0.5
- output_bias: bfloat16 [512], P('dp'), may hold values from -3 to 3
- first_gain: bfloat16 [512], P('dp'), may hold values from 0.099609375 to 1.8984375
- first_shift: bfloat16 [512], P('dp'), may hold values from -1.75 to 1.75
- up_weight: bfloat16 [512, 2048], P('dp'), may hold values from -0.25 to 0.25
- up_bias: bfloat16 [2048], P('dp'), may hold values from -3 to 3
- down_weight: bfloat16 [2048, 512], P('dp'), may hold values from -0.125 to 0.125
- down_bias: bfloat16 [512], P('dp'), may hold values from -3 to 3
- second_gain: bfloat16 [512], P('dp'), may hold values from 0.099609375 to 1.8984375
- second_shift: bfloat16 [512], P('dp'), may hold values from -1.75 to 1.75
- cotangent: bfloat16 [64, 1024, 512], P('dp'), may hold values from -6 to 6
Outputs:
- layer_out: bfloat16 [64, 1024, 512], P('dp')
- input_grad: bfloat16 [64, 1024, 512], P('dp')
- memory_grad: float32 [20, 512], P(None, 'dp')
- query_weight_grad: float32 [512, 512], P('dp')
- query_bias_grad: float32 [512], P('dp')
- key_weight_grad: float32 [512, 512], P('dp')
- value_weight_grad: float32 [512, 512], P('dp')
- value_bias_grad: float32 [512], P('dp')
- output_weight_grad: float32 [512, 512], P('dp')
- output_bias_grad: float32 [512], P('dp')
- first_gain_grad: float32 [512], P('dp')
- first_shift_grad: float32 [512], P('dp')
- up_weight_grad: float32 [512, 2048], P('dp')
- up_bias_grad: float32 [2048], P('dp')
- down_weight_grad: float32 [2048, 512], P('dp')
- down_bias_grad: float32 [512], P('dp')
- second_gain_grad: float32 [512], P('dp')
- second_shift_grad: float32 [512], P('dp')
The draws below stay inside these ranges and needn't reach their ends.
Inputs may be any that keep to these rules, and one draw needn't show every extreme that they name: `lengths`: the number of real tokens of each sequence; later slots are padding that no query attends to, memory tokens are always visible, and some sequence has all 1024 tokens real.
All inputs are finite; a program needn't handle non-finite values.
Results may differ from the reference program's by a relative error of at most 0.013.
Values may be sent and summed in bfloat16 or wider, within the bound.
A program may use at most 256 MiB of HBM per device.

```python
import jax
import jax.numpy as jnp
from jax import lax

D = 512
HEADS = 8
HEAD_DIM = 64
FF = 2048
MEM = 20
LEN = 1024
NSEQ = 64


def draw_lengths(key, part):
    key = jax.random.fold_in(key, 7)
    keys_split = jax.random.split(key, 3)
    values = jax.random.randint(keys_split[0], (NSEQ,), LEN // 8, LEN + 1)
    first = jax.random.randint(keys_split[1], (), 0, NSEQ)
    second = (first + 1 + jax.random.randint(keys_split[2], (), 0, NSEQ - 1)) % NSEQ
    values = values.at[first].set(LEN).at[second].set(LEN // 8)
    return values.astype(jnp.int32)


def shard_levels(stream_key, dims, shards, least, high):
    level = 1.0
    for axis_at, parts in shards:
        draws = jax.random.uniform(jax.random.fold_in(jax.random.fold_in(stream_key, 6), axis_at), (parts,), jnp.float32, least / len(shards), high / len(shards))
        level = level * jnp.repeat(jnp.exp(draws), dims[axis_at] // parts).reshape((-1,) + (1,) * (len(dims) - 1 - axis_at))
    return level


def normal_values(key, dims, width, limit, cuts=(), dtype=jnp.bfloat16):
    level = shard_levels(key, dims, cuts, -0.22, 0.18) if cuts else 1.0
    values = jax.random.normal(key, dims, jnp.float32) * width * level
    return jnp.minimum(jnp.maximum(values, -limit), limit).astype(dtype)


def setup_inputs(seed: int = 0) -> dict:
    arg_keys = jax.random.split(jax.random.key(seed), 20)
    inputs = normal_values(arg_keys[0], (NSEQ, LEN, D), 1.0, 6.0, ((0, 32),))
    lengths = draw_lengths(jax.random.fold_in(arg_keys[19], 71), 0)
    memory = normal_values(arg_keys[2], (MEM, D), 1.0, 6.0, ((1, 32),))
    query_weight = normal_values(arg_keys[3], (D, D), D ** -0.5, 0.25, ((0, 32),))
    query_bias = normal_values(arg_keys[4], (D,), 0.5, 3.0, ((0, 32),))
    key_weight = normal_values(arg_keys[5], (D, D), D ** -0.5, 0.25, ((0, 32),))
    value_weight = normal_values(arg_keys[6], (D, D), D ** -0.5, 0.25, ((0, 32),))
    value_bias = normal_values(arg_keys[7], (D,), 0.5, 3.0, ((0, 32),))
    output_weight = normal_values(arg_keys[8], (D, D), (D // 4) ** -0.5, 0.5, ((0, 32),))
    output_bias = normal_values(arg_keys[9], (D,), 0.5, 3.0, ((0, 32),))
    first_gain = jnp.clip(1.0 + 0.18 * jax.random.normal(arg_keys[10], (D,), jnp.float32), 0.099609375, 1.8984375).astype(jnp.bfloat16)
    first_shift = normal_values(arg_keys[11], (D,), 0.3, 1.75, ((0, 32),))
    up_weight = normal_values(arg_keys[12], (D, FF), D ** -0.5, 0.25, ((0, 32),))
    up_bias = normal_values(arg_keys[13], (FF,), 0.5, 3.0, ((0, 32),))
    down_weight = normal_values(arg_keys[14], (FF, D), FF ** -0.5, 0.125, ((0, 32),))
    down_bias = normal_values(arg_keys[15], (D,), 0.5, 3.0, ((0, 32),))
    second_gain = jnp.clip(1.0 + 0.18 * jax.random.normal(arg_keys[16], (D,), jnp.float32), 0.099609375, 1.8984375).astype(jnp.bfloat16)
    second_shift = normal_values(arg_keys[17], (D,), 0.3, 1.75, ((0, 32),))
    cotangent = normal_values(arg_keys[18], (NSEQ, LEN, D), 1.0, 6.0, ((0, 32),))
    return {"inputs": inputs, "lengths": lengths, "memory": memory, "query_weight": query_weight, "query_bias": query_bias, "key_weight": key_weight, "value_weight": value_weight, "value_bias": value_bias, "output_weight": output_weight, "output_bias": output_bias, "first_gain": first_gain, "first_shift": first_shift, "up_weight": up_weight, "up_bias": up_bias, "down_weight": down_weight, "down_bias": down_bias, "second_gain": second_gain, "second_shift": second_shift, "cotangent": cotangent}


@jax.custom_vjp
def low(v):
    return lax.optimization_barrier(v.astype(jnp.bfloat16)).astype(jnp.float32)

@jax.custom_vjp
def low_back(v):
    return v

def low_keep(v):
    return (low(v), None)

def low_pass(kept, grad):
    return (grad,)

def back_keep(v):
    return (v, None)

def back_low(kept, grad):
    return (low(grad),)
low.defvjp(low_keep, low_pass)
low_back.defvjp(back_keep, back_low)
HIGH = lax.Precision.HIGHEST

def matmul(left, right):
    return jnp.dot(left, right, precision=HIGH)

def layer_norm(value, gain, shift):
    center = value - lax.optimization_barrier(jnp.mean(value, -1, keepdims=True))
    inverse = lax.rsqrt(lax.optimization_barrier(jnp.mean(center * center, -1, keepdims=True)) + 1e-05)
    return center * inverse * gain + shift

def layer_one(params, tokens, length):
    memory, query_weight, query_bias, key_weight, value_weight, value_bias, output_weight, output_bias, first_gain, first_shift, up_weight, up_bias, down_weight, down_bias, second_gain, second_shift = params
    rows = tokens.shape[0]
    joined = jnp.concatenate([memory, tokens], 0)
    total_keys = joined.shape[0]
    scale = HEAD_DIM ** (-0.5)
    queries = low(low_back((matmul(tokens, query_weight) + query_bias) * scale)).reshape(rows, HEADS, HEAD_DIM)
    keyed = low(low_back(matmul(joined, key_weight))).reshape(total_keys, HEADS, HEAD_DIM)
    valued = low(low_back(matmul(joined, value_weight) + value_bias)).reshape(total_keys, HEADS, HEAD_DIM)
    scores = low_back(jnp.einsum('qhd,khd->hqk', queries, keyed, precision=HIGH))
    visible = jnp.arange(total_keys) < MEM + length
    scores = jnp.where(visible[None, None, :], scores, -1e+30)
    top = lax.optimization_barrier(jnp.max(scores, -1, keepdims=True))
    expo = jnp.exp(scores - top)
    probs = low(expo / lax.optimization_barrier(jnp.sum(expo, -1, keepdims=True)))
    attended = jnp.einsum('hqk,khd->qhd', probs, valued, precision=HIGH).reshape(rows, HEADS * HEAD_DIM)
    attended = low(low_back(attended))
    branch = low_back(matmul(attended, output_weight) + output_bias)
    hidden = layer_norm(tokens + branch, first_gain, first_shift)
    inner = low_back(matmul(low(hidden), up_weight) + up_bias)
    acted = low(jax.nn.gelu(inner))
    outer = low_back(matmul(acted, down_weight) + down_bias)
    return layer_norm(hidden + outer, second_gain, second_shift)

def reference(inputs, lengths, memory, query_weight, query_bias, key_weight, value_weight, value_bias, output_weight, output_bias, first_gain, first_shift, up_weight, up_bias, down_weight, down_bias, second_gain, second_shift, cotangent):
    params = tuple((p.astype(jnp.float32) for p in (memory, query_weight, query_bias, key_weight, value_weight, value_bias, output_weight, output_bias, first_gain, first_shift, up_weight, up_bias, down_weight, down_bias, second_gain, second_shift)))

    def step(totals, item):
        tokens, length, grad_out = item
        result, pull = jax.vjp(lambda prm, tok: layer_one(prm, tok, length), params, tokens.astype(jnp.float32))
        param_grads, token_grad = pull(grad_out.astype(jnp.float32))
        totals = jax.tree.map(lambda acc, new: acc + new, totals, param_grads)
        return (totals, (result.astype(jnp.bfloat16), token_grad.astype(jnp.bfloat16)))
    zeros = jax.tree.map(jnp.zeros_like, params)
    totals, (outputs, input_grads) = lax.scan(step, zeros, (inputs, lengths, cotangent))
    return (outputs, input_grads, totals[0], totals[1], totals[2], totals[3], totals[4], totals[5], totals[6], totals[7], totals[8], totals[9], totals[10], totals[11], totals[12], totals[13], totals[14], totals[15])
```

```python
import functools

import jax
import jax.numpy as jnp
from jax import lax
from jax.experimental import pallas as pl
from jax.experimental.pallas import tpu as pltpu
from jax.sharding import PartitionSpec as P

HEADS = 8
HEAD_DIM = 64
EPSILON = 1e-05
LOG2E = 1.4426950408889634
LN2 = 0.6931471805599453
GELU_A = 0.7978845608028654
GELU_B = GELU_A * 0.044715
HIDE = -1e30
KEY_PAD = 32

f32 = jnp.float32
bf16 = jnp.bfloat16
VMEM = pltpu.VMEM
MESH = pl.DeviceIdType.MESH
NN = (((1,), (0,)), ((), ()))
NT = (((1,), (1,)), ((), ()))
TN = (((0,), (0,)), ((), ()))


def dg(left, right, dims):
    return lax.dot_general(left, right, dims, preferred_element_type=f32)


def col_sum(value):
    return jnp.sum(value, 0, keepdims=True)


class Cube:
    def __init__(self, count, sub):
        self.count, self.sub = count, sub
        self.nb = count.bit_length() - 1
        device = lax.axis_index("dp")
        self.device = device
        me = device // sub
        self.bits = [(me // (2**b)) % 2 for b in range(self.nb)]
        self.msb_first = tuple(range(self.nb - 1, -1, -1))

    def partner(self, b):
        return (self.device + (1 - 2 * self.bits[b]) * (2**b * self.sub),)

    def barrier(self):
        sem = pltpu.get_barrier_semaphore()
        for b in range(self.nb):
            pl.semaphore_signal(sem, inc=1, device_id=self.partner(b), device_id_type=MESH)
        pl.semaphore_wait(sem, self.nb)

    def own(self):
        return tuple(self.bits[b] for b in self.msb_first)


def orders(nb):
    if nb >= 4:
        far = list(range(nb - 1, 2, -1))
        return (far + [1, 2, 0], far + [2, 1, 0])
    return (list(range(nb - 1, -1, -1)),) * 2


def gather_copy(cube, ref, order, step, rows, lanes, send, recv):
    b = order[step]
    done = set(order[:step])
    idx = tuple(slice(None) if c in done else cube.bits[c] for c in cube.msb_first)
    view = ref.at[idx + (rows, lanes)]
    return pltpu.make_async_remote_copy(
        src_ref=view,
        dst_ref=view,
        send_sem=send,
        recv_sem=recv,
        device_id=cube.partner(b),
        device_id_type=MESH,
    )


class Scatter:
    def __init__(self, cube, source, lanes, order, bufs, send, recv):
        self.cube, self.source, self.lanes, self.order = cube, source, lanes, order
        self.bufs, self.send, self.recv = bufs, send, recv

    def _half(self, step, mine):
        cube, b = self.cube, self.order[step]
        left = [c for c in cube.msb_first if c not in self.order[:step]]
        bit = cube.bits[b] if mine else 1 - cube.bits[b]
        idx = tuple(bit if c == b else slice(None) for c in left)
        if step == 0:
            return self.source, idx + (slice(None), self.lanes)
        return self.bufs[step - 1], idx

    def copy(self, step):
        ref, idx = self._half(step, False)
        return pltpu.make_async_remote_copy(
            src_ref=ref.at[idx],
            dst_ref=self.bufs[step],
            send_sem=self.send.at[step],
            recv_sem=self.recv.at[step],
            device_id=self.cube.partner(self.order[step]),
            device_id_type=MESH,
        )

    def add(self, step, f32_result=False):
        ref, idx = self._half(step, True)
        into = self.bufs[step]
        free = self.cube.nb - 1 - step
        if f32_result:
            return into[...].astype(f32) + ref[idx].astype(f32)
        at = self.cube.bits[self.order[step]]
        left = [c for c in self.cube.msb_first if c not in self.order[:step]]
        where = left.index(self.order[step])
        for flat in range(2**free):
            sub = tuple((flat >> (free - 1 - k)) & 1 for k in range(free))
            full = sub[:where] + (at,) + sub[where:]
            if step == 0:
                full = full + (slice(None), self.lanes)
            into[sub] = (into[sub].astype(f32) + ref[full].astype(f32)).astype(into.dtype)
        return None


def attend_kernel(
    count, sub, mem_rows,
    len_ref, x_ref, wq_ref, wk_ref, wv_ref, wo_ref, wu_ref, wd_ref, small_ref,
    q_o, k_o, v_o, qt_o, att_o, g1, g2, vec_o, ub_o, mem_o,
    gs, ksel, vt_s, score_a, score_b, top_a, top_b,
    local, send1, recv1, send2, recv2, send3, recv3,
):
    cube = Cube(count, sub)
    nb = cube.nb
    seqs, length, width = x_ref.shape
    keys = k_o.shape[1]
    mem_pad = keys - length
    r = wq_ref.shape[0]
    ff = wu_ref.shape[1]
    cols = ff // width
    fr = wd_ref.shape[0]
    own = cube.own()
    ways = orders(nb)
    half = width // 2
    halves = (slice(0, half), slice(half, width))
    whole = (slice(None), slice(None))
    for j, ref in enumerate((wq_ref, wk_ref, wv_ref)):
        g1[own + (slice(j * r, j * r + r), slice(None))] = ref[...]
    gs[own + whole] = small_ref[...]
    parts = [(wo_ref, slice(0, r))]
    parts += [
        (wu_ref.at[:, c * width : (c + 1) * width], slice(r + c * r, r + c * r + r))
        for c in range(cols)
    ]
    parts += [(wd_ref, slice(r + cols * r, r + cols * r + fr))]
    moves = [
        pltpu.make_async_copy(ref, g2.at[own + (rows, slice(None))], local.at[j])
        for j, (ref, rows) in enumerate(parts)
    ]
    for move in moves:
        move.start()
    cube.barrier()

    def first(step):
        copies = [
            gather_copy(
                cube, g1, ways[k], step, slice(None), halves[k], send1.at[k, step], recv1.at[k, step]
            )
            for k in range(2)
        ]
        return copies + [
            gather_copy(
                cube, gs, ways[0], step, slice(None), slice(None), send3.at[step], recv3.at[step]
            )
        ]

    def second(step):
        return [
            gather_copy(
                cube, g2, ways[k], step, slice(None), halves[k], send2.at[k, step], recv2.at[k, step]
            )
            for k in range(2)
        ]

    for step in range(nb):
        copies = first(step)
        for copy in copies:
            copy.start()
        if step == 0:
            for move in moves:
                move.wait()
        if step == nb - 1:
            for copy in second(0):
                copy.start()
        for copy in copies:
            copy.wait()

    lane = lax.broadcasted_iota(jnp.int32, (1, 128), 1)
    groups = width // 128
    per = 128 // r
    upper = [jnp.zeros((16, 128), f32) for _ in range(groups)]
    lower = [jnp.zeros((16, 128), f32) for _ in range(groups)]
    vecs = [jnp.zeros((16, 128), f32) for _ in range(groups)]
    ups = [jnp.zeros((16, 128), f32) for _ in range(ff // 128)]
    for i in range(count):
        at = tuple((i >> b) & 1 for b in cube.msb_first)
        block = gs[at + whole].astype(f32)
        to = (i % per) * r
        g = i // per
        here = (lane >= to) & (lane < to + r)
        upper[g] = upper[g] + jnp.where(here, pltpu.roll(block, to % 128, 1), 0.0)
        lower[g] = lower[g] + jnp.where(here, pltpu.roll(block, (to - r) % 128, 1), 0.0)
        vecs[g] = vecs[g] + jnp.where(here, pltpu.roll(block, (to - 2 * r) % 128, 1), 0.0)
        to = (i * fr) % 128
        g = (i * fr) // 128
        here = (lane >= to) & (lane < to + fr)
        ups[g] = ups[g] + jnp.where(here, pltpu.roll(block, (to - 3 * r) % 128, 1), 0.0)
    for g in range(groups):
        at = slice(128 * g, 128 * g + 128)
        mem_o[0:16, at] = upper[g].astype(bf16)
        mem_o[16:32, at] = lower[g].astype(bf16)
        vec_o[:, at] = vecs[g]
    for g in range(ff // 128):
        ub_o[:, 128 * g : 128 * g + 128] = ups[g][0:1, :]

    def weight(j):
        return g1[(slice(None),) * nb + (slice(j * r, j * r + r), slice(None))].reshape(width, width)

    bq = vec_o[0:1, :]
    bv = vec_o[1:2, :]

    def put_keys(s, rows, kk, vv, bias):
        kb = kk.astype(bf16)
        vb = vv.astype(bf16)
        k_o[s, rows, :] = kb
        v_o[s, rows, :] = vb
        for h in range(HEADS):
            p, o = h // 2, 64 * (1 - h % 2)
            pattern = jnp.where(
                lane == o, bias, jnp.where((lane > o) & (lane <= o + 3), 1.0, 0.0)
            ).astype(bf16)
            mine = (lane < 64) if h % 2 == 0 else (lane >= 64)
            ksel[s, h, rows, :] = jnp.where(mine, kb[:, 128 * p : 128 * p + 128], pattern)
        vt = vb.T
        for h in range(HEADS):
            vt_s[s, h, 0:64, rows] = vt[64 * h : 64 * h + 64, :]

    top_row = lax.broadcasted_iota(jnp.int32, (16, keys), 0)
    ones = jnp.where(top_row == 0, 1.0, 0.0).astype(bf16)
    for s in range(seqs):
        for h in range(HEADS):
            vt_s[s, h, 64:80, :] = ones
    mem = mem_o[...]
    mem_keys = dg(mem, weight(1), NN)
    mem_values = dg(mem, weight(2), NN) + bv
    mem_row = lax.broadcasted_iota(jnp.int32, (mem_pad, 1), 0)
    for s in range(seqs):
        put_keys(
            s, slice(length, keys), mem_keys, mem_values, jnp.where(mem_row < mem_rows, 0.0, HIDE)
        )
    tile = 512
    tiles = length // tile
    aux = jnp.where(lax.broadcasted_iota(jnp.int32, (64, tile), 0) == 0, 1.0, 0.0).astype(bf16)

    @pl.loop(0, seqs * tiles)
    def _(i):
        s = i // tiles
        start = pl.multiple_of((i % tiles) * tile, tile)
        rows = pl.ds(start, tile)
        xt = x_ref[s, rows, :]
        qb = ((dg(xt, weight(0), NN) + bq) * (LOG2E * HEAD_DIM**-0.5)).astype(bf16)
        q_o[s, rows, :] = qb
        qt = qb.T
        for h in range(HEADS):
            e = h % 2
            qt_o[s, h, 64 * e : 64 * e + 64, rows] = qt[64 * h : 64 * h + 64, :]
            qt_o[s, h, 64 * (1 - e) : 64 * (1 - e) + 64, rows] = aux
        row = lax.broadcasted_iota(jnp.int32, (tile, 1), 0) + start
        put_keys(
            s,
            rows,
            dg(xt, weight(1), NN),
            dg(xt, weight(2), NN) + bv,
            jnp.where(row < len_ref[s], 0.0, HIDE),
        )

    block = score_a.shape[1]
    per_head = length // block
    blocks = seqs * HEADS * per_head

    def place(i):
        s = i // (HEADS * per_head)
        h = (i // per_head) % HEADS
        return s, h, pl.ds(pl.multiple_of((i % per_head) * block, block), block)

    def scores(i, score, top):
        s, h, at = place(i)
        value = dg(ksel[s, h], qt_o[s, h, :, at], NN)
        score[...] = value
        top[...] = jnp.max(value, 0, keepdims=True)

    def mix(i, score, top):
        s, h, at = place(i)
        peak = top[...]
        probs = jnp.exp2(score[...] - peak).astype(bf16)
        mixed = dg(vt_s[s, h], probs, NN)
        total = mixed[64:65, :]
        att_o[s, h, :, at] = (mixed[0:64, :] / total).astype(bf16)
        stat = peak + jnp.log2(total)
        hi = stat.astype(bf16).astype(f32)
        mid = (stat - hi).astype(bf16).astype(f32)
        low = stat - hi - mid
        row = lax.broadcasted_iota(jnp.int32, (16, block), 0)
        extra = jnp.where(
            row == 0,
            1.0,
            jnp.where(row == 1, -hi, jnp.where(row == 2, -mid, jnp.where(row == 3, -low, 0.0))),
        )
        o = pl.multiple_of(64 * (1 - h % 2), 64)
        qt_o[s, h, pl.ds(o, 16), at] = extra.astype(bf16)

    scores(0, score_a, top_a)
    turns = blocks // 2

    @pl.loop(0, turns)
    def _(j):
        for step in range(1, nb):

            @pl.when(j == (step * turns) // nb)
            def _():
                for copy in second(step - 1):
                    copy.wait()
                for copy in second(step):
                    copy.start()

        scores(2 * j + 1, score_b, top_b)
        mix(2 * j, score_a, top_a)
        scores(jnp.minimum(2 * j + 2, blocks - 1), score_a, top_a)
        mix(2 * j + 1, score_b, top_b)

    for copy in second(nb - 1):
        copy.wait()


def attend_call(count, sub, lengths, x, wq, wk, wv, wo, wu, wd, small, mem_rows):
    seqs, length, width = x.shape
    r, ff, fr = wq.shape[0], wu.shape[1], wd.shape[0]
    rows2 = r + (ff // width) * r + fr
    keys = length + KEY_PAD
    nb = count.bit_length() - 1
    cube = (2,) * nb
    block = min(512, length)
    shape = jax.ShapeDtypeStruct
    vm = pl.BlockSpec(memory_space=VMEM)
    dma = pltpu.SemaphoreType.DMA
    return pl.pallas_call(
        functools.partial(attend_kernel, count, sub, mem_rows),
        out_shape=(
            shape((seqs, length, width), bf16),
            shape((seqs, keys, width), bf16),
            shape((seqs, keys, width), bf16),
            shape((seqs, HEADS, 128, length), bf16),
            shape((seqs, HEADS, HEAD_DIM, length), bf16),
            shape(cube + (3 * r, width), bf16),
            shape(cube + (rows2, width), bf16),
            shape((16, width), f32),
            shape((1, ff), f32),
            shape((KEY_PAD, width), bf16),
        ),
        in_specs=[pl.BlockSpec(memory_space=pltpu.SMEM)] + [vm] * 8,
        out_specs=[vm] * 6 + [pl.BlockSpec(memory_space=pl.ANY)] + [vm] * 3,
        scratch_shapes=[
            VMEM(cube + (16, 128), bf16),
            VMEM((seqs, HEADS, keys, 128), bf16),
            VMEM((seqs, HEADS, 80, keys), bf16),
            VMEM((keys, block), f32),
            VMEM((keys, block), f32),
            VMEM((1, block), f32),
            VMEM((1, block), f32),
            dma((2 + ff // width,)),
            dma((2, nb)),
            dma((2, nb)),
            dma((2, nb)),
            dma((2, nb)),
            dma((nb,)),
            dma((nb,)),
        ],
        compiler_params=pltpu.CompilerParams(
            collective_id=0, has_side_effects=True, vmem_limit_bytes=60 * 2**20
        ),
        name="attend",
    )(lengths, x, wq, wk, wv, wo, wu, wd, small)


def norm_forward(value, gain, shift):
    center = value - jnp.mean(value, -1, keepdims=True)
    inverse = lax.rsqrt(jnp.mean(center * center, -1, keepdims=True) + EPSILON)
    normed = center * inverse
    return normed * gain + shift, normed, inverse


def norm_backward(grad, normed, inverse, gain):
    scaled = grad * gain
    return inverse * (
        scaled
        - jnp.mean(scaled, -1, keepdims=True)
        - normed * jnp.mean(scaled * normed, -1, keepdims=True)
    )


def feed_kernel(
    r, fr, steps,
    x_ref, att_ref, dy_ref, g2, vec, ub,
    out_o, res_o, datt_o, part_o, gvec, gub,
    slope_s, act_s, gwo, gwu, gwd,
):
    i = pl.program_id(0)
    rows, width = x_ref.shape[1:]
    count = g2.shape[0]
    cols = g2.shape[1] // r - 1 - fr // r
    per = width // fr

    @pl.when(i == 0)
    def _():
        for ref in (gwo, gwu, gwd, gvec, gub):
            ref[...] = jnp.zeros_like(ref)

    bo, ga, sa, bd, gb, sb = [vec[j : j + 1, :] for j in range(2, 8)]

    def wo():
        return g2[:, 0:r, :].reshape(width, width)

    def wu(c):
        return g2[:, r + c * r : r + c * r + r, :].reshape(width, width)

    def wd(c):
        return g2[c * per : (c + 1) * per, r + cols * r :, :].reshape(width, width)

    att = att_ref[0]
    hidden, normed1, inverse1 = norm_forward(x_ref[0].astype(f32) + dg(att, wo(), TN) + bo, ga, sa)
    low = hidden.astype(bf16)
    outer = hidden + bd
    for c in range(cols):
        at = slice(c * width, (c + 1) * width)
        u = dg(low, wu(c), NN) + ub[:, at]
        u2 = u * u
        t = jnp.tanh(u * (GELU_A + GELU_B * u2))
        hu = 0.5 * u
        act = (hu + hu * t).astype(bf16)
        act_s[c] = act
        slope_s[c] = (
            (0.5 + 0.5 * t) + (hu * (1.0 - t * t)) * (GELU_A + 3.0 * GELU_B * u2)
        ).astype(bf16)
        outer = outer + dg(act, wd(c), NN)
    out, normed2, inverse2 = norm_forward(outer, gb, sb)
    out_o[0] = out.astype(bf16)
    dy = dy_ref[0].astype(f32)
    gvec[6:7, :] += col_sum(dy * normed2)
    gvec[7:8, :] += col_sum(dy)
    d_res2 = norm_backward(dy, normed2, inverse2, gb)
    d_outer = d_res2.astype(bf16)
    gvec[5:6, :] += col_sum(d_outer.astype(f32))
    d_hidden = d_res2
    for c in range(cols):
        at = slice(c * width, (c + 1) * width)
        d_act = dg(d_outer, wd(c), NT)
        d_inner = (d_act * slope_s[c].astype(f32)).astype(bf16)
        gwd[at, :] += dg(act_s[c], d_outer, TN)
        gwu[:, at] += dg(low, d_inner, TN)
        gub[:, at] += col_sum(d_inner.astype(f32))
        d_hidden = d_hidden + dg(d_inner, wu(c), NT)
    gvec[3:4, :] += col_sum(d_hidden * normed1)
    gvec[4:5, :] += col_sum(d_hidden)
    d_res1 = norm_backward(d_hidden, normed1, inverse1, ga)
    res_o[0] = d_res1
    d_branch = d_res1.astype(bf16)
    gvec[2:3, :] += col_sum(d_branch.astype(f32))
    gwo[...] += dg(att, d_branch, NN)
    datt_o[0] = dg(d_branch, wo(), NT).astype(bf16)

    @pl.when(i == steps - 1)
    def _():
        part_o[:, 0:r, :] = gwo[...].astype(bf16).reshape(count, r, width)
        for c in range(cols):
            part_o[:, r + c * r : r + c * r + r, :] = (
                gwu[:, c * width : (c + 1) * width].astype(bf16).reshape(count, r, width)
            )
        part_o[:, r + cols * r :, :] = gwd[...].astype(bf16).reshape(count, fr, width)


def feed_call(x, att, dy, g2, vec, ub, r, fr):
    seqs, length, width = x.shape
    ff = ub.shape[1]
    tile = min(512, length)
    tiles = length // tile
    shape = jax.ShapeDtypeStruct
    rows = pl.BlockSpec((1, tile, width), lambda i: (i // tiles, i % tiles, 0))

    def full(a):
        return pl.BlockSpec(a.shape, lambda i: (0,) * len(a.shape))

    outs = (
        shape((seqs, length, width), bf16),
        shape((seqs, length, width), f32),
        shape((seqs, length, width), bf16),
        shape(g2.shape, bf16),
        shape((8, width), f32),
        shape((1, ff), f32),
    )
    return pl.pallas_call(
        functools.partial(feed_kernel, r, fr, seqs * tiles),
        grid=(seqs * tiles,),
        out_shape=outs,
        in_specs=[
            rows,
            pl.BlockSpec((1, width, tile), lambda i: (i // tiles, 0, i % tiles)),
            rows,
            full(g2),
            full(vec),
            full(ub),
        ],
        out_specs=[rows, rows, rows] + [full(a) for a in outs[3:]],
        scratch_shapes=[
            VMEM((ff // width, tile, width), bf16),
            VMEM((ff // width, tile, width), bf16),
            VMEM((width, width), f32),
            VMEM((width, ff), f32),
            VMEM((ff, width), f32),
        ],
        compiler_params=pltpu.CompilerParams(vmem_limit_bytes=60 * 2**20),
        name="feed",
    )(x, att, dy, g2, vec, ub)


def pull_kernel(
    count, sub, mem_rows, r, fr,
    len_ref, x_ref, mem_ref, q_ref, k_ref, v_ref, qt_ref, att_ref, da_ref, res_ref, g1, part1,
    gvec_ref, gub_ref,
    dx_o, gwq_o, gwk_o, gwv_o, gwo_o, gwu_o, gwd_o, small_o,
    ksel, vsel, kt, dot_s, p_a, d_a, p_b, d_b, dq_s, dk_s, dv_s, dqt,
    dv_0, dv_1, dk_0, dk_1, part2, small_s, *rest,
):
    cube = Cube(count, sub)
    nb = cube.nb
    bufs = [rest[k * nb : (k + 1) * nb] for k in range(5)]
    send, recv = rest[5 * nb :]
    seqs, length, width = x_ref.shape
    keys = k_ref.shape[1]
    ff = gub_ref.shape[1]
    cols = ff // width
    half = width // 2
    halves = (slice(0, half), slice(half, width))
    ways = [list(reversed(order)) for order in orders(nb)]
    feeds = [
        Scatter(cube, part1, halves[k], ways[k], bufs[k], send.at[k], recv.at[k]) for k in range(2)
    ]
    heads = [
        Scatter(cube, part2, halves[k], ways[k], bufs[2 + k], send.at[2 + k], recv.at[2 + k])
        for k in range(2)
    ]
    smalls = [Scatter(cube, small_s, slice(None), ways[0], bufs[4], send.at[4], recv.at[4])]

    def start(group, step):
        for part in group:
            part.copy(step).start()

    def finish(group, step):
        for part in group:
            part.copy(step).wait()
        if step < nb - 1:
            for part in group:
                part.add(step)

    cube.barrier()
    start(feeds, 0)

    lane = lax.broadcasted_iota(jnp.int32, (1, 128), 1)
    key_row = lax.broadcasted_iota(jnp.int32, (keys, 1), 0)
    block = p_a.shape[1]
    per_head = length // block
    dv_t, dk_t = (dv_0, dv_1), (dk_0, dk_1)
    temp = ((p_a, d_a), (p_b, d_b))

    def pair(j):
        s = j // (HEADS // 2)
        p = j % (HEADS // 2)
        at = pl.ds(pl.multiple_of(128 * p, 128), 128)
        kp = k_ref[s, :, at]
        vp = v_ref[s, :, at]
        kt[...] = kp.T
        da = da_ref[s, :, at]
        dat = da.T
        seen = (key_row < len_ref[s]) | ((key_row >= length) & (key_row < length + mem_rows))
        bias = jnp.where(seen, 0.0, HIDE)
        for e in range(2):
            o = 64 * (1 - e)
            mine = (lane < 64) if e == 0 else (lane >= 64)
            pattern = jnp.where(
                lane == o, bias, jnp.where((lane > o) & (lane <= o + 3), 1.0, 0.0)
            ).astype(bf16)
            ksel[e] = jnp.where(mine, kp, pattern)
            vsel[e] = jnp.where(
                mine, vp, jnp.where((lane >= o) & (lane < o + 2), 1.0, 0.0).astype(bf16)
            )
            dt = dat[64 * e : 64 * e + 64, :]
            delta = col_sum(dt.astype(f32) * att_ref[s, 2 * p + e].astype(f32))
            hi = delta.astype(bf16).astype(f32)
            row = lax.broadcasted_iota(jnp.int32, (64, length), 0)
            dot_s[e, 64 * e : 64 * e + 64, :] = dt
            dot_s[e, o : o + 64, :] = jnp.where(
                row == 0, -hi, jnp.where(row == 1, hi - delta, 0.0)
            ).astype(bf16)

        def probs(b):
            e, c = b // per_head, b % per_head
            cut = slice(c * block, (c + 1) * block)
            prob = jnp.exp2(dg(ksel[e], qt_ref[s, 2 * p + e, :, cut], NN))
            grad = dg(vsel[e], dot_s[e, :, cut], NN)
            temp[b % 2][0][...] = prob.astype(bf16)
            temp[b % 2][1][...] = (prob * grad).astype(bf16)

        def pulls(b):
            e, c = b // per_head, b % per_head
            cut = slice(c * block, (c + 1) * block)
            prob, grad = temp[b % 2]
            dv = dg(prob[...], da[cut, :], NN)
            dk = dg(grad[...], q_ref[s, cut, at], NN)
            dqt[64 * e : 64 * e + 64, cut] = dg(kt[64 * e : 64 * e + 64, :], grad[...], NN)
            if c == 0:
                dv_t[e][...] = dv
                dk_t[e][...] = dk
            else:
                dv_t[e][...] += dv
                dk_t[e][...] += dk

        probs(0)
        for b in range(2 * per_head):
            if b + 1 < 2 * per_head:
                probs(b + 1)
            pulls(b)
        even = lane < 64
        dv_s[s, :, at] = jnp.where(even, dv_0[...], dv_1[...]).astype(bf16)
        dk_s[s, :, at] = (jnp.where(even, dk_0[...], dk_1[...]) * LN2).astype(bf16)
        dq_s[s, :, at] = dqt[...].T.astype(bf16)

    turns = seqs * (HEADS // 2)

    @pl.loop(0, turns)
    def _(j):
        for step in range(nb - 1):

            @pl.when(j == ((step + 1) * turns) // nb)
            def _():
                finish(feeds, step)
                start(feeds, step + 1)

        pair(j)

    def weight(j):
        return g1[(slice(None),) * nb + (slice(j * r, j * r + r), slice(None))].reshape(width, width)

    scale = HEAD_DIM**-0.5
    mem = mem_ref[...]
    tail = slice(length, keys)
    sums = []
    for j, ref in enumerate((dq_s, dk_s, dv_s)):
        total = 0.0
        for s in range(seqs):
            total = total + dg(x_ref[s], ref[s, 0:length, :], TN)
            if j:
                total = total + dg(mem, ref[s, tail, :], TN)
        if j == 0:
            total = total * scale
        cuts = (slice(None),) * nb + (slice(j * r, j * r + r), slice(None))
        part2[cuts] = total.astype(bf16).reshape((2,) * nb + (r, width))
    start(heads, 0)
    bq = sum(col_sum(dq_s[s].astype(f32)) for s in range(seqs)) * scale
    bv = sum(col_sum(dv_s[s].astype(f32)) for s in range(seqs))
    gmem = sum(
        dg(dk_s[s, tail, :], weight(1), NT) + dg(dv_s[s, tail, :], weight(2), NT)
        for s in range(seqs)
    )
    vec_row = lax.broadcasted_iota(jnp.int32, (8, width), 0)
    vecs = jnp.where(vec_row == 0, bq, jnp.where(vec_row == 1, bv, gvec_ref[...]))
    per = 128 // r
    row8 = lax.broadcasted_iota(jnp.int32, (8, 128), 0)
    for i in range(count):
        at = tuple((i >> b) & 1 for b in cube.msb_first)
        g, off = i // per, (i % per) * r
        cut = slice(128 * g, 128 * g + 128)
        up = gub_ref[:, 128 * (i * fr // 128) : 128 * (i * fr // 128) + 128]
        up = jnp.where(row8 == 0, jnp.broadcast_to(up, (8, 128)), 0.0)
        up = pltpu.roll(up, (3 * r - (i * fr) % 128) % 128, 1)
        for k in range(2):
            top = pltpu.roll(gmem[8 * k : 8 * k + 8, cut], -off % 128, 1)
            block8 = jnp.where(lane < r, top, 0.0)
            if k == 0:
                low = pltpu.roll(gmem[16:24, cut], (r - off) % 128, 1)
                vec = pltpu.roll(vecs[:, cut], (2 * r - off) % 128, 1)
                block8 = jnp.where((lane >= r) & (lane < 2 * r), low, block8)
                block8 = jnp.where((lane >= 2 * r) & (lane < 3 * r), vec, block8)
                block8 = jnp.where((lane >= 3 * r) & (lane < 3 * r + fr), up, block8)
            small_s[at + (slice(8 * k, 8 * k + 8), slice(None))] = block8
    start(smalls, 0)

    tile = 512
    tiles = length // tile

    def inputs(i):
        s, rows = i // tiles, pl.ds((i % tiles) * tile, tile)
        dx = res_ref[s, rows, :] + dg(dq_s[s, rows, :], weight(0), NT) * scale
        dx = dx + dg(dk_s[s, rows, :], weight(1), NT) + dg(dv_s[s, rows, :], weight(2), NT)
        dx_o[s, rows, :] = dx.astype(bf16)

    finish(feeds, nb - 1)
    for k in range(2):
        total = feeds[k].add(nb - 1, True)
        gwo_o[:, halves[k]] = total[0:r, :]
        for c in range(cols):
            lo = c * width + halves[k].start
            gwu_o[:, lo : lo + half] = total[r + c * r : r + c * r + r, :]
        gwd_o[:, halves[k]] = total[r + cols * r :, :]
    todo = list(range(seqs * tiles))
    for step in range(nb):
        if todo:
            inputs(todo.pop(0))
        finish(heads + smalls, step)
        if step + 1 < nb:
            start(heads + smalls, step + 1)
    for i in todo:
        inputs(i)
    for k in range(2):
        total = heads[k].add(nb - 1, True)
        for j, ref in enumerate((gwq_o, gwk_o, gwv_o)):
            ref[:, halves[k]] = total[j * r : j * r + r, :]
    small_o[...] = smalls[0].add(nb - 1, True)


def pull_call(count, sub, mem_rows, r, fr, lengths, x, mem, q, k, v, qt, att, da, res, g1, part1, gvec, gub):
    seqs, length, width = x.shape
    keys = k.shape[1]
    ff = gub.shape[1]
    rows2 = part1.shape[-2]
    nb = count.bit_length() - 1
    cube = (2,) * nb
    block = min(512, length)
    half = width // 2
    shape = jax.ShapeDtypeStruct
    vm = pl.BlockSpec(memory_space=VMEM)

    def steps(tail, dtype):
        return [VMEM((2,) * (nb - 1 - step) + tail, dtype) for step in range(nb)]

    return pl.pallas_call(
        functools.partial(pull_kernel, count, sub, mem_rows, r, fr),
        out_shape=(
            shape((seqs, length, width), bf16),
            shape((r, width), f32),
            shape((r, width), f32),
            shape((r, width), f32),
            shape((r, width), f32),
            shape((r, ff), f32),
            shape((fr, width), f32),
            shape((16, 128), f32),
        ),
        in_specs=[pl.BlockSpec(memory_space=pltpu.SMEM)] + [vm] * 13,
        out_specs=[vm] * 8,
        scratch_shapes=[
            VMEM((2, keys, 128), bf16),
            VMEM((2, keys, 128), bf16),
            VMEM((128, keys), bf16),
            VMEM((2, 128, length), bf16),
        ]
        + [VMEM((keys, block), bf16)] * 4
        + [
            VMEM((seqs, length, width), bf16),
            VMEM((seqs, keys, width), bf16),
            VMEM((seqs, keys, width), bf16),
            VMEM((128, length), f32),
        ]
        + [VMEM((keys, 128), f32)] * 4
        + [VMEM(cube + (3 * r, width), bf16), VMEM(cube + (16, 128), f32)]
        + steps((rows2, half), bf16) * 2
        + steps((3 * r, half), bf16) * 2
        + steps((16, 128), f32)
        + [pltpu.SemaphoreType.DMA((5, nb)), pltpu.SemaphoreType.DMA((5, nb))],
        compiler_params=pltpu.CompilerParams(
            collective_id=1, has_side_effects=True, vmem_limit_bytes=60 * 2**20
        ),
        name="pull",
    )(lengths, x, mem, q, k, v, qt, att, da, res, g1, part1, gvec, gub)


DIMS = (1, 0, 0, 0, 0, 0, 0, 0, 0, 0, 0, 0, 0, 0, 0, 0)


def on_device(devices, inputs, lengths, *rest):
    params, cotangent = rest[:-1], rest[-1]
    width = inputs.shape[2]
    count = min(devices, width // 16)
    sub = devices // count
    sets = [list(range(g * sub, (g + 1) * sub)) for g in range(count)]
    if sub > 1:
        params = tuple(
            lax.all_gather(a, "dp", axis=d, tiled=True, axis_index_groups=sets)
            for a, d in zip(params, DIMS, strict=True)
        )
    (memory, wq, bq, wk, wv, bv, wo, bo, ga, sa, wu, bu, wd, bd, gb, sb) = params
    r, fr = wq.shape[0], wd.shape[0]
    mem_rows = memory.shape[0]

    def fill(a, lanes):
        return jnp.pad(a, ((0, 16 - a.shape[0]), (0, lanes - a.shape[1])))

    vecs = jnp.stack([bq, bv, bo, ga, sa, bd, gb, sb])
    small = jnp.concatenate(
        [memory[0:16], fill(memory[16:], r), fill(vecs, r), fill(bu[None], 128 - 3 * r)], 1
    )
    q, k, v, qt, att, g1, g2, vec, ub, mem = attend_call(
        count, sub, lengths, inputs, wq, wk, wv, wo, wu, wd, small, mem_rows
    )
    seqs, length = inputs.shape[:2]
    layer_out, res, datt, part1, gvec, gub = feed_call(
        inputs,
        att.reshape(seqs, width, length),
        cotangent,
        g2.reshape((count,) + g2.shape[-2:]),
        vec,
        ub,
        r,
        fr,
    )
    dx, gwq, gwk, gwv, gwo, gwu, gwd, tiny = pull_call(
        count, sub, mem_rows, r, fr, lengths, inputs, mem, q, k, v, qt, att, datt, res, g1,
        part1.reshape(g2.shape), gvec, gub,
    )
    gmem = jnp.concatenate([tiny[:, 0:r], tiny[0 : mem_rows - 16, r : 2 * r]], 0)
    gbq, gbv, gbo, gga, gsa, gbd, ggb, gsb = [tiny[j, 2 * r : 3 * r] for j in range(8)]
    gbu = tiny[0, 3 * r : 3 * r + fr]
    grads = (gmem, gwq, gbq, gwk, gwv, gbv, gwo, gbo, gga, gsa, gwu, gbu, gwd, gbd, ggb, gsb)
    if sub > 1:
        grads = tuple(
            lax.psum_scatter(a, "dp", scatter_dimension=d, tiled=True, axis_index_groups=sets)
            for a, d in zip(grads, DIMS, strict=True)
        )
    return (layer_out, dx) + grads


def solution(mesh):
    rows, row, mem = P("dp", None), P("dp"), P(None, "dp")
    full = P("dp", None, None)
    params = (mem, rows, row, rows, rows, row, rows, row, row, row, rows, row, rows, row, row, row)
    return jax.shard_map(
        functools.partial(on_device, mesh.shape["dp"]),
        mesh=mesh,
        in_specs=(full, P("dp")) + params + (full,),
        out_specs=(full, full) + params,
        check_vma=False,
    )
```

```python
import functools

import jax
import jax.numpy as jnp
from jax import lax
from jax.experimental import pallas as pl
from jax.experimental.pallas import tpu as pltpu
from jax.sharding import PartitionSpec as P

HEADS = 8
HEAD_DIM = 64
EPSILON = 1e-05
LOG2E = 1.4426950408889634
LN2 = 0.6931471805599453
GELU_A = 0.7978845608028654
GELU_B = GELU_A * 0.044715
HIDE = -1e30
VEC = 20
KEY_PAD = 32

f32 = jnp.float32
bf16 = jnp.bfloat16
VMEM = pltpu.VMEM
MESH = pl.DeviceIdType.MESH
NN = (((1,), (0,)), ((), ()))
NT = (((1,), (1,)), ((), ()))
TN = (((0,), (0,)), ((), ()))


def dg(left, right, dims):
    return lax.dot_general(left, right, dims, preferred_element_type=f32)


def col_sum(value):
    return jnp.sum(value, 0, keepdims=True)


class Cube:
    def __init__(self, count, sub):
        self.count, self.sub = count, sub
        self.nb = count.bit_length() - 1
        device = lax.axis_index("dp")
        self.device = device
        me = device // sub
        self.bits = [(me // (2**b)) % 2 for b in range(self.nb)]
        self.msb_first = tuple(range(self.nb - 1, -1, -1))

    def partner(self, flips):
        to = self.device
        for b in flips:
            to = to + (1 - 2 * self.bits[b]) * (2**b * self.sub)
        return (to,)

    def barrier(self, routes):
        groups = sorted({flips for route in routes for group in route for flips in masks(group)})
        sem = pltpu.get_barrier_semaphore()
        for flips in groups:
            pl.semaphore_signal(sem, inc=1, device_id=self.partner(flips), device_id_type=MESH)
        pl.semaphore_wait(sem, len(groups))

    def own(self):
        return tuple(self.bits[b] for b in self.msb_first)


def masks(group):
    return [
        tuple(b for k, b in enumerate(group) if (m >> k) & 1) for m in range(1, 2 ** len(group))
    ]


def routes(nb):
    if nb >= 4:
        far = list(range(nb - 1, 2, -1))
        groups = [tuple(far[k : k + 2]) for k in range(0, len(far), 2)]
        return (groups + [(1,), (2,), (0,)], groups + [(2,), (1,), (0,)])
    return ([(b,) for b in range(nb - 1, -1, -1)],) * 2


def most(route):
    return max(2 ** len(group) - 1 for group in route)


def gather_copies(cube, ref, route, step, lanes, send, recv):
    done = {b for group in route[:step] for b in group}
    idx = tuple(slice(None) if c in done else cube.bits[c] for c in cube.msb_first)
    view = ref.at[idx + (slice(None), lanes)]
    return [
        pltpu.make_async_remote_copy(
            src_ref=view,
            dst_ref=view,
            send_sem=send.at[step, k],
            recv_sem=recv.at[step, k],
            device_id=cube.partner(flips),
            device_id_type=MESH,
        )
        for k, flips in enumerate(masks(route[step]))
    ]


class Scatter:
    def __init__(self, cube, source, lanes, route, bufs, send, recv):
        self.cube, self.source, self.lanes, self.route = cube, source, lanes, route
        self.bufs, self.send, self.recv = bufs, send, recv
        self.steps = len(route)

    def _piece(self, step, flips, rest=None):
        cube = self.cube
        gone = {b for group in self.route[:step] for b in group}
        left = [c for c in cube.msb_first if c not in gone]
        rest = iter(rest) if rest is not None else None
        idx = ()
        for c in left:
            if c in self.route[step]:
                idx += (1 - cube.bits[c] if c in flips else cube.bits[c],)
            else:
                idx += (slice(None) if rest is None else next(rest),)
        if step == 0:
            return self.source, idx + (slice(None), self.lanes)
        return self.bufs[step - 1].at[0], idx

    def copies(self, step):
        out = []
        for k, flips in enumerate(masks(self.route[step])):
            ref, idx = self._piece(step, flips)
            out.append(
                pltpu.make_async_remote_copy(
                    src_ref=ref.at[idx],
                    dst_ref=self.bufs[step].at[k],
                    send_sem=self.send.at[step, k],
                    recv_sem=self.recv.at[step, k],
                    device_id=self.cube.partner(flips),
                    device_id_type=MESH,
                )
            )
        return out

    def total(self, step, rest=None):
        ref, idx = self._piece(step, (), rest)
        value = ref[idx].astype(f32)
        for k in range(2 ** len(self.route[step]) - 1):
            value = value + self.bufs[step][(k,) + tuple(rest or ())].astype(f32)
        return value

    def add(self, step):
        free = self.cube.nb - sum(len(group) for group in self.route[: step + 1])
        into = self.bufs[step]
        for flat in range(2**free):
            rest = tuple((flat >> (free - 1 - k)) & 1 for k in range(free))
            into[(0,) + rest] = self.total(step, rest).astype(into.dtype)


def scatter_bufs(nb, route, tail, dtype):
    bufs, left = [], nb
    for group in route:
        left -= len(group)
        bufs.append(VMEM((2 ** len(group) - 1,) + (2,) * left + tail, dtype))
    return bufs


def attend_kernel(
    count, sub, mem_rows,
    len_ref, x_any, wq_ref, wk_ref, wv_ref, wo_ref, wu_ref, wd_ref, memt_ref, ub_ref, *rest,
):
    vec_refs, rest = rest[:8], rest[8:]
    (
    q_any, k_any, v_any, qt_any, att_any, g1_any, g2, vec_o, ub_o, mem_o,
    x_ref, q_o, k_o, v_o, qt_o, att_o, g1,
    gs, ksel, vt_s, score_a, score_b, top_a, top_b,
    flat_s, wide_s,
    local, x_sem, out_sem, head_sem, send1, recv1, send2, recv2, send3, recv3,
    ) = rest
    cube = Cube(count, sub)
    nb = cube.nb
    seqs, length, width = x_ref.shape
    keys = k_o.shape[2]
    mem_pad = keys - length
    r = wq_ref.shape[0]
    ff = wu_ref.shape[1]
    cols = ff // width
    fr = wd_ref.shape[0]
    own = cube.own()
    ways = routes(nb)
    steps = len(ways[0])
    half = width // 2
    halves = (slice(0, half), slice(half, width))
    whole = (slice(None), slice(None))
    x_load = pltpu.make_async_copy(x_any, x_ref, x_sem)
    x_load.start()
    for j, ref in enumerate((wq_ref, wk_ref, wv_ref)):
        g1[own + (slice(j * r, j * r + r), slice(None))] = ref[...]
    wide_s[...] = jnp.zeros_like(wide_s)
    flat_s[...] = jnp.zeros_like(flat_s)
    for j, ref in enumerate(vec_refs):
        wide_s[VEC + j : VEC + j + 1, 0:r] = ref[...].astype(f32)
    flat_s[0:r, 0:mem_rows] = memt_ref[...].astype(f32)
    flat_s[0:1, 64 : 64 + fr] = ub_ref[...].astype(f32)
    gs[own + whole] = (flat_s[...] + wide_s[...].T[0:16, :]).astype(bf16)
    parts = [(wo_ref, slice(0, r))]
    parts += [
        (wu_ref.at[:, c * width : (c + 1) * width], slice(r + c * r, r + c * r + r))
        for c in range(cols)
    ]
    parts += [(wd_ref, slice(r + cols * r, r + cols * r + fr))]
    moves = [
        pltpu.make_async_copy(ref, g2.at[own + (rows, slice(None))], local.at[j])
        for j, (ref, rows) in enumerate(parts)
    ]
    for move in moves:
        move.start()
    cube.barrier(ways)

    def first(step):
        copies = []
        for k in range(2):
            copies += gather_copies(cube, g1, ways[k], step, halves[k], send1.at[k], recv1.at[k])
        return copies + gather_copies(cube, gs, ways[0], step, slice(None), send3, recv3)

    chunks = 4
    chunk = width // chunks

    def second(c, step):
        lanes = slice(c * chunk, (c + 1) * chunk)
        return gather_copies(cube, g2, ways[c % 2], step, lanes, send2.at[c], recv2.at[c])

    def advance(c, step):
        if step > 0:
            for copy in second(c, step - 1):
                copy.wait()
        if step < steps:
            for copy in second(c, step):
                copy.start()

    for step in range(steps):
        copies = first(step)
        for copy in copies:
            copy.start()
        if step == 0:
            for move in moves:
                move.wait()
        for copy in copies:
            copy.wait()
        for slot, c, part in ((0, 0, 0), (1, 1, 0), (2, 0, 1), (2, 1, 1), (2, 2, 0)):
            if step == slot:
                advance(c, part)
    g1_out = pltpu.make_async_copy(g1, g1_any, out_sem.at[0])
    g1_out.start()
    x_load.wait()

    lane = lax.broadcasted_iota(jnp.int32, (1, 128), 1)
    every = gs[...].astype(f32).reshape(width, 128).T
    mem_o[0:16, :] = every[0:16, :].astype(bf16)
    rest_row = lax.broadcasted_iota(jnp.int32, (16, width), 0)
    mem_o[16:32, :] = jnp.where(rest_row < mem_rows - 16, every[16:32, :], 0.0).astype(bf16)
    vec_o[...] = every[VEC : VEC + 8, :]
    ups = [jnp.zeros((16, 128), f32) for _ in range(ff // 128)]
    for i in range(count):
        at = tuple((i >> b) & 1 for b in cube.msb_first)
        to = (i * fr) % 128
        here = (lane >= to) & (lane < to + fr)
        rolled = pltpu.roll(gs[at + whole].astype(f32), (to - 64) % 128, 1)
        ups[i * fr // 128] = ups[i * fr // 128] + jnp.where(here, rolled, 0.0)
    for g in range(ff // 128):
        ub_o[:, 128 * g : 128 * g + 128] = ups[g][0:1, :]

    def weight(j):
        return g1[(slice(None),) * nb + (slice(j * r, j * r + r), slice(None))].reshape(width, width)

    bq = vec_o[0:1, :]
    bv = vec_o[1:2, :]

    def put_keys(s, rows, kk, vv, bias):
        kb = kk.astype(bf16)
        vb = vv.astype(bf16)
        for p in range(HEADS // 2):
            k_o[s, p, rows, :] = kb[:, 128 * p : 128 * p + 128]
            v_o[s, p, rows, :] = vb[:, 128 * p : 128 * p + 128]
        for h in range(HEADS):
            p, o = h // 2, 64 * (1 - h % 2)
            pattern = jnp.where(
                lane == o, bias, jnp.where((lane > o) & (lane <= o + 3), 1.0, 0.0)
            ).astype(bf16)
            mine = (lane < 64) if h % 2 == 0 else (lane >= 64)
            ksel[s, h, rows, :] = jnp.where(mine, kb[:, 128 * p : 128 * p + 128], pattern)
        vt = vb.T
        for h in range(HEADS):
            vt_s[s, h, 0:64, rows] = vt[64 * h : 64 * h + 64, :]

    top_row = lax.broadcasted_iota(jnp.int32, (16, keys), 0)
    ones = jnp.where(top_row == 0, 1.0, 0.0).astype(bf16)
    for s in range(seqs):
        for h in range(HEADS):
            vt_s[s, h, 64:80, :] = ones
    mem = mem_o[...]
    mem_keys = dg(mem, weight(1), NN)
    mem_values = dg(mem, weight(2), NN) + bv
    mem_row = lax.broadcasted_iota(jnp.int32, (mem_pad, 1), 0)
    for s in range(seqs):
        put_keys(
            s, slice(length, keys), mem_keys, mem_values, jnp.where(mem_row < mem_rows, 0.0, HIDE)
        )
    tile = 512
    tiles = length // tile
    aux = jnp.where(lax.broadcasted_iota(jnp.int32, (64, tile), 0) == 0, 1.0, 0.0).astype(bf16)

    @pl.loop(0, seqs * tiles)
    def _(i):
        for slot, c, step in ((0, 3, 0), (2, 0, 2), (2, 1, 2), (3, 2, 1)):

            @pl.when(i == slot)
            def _():
                advance(c, step)

        s = i // tiles
        start = pl.multiple_of((i % tiles) * tile, tile)
        rows = pl.ds(start, tile)
        xt = x_ref[s, rows, :]
        qb = ((dg(xt, weight(0), NN) + bq) * (LOG2E * HEAD_DIM**-0.5)).astype(bf16)
        for p in range(HEADS // 2):
            q_o[s, p, rows, :] = qb[:, 128 * p : 128 * p + 128]
        qt = qb.T
        for h in range(HEADS):
            e = h % 2
            qt_o[s, h, 64 * e : 64 * e + 64, rows] = qt[64 * h : 64 * h + 64, :]
            qt_o[s, h, 64 * (1 - e) : 64 * (1 - e) + 64, rows] = aux
        row = lax.broadcasted_iota(jnp.int32, (tile, 1), 0) + start
        put_keys(
            s,
            rows,
            dg(xt, weight(1), NN),
            dg(xt, weight(2), NN) + bv,
            jnp.where(row < len_ref[s], 0.0, HIDE),
        )

    block = score_a.shape[1]
    per_head = length // block
    blocks = seqs * HEADS * per_head

    def place(i):
        s = i // (HEADS * per_head)
        h = (i // per_head) % HEADS
        return s, h, pl.ds(pl.multiple_of((i % per_head) * block, block), block)

    def scores(i, score, top):
        s, h, at = place(i)
        value = dg(ksel[s, h], qt_o[s, h, :, at], NN)
        score[...] = value
        top[...] = jnp.max(value, 0, keepdims=True)

    def mix(i, score, top):
        s, h, at = place(i)
        peak = top[...]
        probs = jnp.exp2(score[...] - peak).astype(bf16)
        mixed = dg(vt_s[s, h], probs, NN)
        total = mixed[64:65, :]
        att_o[s, h, :, at] = (mixed[0:64, :] / total).astype(bf16)
        stat = peak + jnp.log2(total)
        hi = stat.astype(bf16).astype(f32)
        mid = (stat - hi).astype(bf16).astype(f32)
        low = stat - hi - mid
        row = lax.broadcasted_iota(jnp.int32, (16, block), 0)
        extra = jnp.where(
            row == 0,
            1.0,
            jnp.where(row == 1, -hi, jnp.where(row == 2, -mid, jnp.where(row == 3, -low, 0.0))),
        )
        o = pl.multiple_of(64 * (1 - h % 2), 64)
        qt_o[s, h, pl.ds(o, 16), at] = extra.astype(bf16)

    outs = [
        pltpu.make_async_copy(src, dst, out_sem.at[1 + n])
        for n, (src, dst) in enumerate(((q_o, q_any), (k_o, k_any), (v_o, v_any)))
    ]
    for out in outs:
        out.start()
    scores(0, score_a, top_a)
    turns = blocks // 2
    heads_a_turn = max(1, 2 // per_head)

    def head_outs(j):
        s, h = j // HEADS, j % HEADS
        return [
            pltpu.make_async_copy(qt_o.at[s, h], qt_any.at[s, h], head_sem.at[j, 0]),
            pltpu.make_async_copy(att_o.at[s, h], att_any.at[s, h], head_sem.at[j, 1]),
        ]

    plan = ((0, 3, 1), (3, 0, 3), (4, 1, 3), (4, 2, 2), (5, 3, 2), (10, 2, 3), (11, 3, 3))

    @pl.loop(0, turns)
    def _(j):
        for slot, c, step in plan:

            @pl.when(j == (slot * turns) // 16)
            def _():
                advance(c, step)

        scores(2 * j + 1, score_b, top_b)
        mix(2 * j, score_a, top_a)
        scores(jnp.minimum(2 * j + 2, blocks - 1), score_a, top_a)
        mix(2 * j + 1, score_b, top_b)
        for k in range(heads_a_turn):
            for out in head_outs(j * heads_a_turn + k):
                out.start()

    for c in range(chunks):
        advance(c, steps)
    for out in outs + [g1_out]:
        out.wait()

    @pl.loop(0, seqs * HEADS)
    def _(j):
        for out in head_outs(j):
            out.wait()


def attend_call(count, sub, lengths, x, wq, wk, wv, wo, wu, wd, memt, ub, vecs, mem_rows):
    seqs, length, width = x.shape
    r, ff, fr = wq.shape[0], wu.shape[1], wd.shape[0]
    rows2 = r + (ff // width) * r + fr
    keys = length + KEY_PAD
    nb = count.bit_length() - 1
    cube = (2,) * nb
    way = routes(nb)[0]
    links = (len(way), most(way))
    block = min(512, length)
    pairs = HEADS // 2
    shape = jax.ShapeDtypeStruct
    vm = pl.BlockSpec(memory_space=VMEM)
    hbm = pl.BlockSpec(memory_space=pl.ANY)
    dma = pltpu.SemaphoreType.DMA
    kept = (
        shape((seqs, pairs, length, 128), bf16),
        shape((seqs, pairs, keys, 128), bf16),
        shape((seqs, pairs, keys, 128), bf16),
        shape((seqs, HEADS, 128, length), bf16),
        shape((seqs, HEADS, HEAD_DIM, length), bf16),
        shape(cube + (3 * r, width), bf16),
    )
    return pl.pallas_call(
        functools.partial(attend_kernel, count, sub, mem_rows),
        out_shape=kept
        + (
            shape(cube + (rows2, width), bf16),
            shape((8, width), f32),
            shape((1, ff), f32),
            shape((KEY_PAD, width), bf16),
        ),
        in_specs=[pl.BlockSpec(memory_space=pltpu.SMEM), hbm] + [vm] * 16,
        out_specs=[hbm] * 7 + [vm] * 3,
        scratch_shapes=[VMEM(x.shape, bf16)]
        + [VMEM(a.shape, bf16) for a in kept]
        + [
            VMEM(cube + (16, 128), bf16),
            VMEM((seqs, HEADS, keys, 128), bf16),
            VMEM((seqs, HEADS, 80, keys), bf16),
            VMEM((keys, block), f32),
            VMEM((keys, block), f32),
            VMEM((1, block), f32),
            VMEM((1, block), f32),
            VMEM((16, 128), f32),
            VMEM((128, 128), f32),
            dma((2 + ff // width,)),
            dma,
            dma((4,)),
            dma((seqs * HEADS, 2)),
            dma((2,) + links),
            dma((2,) + links),
            dma((4,) + links),
            dma((4,) + links),
            dma(links),
            dma(links),
        ],
        compiler_params=pltpu.CompilerParams(
            collective_id=0, has_side_effects=True, vmem_limit_bytes=60 * 2**20
        ),
        name="attend",
    )(lengths, x, wq, wk, wv, wo, wu, wd, memt, ub, *vecs)


def norm_forward(value, gain, shift):
    center = value - jnp.mean(value, -1, keepdims=True)
    inverse = lax.rsqrt(jnp.mean(center * center, -1, keepdims=True) + EPSILON)
    normed = center * inverse
    return normed * gain + shift, normed, inverse


def norm_backward(grad, normed, inverse, gain):
    scaled = grad * gain
    return inverse * (
        scaled
        - jnp.mean(scaled, -1, keepdims=True)
        - normed * jnp.mean(scaled * normed, -1, keepdims=True)
    )


def feed_kernel(
    r, fr, steps,
    x_ref, att_ref, dy_ref, g2, vec, ub,
    out_o, res_o, datt_o, part_o, gvec, gub,
    slope_s, act_s, gwo, gwu, gwd,
):
    i = pl.program_id(0)
    rows, width = x_ref.shape[1:]
    count = g2.shape[0]
    cols = g2.shape[1] // r - 1 - fr // r
    per = width // fr

    @pl.when(i == 0)
    def _():
        for ref in (gwo, gwu, gwd, gvec, gub):
            ref[...] = jnp.zeros_like(ref)

    bo, ga, sa, bd, gb, sb = [vec[j : j + 1, :] for j in range(2, 8)]

    def wo():
        return g2[:, 0:r, :].reshape(width, width)

    def wu(c):
        return g2[:, r + c * r : r + c * r + r, :].reshape(width, width)

    def wd(c):
        return g2[c * per : (c + 1) * per, r + cols * r :, :].reshape(width, width)

    att = att_ref[0]
    hidden, normed1, inverse1 = norm_forward(x_ref[0].astype(f32) + dg(att, wo(), TN) + bo, ga, sa)
    low = hidden.astype(bf16)
    outer = hidden + bd
    for c in range(cols):
        at = slice(c * width, (c + 1) * width)
        u = dg(low, wu(c), NN) + ub[:, at]
        u2 = u * u
        t = jnp.tanh(u * (GELU_A + GELU_B * u2))
        hu = 0.5 * u
        act = (hu + hu * t).astype(bf16)
        act_s[c] = act
        slope_s[c] = (
            (0.5 + 0.5 * t) + (hu * (1.0 - t * t)) * (GELU_A + 3.0 * GELU_B * u2)
        ).astype(bf16)
        outer = outer + dg(act, wd(c), NN)
    out, normed2, inverse2 = norm_forward(outer, gb, sb)
    out_o[0] = out.astype(bf16)
    dy = dy_ref[0].astype(f32)
    gvec[6:7, :] += col_sum(dy * normed2)
    gvec[7:8, :] += col_sum(dy)
    d_res2 = norm_backward(dy, normed2, inverse2, gb)
    d_outer = d_res2.astype(bf16)
    gvec[5:6, :] += col_sum(d_outer.astype(f32))
    d_hidden = d_res2
    for c in range(cols):
        at = slice(c * width, (c + 1) * width)
        d_act = dg(d_outer, wd(c), NT)
        d_inner = (d_act * slope_s[c].astype(f32)).astype(bf16)
        gwd[at, :] += dg(act_s[c], d_outer, TN)
        gwu[:, at] += dg(low, d_inner, TN)
        gub[:, at] += col_sum(d_inner.astype(f32))
        d_hidden = d_hidden + dg(d_inner, wu(c), NT)
    gvec[3:4, :] += col_sum(d_hidden * normed1)
    gvec[4:5, :] += col_sum(d_hidden)
    d_res1 = norm_backward(d_hidden, normed1, inverse1, ga)
    res_o[0] = d_res1
    d_branch = d_res1.astype(bf16)
    gvec[2:3, :] += col_sum(d_branch.astype(f32))
    gwo[...] += dg(att, d_branch, NN)
    d_att = dg(d_branch, wo(), NT).astype(bf16)
    for p in range(width // 128):
        datt_o[0, p] = d_att[:, 128 * p : 128 * p + 128]

    @pl.when(i == steps - 1)
    def _():
        part_o[:, 0:r, :] = gwo[...].astype(bf16).reshape(count, r, width)
        for c in range(cols):
            part_o[:, r + c * r : r + c * r + r, :] = (
                gwu[:, c * width : (c + 1) * width].astype(bf16).reshape(count, r, width)
            )
        part_o[:, r + cols * r :, :] = gwd[...].astype(bf16).reshape(count, fr, width)


def feed_call(x, att, dy, g2, vec, ub, r, fr):
    seqs, length, width = x.shape
    ff = ub.shape[1]
    tile = min(512, length)
    tiles = length // tile
    shape = jax.ShapeDtypeStruct
    rows = pl.BlockSpec((1, tile, width), lambda i: (i // tiles, i % tiles, 0))

    def full(a):
        return pl.BlockSpec(a.shape, lambda i: (0,) * len(a.shape))

    outs = (
        shape((seqs, length, width), bf16),
        shape((seqs, length, width), f32),
        shape((seqs, width // 128, length, 128), bf16),
        shape(g2.shape, bf16),
        shape((8, width), f32),
        shape((1, ff), f32),
    )
    return pl.pallas_call(
        functools.partial(feed_kernel, r, fr, seqs * tiles),
        grid=(seqs * tiles,),
        out_shape=outs,
        in_specs=[
            rows,
            pl.BlockSpec((1, width, tile), lambda i: (i // tiles, 0, i % tiles)),
            rows,
            full(g2),
            full(vec),
            full(ub),
        ],
        out_specs=[
            rows,
            rows,
            pl.BlockSpec((1, width // 128, tile, 128), lambda i: (i // tiles, 0, i % tiles, 0)),
        ]
        + [full(a) for a in outs[3:]],
        scratch_shapes=[
            VMEM((ff // width, tile, width), bf16),
            VMEM((ff // width, tile, width), bf16),
            VMEM((width, width), f32),
            VMEM((width, ff), f32),
            VMEM((ff, width), f32),
        ],
        compiler_params=pltpu.CompilerParams(vmem_limit_bytes=60 * 2**20),
        name="feed",
    )(x, att, dy, g2, vec, ub)


def pull_kernel(
    count, sub, mem_rows, r, fr,
    len_ref, x_any, mem_ref, q_any, k_any, v_any, qt_any, att_any, da_any, res_any, g1_any, part1,
    gvec_ref, gub_ref,
    dx_any, sums_o, small_o,
    x_ref, q_ref, k_ref, v_ref, qt_ref, att_ref, da_ref, res_ref, g1, dx_o,
    ksel, vsel, kt, dot_s, p_a, d_a, p_b, d_b, dq_s, dk_s, dv_s, dqt,
    dv_0, dv_1, dk_0, dk_1, part2, small_s, *rest,
):
    cube = Cube(count, sub)
    nb = cube.nb
    ways = [list(reversed(route)) for route in routes(nb)]
    steps = len(ways[0])
    bufs = [rest[k * steps : (k + 1) * steps] for k in range(5)]
    send, recv, load_sem, late_sem, out_sem = rest[5 * steps :]
    seqs, length, width = x_ref.shape
    keys = k_ref.shape[2]
    ff = gub_ref.shape[1]
    cols = ff // width
    half = width // 2
    halves = (slice(0, half), slice(half, width))
    pairs = HEADS // 2
    feeds = [
        Scatter(cube, part1, halves[k], ways[k], bufs[k], send.at[k], recv.at[k]) for k in range(2)
    ]
    heads = [
        Scatter(cube, part2, halves[k], ways[k], bufs[2 + k], send.at[2 + k], recv.at[2 + k])
        for k in range(2)
    ]
    smalls = Scatter(cube, small_s, slice(None), ways[0], bufs[4], send.at[4], recv.at[4])

    def start(group, step):
        for part in group:
            for copy in part.copies(step):
                copy.start()

    def finish(group, step):
        for part in group:
            for copy in part.copies(step):
                copy.wait()
        if step < steps - 1:
            for part in group:
                part.add(step)

    def loads(j):
        p, s = j // seqs, j % seqs
        own = ((q_any, q_ref), (k_any, k_ref), (v_any, v_ref), (da_any, da_ref))
        out = [
            pltpu.make_async_copy(a.at[s, p], b.at[s, p], load_sem.at[j, n])
            for n, (a, b) in enumerate(own)
        ]
        both = pl.ds(2 * p, 2)
        return out + [
            pltpu.make_async_copy(a.at[s, both], b.at[s, both], load_sem.at[j, 4 + n])
            for n, (a, b) in enumerate(((qt_any, qt_ref), (att_any, att_ref)))
        ]

    late = [
        pltpu.make_async_copy(a, b, late_sem.at[n])
        for n, (a, b) in enumerate(((x_any, x_ref), (g1_any, g1), (res_any, res_ref)))
    ]

    @pl.loop(0, seqs * pairs)
    def _(j):
        for load in loads(j):
            load.start()

    for load in late:
        load.start()
    cube.barrier(ways)
    start(feeds, 0)

    lane = lax.broadcasted_iota(jnp.int32, (1, 128), 1)
    key_row = lax.broadcasted_iota(jnp.int32, (keys, 1), 0)
    block = p_a.shape[1]
    per_head = length // block
    dv_t, dk_t = (dv_0, dv_1), (dk_0, dk_1)
    temp = ((p_a, d_a), (p_b, d_b))

    def pair(j):
        p, s = j // seqs, j % seqs
        at = pl.ds(pl.multiple_of(128 * p, 128), 128)
        kp = k_ref[s, p]
        vp = v_ref[s, p]
        kt[...] = kp.T
        da = da_ref[s, p]
        dat = da.T
        seen = (key_row < len_ref[s]) | ((key_row >= length) & (key_row < length + mem_rows))
        bias = jnp.where(seen, 0.0, HIDE)
        for e in range(2):
            o = 64 * (1 - e)
            mine = (lane < 64) if e == 0 else (lane >= 64)
            pattern = jnp.where(
                lane == o, bias, jnp.where((lane > o) & (lane <= o + 3), 1.0, 0.0)
            ).astype(bf16)
            ksel[e] = jnp.where(mine, kp, pattern)
            vsel[e] = jnp.where(
                mine, vp, jnp.where((lane >= o) & (lane < o + 2), 1.0, 0.0).astype(bf16)
            )
            dt = dat[64 * e : 64 * e + 64, :]
            delta = col_sum(dt.astype(f32) * att_ref[s, 2 * p + e].astype(f32))
            hi = delta.astype(bf16).astype(f32)
            row = lax.broadcasted_iota(jnp.int32, (64, length), 0)
            dot_s[e, 64 * e : 64 * e + 64, :] = dt
            dot_s[e, o : o + 64, :] = jnp.where(
                row == 0, -hi, jnp.where(row == 1, hi - delta, 0.0)
            ).astype(bf16)

        def probs(b):
            e, c = b // per_head, b % per_head
            cut = slice(c * block, (c + 1) * block)
            prob = jnp.exp2(dg(ksel[e], qt_ref[s, 2 * p + e, :, cut], NN))
            grad = dg(vsel[e], dot_s[e, :, cut], NN)
            temp[b % 2][0][...] = prob.astype(bf16)
            temp[b % 2][1][...] = (prob * grad).astype(bf16)

        def pulls(b):
            e, c = b // per_head, b % per_head
            cut = slice(c * block, (c + 1) * block)
            prob, grad = temp[b % 2]
            dv = dg(prob[...], da[cut, :], NN)
            dk = dg(grad[...], q_ref[s, p, cut, :], NN)
            dqt[64 * e : 64 * e + 64, cut] = dg(kt[64 * e : 64 * e + 64, :], grad[...], NN)
            if c == 0:
                dv_t[e][...] = dv
                dk_t[e][...] = dk
            else:
                dv_t[e][...] += dv
                dk_t[e][...] += dk

        probs(0)
        for b in range(2 * per_head):
            if b + 1 < 2 * per_head:
                probs(b + 1)
            pulls(b)
        even = lane < 64
        dv_s[s, :, at] = jnp.where(even, dv_0[...], dv_1[...]).astype(bf16)
        dk_s[s, :, at] = (jnp.where(even, dk_0[...], dk_1[...]) * LN2).astype(bf16)
        dq_s[s, :, at] = dqt[...].T.astype(bf16)

    def weight(j):
        return g1[(slice(None),) * nb + (slice(j * r, j * r + r), slice(None))].reshape(width, width)

    scale = HEAD_DIM**-0.5
    tail = slice(length, keys)

    def terms(k):
        mem = mem_ref[...]
        for j, ref in enumerate((dq_s, dk_s, dv_s)):
            total = 0.0
            for s in range(seqs):
                total = total + dg(x_ref[s], ref[s, 0:length, halves[k]], TN)
                if j:
                    total = total + dg(mem, ref[s, tail, halves[k]], TN)
            if j == 0:
                total = total * scale
            cuts = (slice(None),) * nb + (slice(j * r, j * r + r), halves[k])
            part2[cuts] = total.astype(bf16).reshape((2,) * nb + (r, half))

    turns = seqs * pairs

    @pl.loop(0, turns)
    def _(j):
        for load in loads(j):
            load.wait()

        for slot, step in ((1, 0), (3, 1), (4, 2)):

            @pl.when(j == (slot * turns) // 8)
            def _():
                finish(feeds, step)
                start(feeds, step + 1)

        @pl.when(j == turns // 2)
        def _():
            for load in late:
                load.wait()
            terms(0)
            start(heads[:1], 0)

        for slot, step in ((5, 0), (6, 1), (7, 2)):

            @pl.when(j == (slot * turns) // 8)
            def _():
                finish(heads[:1], step)
                start(heads[:1], step + 1)

        pair(j)

    terms(1)
    start(heads[1:], 0)
    bq = sum(col_sum(dq_s[s].astype(f32)) for s in range(seqs)) * scale
    bv = sum(col_sum(dv_s[s].astype(f32)) for s in range(seqs))
    gmem = sum(
        dg(dk_s[s, tail, :], weight(1), NT) + dg(dv_s[s, tail, :], weight(2), NT)
        for s in range(seqs)
    )
    vec_row = lax.broadcasted_iota(jnp.int32, (8, width), 0)
    vecs = jnp.where(vec_row == 0, bq, jnp.where(vec_row == 1, bv, gvec_ref[...]))
    flat = jnp.concatenate(
        [
            gmem[0:16, :],
            jnp.concatenate([gmem[16:20, :], vecs[0:4, :]], 0),
            jnp.concatenate([vecs[4:8, :], jnp.zeros((4, width), f32)], 0),
            jnp.zeros((96, width), f32),
        ],
        0,
    )
    small_s[...] = flat.T.reshape((2,) * nb + (16, 128))
    for i in range(count):
        at = tuple((i >> b) & 1 for b in cube.msb_first)
        off = (i * fr) % 128
        up = jnp.broadcast_to(gub_ref[:, i * fr - off : i * fr - off + 128], (8, 128))
        up = pltpu.roll(up, (64 - off) % 128, 1)
        small_s[at + (slice(0, 1), slice(64, 64 + fr))] = up[0:1, 64 : 64 + fr]
    start([smalls], 0)
    tile = 512
    tiles = length // tile

    def inputs(i):
        s, rows = i // tiles, pl.ds((i % tiles) * tile, tile)
        dx = res_ref[s, rows, :] + dg(dq_s[s, rows, :], weight(0), NT) * scale
        dx = dx + dg(dk_s[s, rows, :], weight(1), NT) + dg(dv_s[s, rows, :], weight(2), NT)
        dx_o[s, rows, :] = dx.astype(bf16)
        out = pltpu.make_async_copy(dx_o.at[s, rows], dx_any.at[s, rows], out_sem.at[i])
        out.start()
        return out

    def total(part, lo, hi, k):
        value = part.total(steps - 1)
        sums_o[lo:hi, halves[k]] = value

    todo = list(range(seqs * tiles))
    outs = []
    group = heads[1:] + [smalls]
    for step in range(steps):
        if todo:
            outs.append(inputs(todo.pop(0)))
        if step == steps - 2:
            finish(feeds, steps - 1)
            for k in range(2):
                total(feeds[k], 3 * r, sums_o.shape[0], k)
            finish(heads[:1], steps - 1)
            total(heads[0], 0, 3 * r, 0)
        finish(group, step)
        if step + 1 < steps:
            start(group, step + 1)
    for i in todo:
        outs.append(inputs(i))
    total(heads[1], 0, 3 * r, 1)
    small_o[...] = smalls.total(steps - 1)
    for out in outs:
        out.wait()


def pull_call(count, sub, mem_rows, r, fr, lengths, x, mem, q, k, v, qt, att, da, res, g1, part1, gvec, gub):
    seqs, length, width = x.shape
    keys = k.shape[2]
    rows2 = part1.shape[-2]
    nb = count.bit_length() - 1
    cube = (2,) * nb
    way = list(reversed(routes(nb)[0]))
    links = (len(way), most(way))
    block = min(512, length)
    half = width // 2
    turns = seqs * (HEADS // 2)
    shape = jax.ShapeDtypeStruct
    vm = pl.BlockSpec(memory_space=VMEM)
    hbm = pl.BlockSpec(memory_space=pl.ANY)
    dma = pltpu.SemaphoreType.DMA
    return pl.pallas_call(
        functools.partial(pull_kernel, count, sub, mem_rows, r, fr),
        out_shape=(
            shape((seqs, length, width), bf16),
            shape((3 * r + rows2, width), f32),
            shape((16, 128), f32),
        ),
        in_specs=[pl.BlockSpec(memory_space=pltpu.SMEM), hbm, vm] + [hbm] * 8 + [vm] * 3,
        out_specs=[hbm, vm, vm],
        scratch_shapes=[VMEM(a.shape, a.dtype) for a in (x, q, k, v, qt, att, da, res, g1, x)]
        + [
            VMEM((2, keys, 128), bf16),
            VMEM((2, keys, 128), bf16),
            VMEM((128, keys), bf16),
            VMEM((2, 128, length), bf16),
        ]
        + [VMEM((keys, block), bf16)] * 4
        + [
            VMEM((seqs, length, width), bf16),
            VMEM((seqs, keys, width), bf16),
            VMEM((seqs, keys, width), bf16),
            VMEM((128, length), f32),
        ]
        + [VMEM((keys, 128), f32)] * 4
        + [VMEM(cube + (3 * r, width), bf16), VMEM(cube + (16, 128), f32)]
        + scatter_bufs(nb, way, (rows2, half), bf16) * 2
        + scatter_bufs(nb, way, (3 * r, half), bf16) * 2
        + scatter_bufs(nb, way, (16, 128), f32)
        + [dma((5,) + links)] * 2
        + [dma((turns, 6)), dma((3,)), dma((seqs * (length // 512),))],
        compiler_params=pltpu.CompilerParams(
            collective_id=1, has_side_effects=True, vmem_limit_bytes=62 * 2**20
        ),
        name="pull",
    )(lengths, x, mem, q, k, v, qt, att, da, res, g1, part1, gvec, gub)


def results_kernel(r, fr, mem_rows, dx_ref, sums, small, dx_o, *outs):
    outs, sem = outs[:-1], outs[-1]
    move = pltpu.make_async_copy(dx_ref, dx_o, sem)
    move.start()
    gq, gk, gv, go, gu, gd, gm, gb = outs[:8]
    vecs = outs[8:]
    width = gq.shape[1]
    cols = gu.shape[1] // width
    for n, ref in enumerate((gq, gk, gv, go)):
        ref[...] = sums[n * r : (n + 1) * r, :]
    for c in range(cols):
        gu[:, c * width : (c + 1) * width] = sums[(4 + c) * r : (5 + c) * r, :]
    gd[...] = sums[(4 + cols) * r :, :]
    value = small[...]
    gm[...] = value[0:r, 0:mem_rows]
    turned = jnp.concatenate([value, jnp.zeros((112, 128), f32)], 0).T
    for n, ref in enumerate(vecs):
        ref[...] = turned[VEC + n : VEC + n + 1, 0:r]
    gb[...] = value[0:1, 64 : 64 + fr]
    move.wait()


def results_call(r, fr, mem_rows, ff, dx, sums, small):
    width = sums.shape[1]
    shape = jax.ShapeDtypeStruct
    vm = pl.BlockSpec(memory_space=VMEM)
    hbm = pl.BlockSpec(memory_space=pl.ANY)
    mats = [(r, width)] * 4 + [(r, ff), (fr, width), (r, mem_rows), (1, fr)] + [(1, r)] * 8
    return pl.pallas_call(
        functools.partial(results_kernel, r, fr, mem_rows),
        out_shape=(shape(dx.shape, dx.dtype),) + tuple(shape(m, f32) for m in mats),
        in_specs=[vm, vm, vm],
        out_specs=[hbm] + [vm] * len(mats),
        scratch_shapes=[pltpu.SemaphoreType.DMA],
        name="results",
    )(dx, sums, small)


DIMS = (1, 0, 0, 0, 0, 0, 0, 0, 0, 0, 0, 0, 0, 0, 0, 0)


def on_device(devices, inputs, lengths, *rest):
    params, cotangent = rest[:-1], rest[-1]
    width = inputs.shape[2]
    count = min(devices, width // 16)
    sub = devices // count
    sets = [list(range(g * sub, (g + 1) * sub)) for g in range(count)]
    if sub > 1:
        params = tuple(
            lax.all_gather(a, "dp", axis=d, tiled=True, axis_index_groups=sets)
            for a, d in zip(params, DIMS, strict=True)
        )
    (memory, wq, bq, wk, wv, bv, wo, bo, ga, sa, wu, bu, wd, bd, gb, sb) = params
    r, fr = wq.shape[0], wd.shape[0]
    mem_rows = memory.shape[0]

    vecs = [a.reshape(1, r) for a in (bq, bv, bo, ga, sa, bd, gb, sb)]
    q, k, v, qt, att, g1, g2, vec, ub, mem = attend_call(
        count, sub, lengths, inputs, wq, wk, wv, wo, wu, wd, memory.T, bu.reshape(1, fr), vecs, mem_rows
    )
    seqs, length = inputs.shape[:2]
    layer_out, res, datt, part1, gvec, gub = feed_call(
        inputs,
        att.reshape(seqs, width, length),
        cotangent,
        g2.reshape((count,) + g2.shape[-2:]),
        vec,
        ub,
        r,
        fr,
    )
    dx, sums, tiny = pull_call(
        count, sub, mem_rows, r, fr, lengths, inputs, mem, q, k, v, qt, att, datt, res, g1,
        part1.reshape(g2.shape), gvec, gub,
    )
    dx, gwq, gwk, gwv, gwo, gwu, gwd, gmem, gbu, *vecs = results_call(
        r, fr, mem_rows, wu.shape[1], dx, sums, tiny
    )
    gmem = gmem.T
    gbu = gbu.reshape(fr)
    gbq, gbv, gbo, gga, gsa, gbd, ggb, gsb = [a.reshape(r) for a in vecs]
    grads = (gmem, gwq, gbq, gwk, gwv, gbv, gwo, gbo, gga, gsa, gwu, gbu, gwd, gbd, ggb, gsb)
    if sub > 1:
        grads = tuple(
            lax.psum_scatter(a, "dp", scatter_dimension=d, tiled=True, axis_index_groups=sets)
            for a, d in zip(grads, DIMS, strict=True)
        )
    return (layer_out, dx) + grads


def solution(mesh):
    rows, row, mem = P("dp", None), P("dp"), P(None, "dp")
    full = P("dp", None, None)
    params = (mem, rows, row, rows, rows, row, rows, row, row, row, rows, row, rows, row, row, row)
    return jax.shard_map(
        functools.partial(on_device, mesh.shape["dp"]),
        mesh=mesh,
        in_specs=(full, P("dp")) + params + (full,),
        out_specs=(full, full) + params,
        check_vma=False,
    )
```

```python
import functools

import jax
import jax.numpy as jnp
from jax import lax
from jax.experimental import pallas as pl
from jax.experimental.pallas import tpu as pltpu
from jax.sharding import PartitionSpec as P

HEADS = 8
HEAD_DIM = 64
EPSILON = 1e-05
LOG2E = 1.4426950408889634
LN2 = 0.6931471805599453
GELU_A = 0.7978845608028654
GELU_B = GELU_A * 0.044715
HIDE = -1e30
VEC = 20
KEY_PAD = 32

f32 = jnp.float32
bf16 = jnp.bfloat16
VMEM = pltpu.VMEM
MESH = pl.DeviceIdType.MESH
NN = (((1,), (0,)), ((), ()))
NT = (((1,), (1,)), ((), ()))
TN = (((0,), (0,)), ((), ()))


def dg(left, right, dims):
    return lax.dot_general(left, right, dims, preferred_element_type=f32)


def col_sum(value):
    return jnp.sum(value, 0, keepdims=True)


class Cube:
    def __init__(self, count, sub):
        self.count, self.sub = count, sub
        self.nb = count.bit_length() - 1
        device = lax.axis_index("dp")
        self.device = device
        me = device // sub
        self.bits = [(me // (2**b)) % 2 for b in range(self.nb)]
        self.msb_first = tuple(range(self.nb - 1, -1, -1))

    def partner(self, flips):
        to = self.device
        for b in flips:
            to = to + (1 - 2 * self.bits[b]) * (2**b * self.sub)
        return (to,)

    def barrier(self, routes):
        groups = sorted({flips for route in routes for group in route for flips in masks(group)})
        sem = pltpu.get_barrier_semaphore()
        for flips in groups:
            pl.semaphore_signal(sem, inc=1, device_id=self.partner(flips), device_id_type=MESH)
        pl.semaphore_wait(sem, len(groups))

    def own(self):
        return tuple(self.bits[b] for b in self.msb_first)


def masks(group):
    return [
        tuple(b for k, b in enumerate(group) if (m >> k) & 1) for m in range(1, 2 ** len(group))
    ]


def routes(nb):
    if nb >= 4:
        far = list(range(nb - 1, 2, -1))
        groups = [tuple(far[k : k + 2]) for k in range(0, len(far), 2)]
        return (groups + [(1,), (2,), (0,)], groups + [(2,), (1,), (0,)])
    return ([(b,) for b in range(nb - 1, -1, -1)],) * 2


def most(route):
    return max(2 ** len(group) - 1 for group in route)


def gather_copies(cube, ref, route, step, lanes, send, recv):
    done = {b for group in route[:step] for b in group}
    idx = tuple(slice(None) if c in done else cube.bits[c] for c in cube.msb_first)
    view = ref.at[idx + (slice(None), lanes)]
    return [
        pltpu.make_async_remote_copy(
            src_ref=view,
            dst_ref=view,
            send_sem=send.at[step, k],
            recv_sem=recv.at[step, k],
            device_id=cube.partner(flips),
            device_id_type=MESH,
        )
        for k, flips in enumerate(masks(route[step]))
    ]


class Scatter:
    def __init__(self, cube, source, lanes, route, bufs, send, recv):
        self.cube, self.source, self.lanes, self.route = cube, source, lanes, route
        self.bufs, self.send, self.recv = bufs, send, recv
        self.steps = len(route)

    def _piece(self, step, flips, rest=None):
        cube = self.cube
        gone = {b for group in self.route[:step] for b in group}
        left = [c for c in cube.msb_first if c not in gone]
        rest = iter(rest) if rest is not None else None
        idx = ()
        for c in left:
            if c in self.route[step]:
                idx += (1 - cube.bits[c] if c in flips else cube.bits[c],)
            else:
                idx += (slice(None) if rest is None else next(rest),)
        if step == 0:
            return self.source, idx + (slice(None), self.lanes)
        return self.bufs[step - 1].at[0], idx

    def copies(self, step):
        out = []
        for k, flips in enumerate(masks(self.route[step])):
            ref, idx = self._piece(step, flips)
            out.append(
                pltpu.make_async_remote_copy(
                    src_ref=ref.at[idx],
                    dst_ref=self.bufs[step].at[k],
                    send_sem=self.send.at[step, k],
                    recv_sem=self.recv.at[step, k],
                    device_id=self.cube.partner(flips),
                    device_id_type=MESH,
                )
            )
        return out

    def total(self, step, rest=None):
        ref, idx = self._piece(step, (), rest)
        value = ref[idx].astype(f32)
        for k in range(2 ** len(self.route[step]) - 1):
            value = value + self.bufs[step][(k,) + tuple(rest or ())].astype(f32)
        return value

    def add(self, step):
        free = self.cube.nb - sum(len(group) for group in self.route[: step + 1])
        into = self.bufs[step]
        for flat in range(2**free):
            rest = tuple((flat >> (free - 1 - k)) & 1 for k in range(free))
            into[(0,) + rest] = self.total(step, rest).astype(into.dtype)


def scatter_bufs(nb, route, tail, dtype):
    bufs, left = [], nb
    for group in route:
        left -= len(group)
        bufs.append(VMEM((2 ** len(group) - 1,) + (2,) * left + tail, dtype))
    return bufs


def attend_kernel(
    count, sub, mem_rows,
    len_ref, x_any, wq_ref, wk_ref, wv_ref, wo_ref, wu_ref, wd_ref, memt_ref, ub_ref, *rest,
):
    vec_refs, rest = rest[:8], rest[8:]
    (
    q_any, k_any, v_any, att_any, inv_any, g1_any, prob_any, g2, vec_o, ub_o, mem_o,
    x_ref, q_o, k_o, v_o, att_o, inv_o, g1,
    qt_o, gs, ksel, vt_s, score_a, score_b, prob_s, top_a, top_b,
    flat_s, wide_s,
    local, x_sem, out_sem, head_sem, prob_sem, send1, recv1, send2, recv2, send3, recv3,
    ) = rest
    cube = Cube(count, sub)
    nb = cube.nb
    seqs, length, width = x_ref.shape
    keys = v_o.shape[2]
    mem_pad = keys - length
    r = wq_ref.shape[0]
    ff = wu_ref.shape[1]
    cols = ff // width
    fr = wd_ref.shape[0]
    own = cube.own()
    ways = routes(nb)
    steps = len(ways[0])
    half = width // 2
    halves = (slice(0, half), slice(half, width))
    whole = (slice(None), slice(None))
    x_load = pltpu.make_async_copy(x_any, x_ref, x_sem)
    x_load.start()
    for j, ref in enumerate((wq_ref, wk_ref, wv_ref)):
        g1[own + (slice(j * r, j * r + r), slice(None))] = ref[...]
    wide_s[...] = jnp.zeros_like(wide_s)
    flat_s[...] = jnp.zeros_like(flat_s)
    for j, ref in enumerate(vec_refs):
        wide_s[VEC + j : VEC + j + 1, 0:r] = ref[...].astype(f32)
    flat_s[0:r, 0:mem_rows] = memt_ref[...].astype(f32)
    flat_s[0:1, 64 : 64 + fr] = ub_ref[...].astype(f32)
    gs[own + whole] = (flat_s[...] + wide_s[...].T[0:16, :]).astype(bf16)
    parts = [(wo_ref, slice(0, r))]
    parts += [
        (wu_ref.at[:, c * width : (c + 1) * width], slice(r + c * r, r + c * r + r))
        for c in range(cols)
    ]
    parts += [(wd_ref, slice(r + cols * r, r + cols * r + fr))]
    moves = [
        pltpu.make_async_copy(ref, g2.at[own + (rows, slice(None))], local.at[j])
        for j, (ref, rows) in enumerate(parts)
    ]
    for move in moves:
        move.start()
    cube.barrier(ways)

    def first(step):
        copies = []
        for k in range(2):
            copies += gather_copies(cube, g1, ways[k], step, halves[k], send1.at[k], recv1.at[k])
        return copies + gather_copies(cube, gs, ways[0], step, slice(None), send3, recv3)

    chunks = 4
    chunk = width // chunks

    def second(c, step):
        lanes = slice(c * chunk, (c + 1) * chunk)
        return gather_copies(cube, g2, ways[c % 2], step, lanes, send2.at[c], recv2.at[c])

    def advance(c, step):
        if step > 0:
            for copy in second(c, step - 1):
                copy.wait()
        if step < steps:
            for copy in second(c, step):
                copy.start()

    for step in range(steps):
        copies = first(step)
        for copy in copies:
            copy.start()
        if step == 0:
            for move in moves:
                move.wait()
        for copy in copies:
            copy.wait()
        for slot, c, part in ((0, 0, 0), (1, 1, 0), (2, 0, 1), (2, 1, 1), (2, 2, 0)):
            if step == slot:
                advance(c, part)
    g1_out = pltpu.make_async_copy(g1, g1_any, out_sem.at[0])
    g1_out.start()
    x_load.wait()

    lane = lax.broadcasted_iota(jnp.int32, (1, 128), 1)
    every = gs[...].astype(f32).reshape(width, 128).T
    mem_o[0:16, :] = every[0:16, :].astype(bf16)
    rest_row = lax.broadcasted_iota(jnp.int32, (16, width), 0)
    mem_o[16:32, :] = jnp.where(rest_row < mem_rows - 16, every[16:32, :], 0.0).astype(bf16)
    vec_o[...] = every[VEC : VEC + 8, :]
    ups = [jnp.zeros((16, 128), f32) for _ in range(ff // 128)]
    for i in range(count):
        at = tuple((i >> b) & 1 for b in cube.msb_first)
        to = (i * fr) % 128
        here = (lane >= to) & (lane < to + fr)
        rolled = pltpu.roll(gs[at + whole].astype(f32), (to - 64) % 128, 1)
        ups[i * fr // 128] = ups[i * fr // 128] + jnp.where(here, rolled, 0.0)
    for g in range(ff // 128):
        ub_o[:, 128 * g : 128 * g + 128] = ups[g][0:1, :]

    def weight(j):
        return g1[(slice(None),) * nb + (slice(j * r, j * r + r), slice(None))].reshape(width, width)

    bq = vec_o[0:1, :]
    bv = vec_o[1:2, :]

    def put_keys(s, rows, kk, vv, bias):
        kb = kk.astype(bf16)
        vb = vv.astype(bf16)
        kt = kb.T
        for p in range(HEADS // 2):
            k_o[s, p, :, rows] = kt[128 * p : 128 * p + 128, :]
            v_o[s, p, rows, :] = vb[:, 128 * p : 128 * p + 128]
        for h in range(HEADS):
            p, o = h // 2, 64 * (1 - h % 2)
            pattern = jnp.where(lane == o, bias, 0.0).astype(bf16)
            mine = (lane < 64) if h % 2 == 0 else (lane >= 64)
            ksel[s, h, rows, :] = jnp.where(mine, kb[:, 128 * p : 128 * p + 128], pattern)
        vt = vb.T
        for h in range(HEADS):
            vt_s[s, h, 0:64, rows] = vt[64 * h : 64 * h + 64, :]

    top_row = lax.broadcasted_iota(jnp.int32, (16, keys), 0)
    ones = jnp.where(top_row == 0, 1.0, 0.0).astype(bf16)
    for s in range(seqs):
        for h in range(HEADS):
            vt_s[s, h, 64:80, :] = ones
    mem = mem_o[...]
    mem_keys = dg(mem, weight(1), NN)
    mem_values = dg(mem, weight(2), NN) + bv
    mem_row = lax.broadcasted_iota(jnp.int32, (mem_pad, 1), 0)
    for s in range(seqs):
        put_keys(
            s, slice(length, keys), mem_keys, mem_values, jnp.where(mem_row < mem_rows, 0.0, HIDE)
        )
    tile = 512
    tiles = length // tile
    aux = jnp.where(lax.broadcasted_iota(jnp.int32, (64, tile), 0) == 0, 1.0, 0.0).astype(bf16)

    @pl.loop(0, seqs * tiles)
    def _(i):
        for slot, c, step in ((0, 3, 0), (2, 0, 2), (2, 1, 2), (3, 2, 1)):

            @pl.when(i == slot)
            def _():
                advance(c, step)

        s = i // tiles
        start = pl.multiple_of((i % tiles) * tile, tile)
        rows = pl.ds(start, tile)
        xt = x_ref[s, rows, :]
        qb = ((dg(xt, weight(0), NN) + bq) * (LOG2E * HEAD_DIM**-0.5)).astype(bf16)
        qt = qb.T
        for p in range(HEADS // 2):
            q_o[s, p, :, rows] = qt[128 * p : 128 * p + 128, :]
        for h in range(HEADS):
            e = h % 2
            qt_o[s, h, 64 * e : 64 * e + 64, rows] = qt[64 * h : 64 * h + 64, :]
            qt_o[s, h, 64 * (1 - e) : 64 * (1 - e) + 64, rows] = aux
        row = lax.broadcasted_iota(jnp.int32, (tile, 1), 0) + start
        put_keys(
            s,
            rows,
            dg(xt, weight(1), NN),
            dg(xt, weight(2), NN) + bv,
            jnp.where(row < len_ref[s], 0.0, HIDE),
        )

    block = score_a.shape[1]
    per_head = length // block
    blocks = seqs * HEADS * per_head

    def place(i):
        s = i // (HEADS * per_head)
        h = (i // per_head) % HEADS
        return s, h, pl.ds(pl.multiple_of((i % per_head) * block, block), block)

    cuts = [slice(c, c + 256) for c in range(0, length - 256, 256)] + [slice(length - 256, keys)]

    def turn(i, now, then):
        if i is not None:
            score, top, slot = now
            s, h, at = place(i)
            peak = top[...]
            mixed = 0.0
        if then is not None:
            next_i, next_score, next_top = then
            next_s, next_h, next_at = place(next_i)
            column = qt_o[next_s, next_h, :, next_at]
            high = None
        for cut in cuts:
            if then is not None:
                value = dg(ksel[next_s, next_h, cut, :], column, NN)
                next_score[cut, :] = value
                part = jnp.max(value.reshape(-1, 8, block), 0)
                high = part if high is None else jnp.maximum(high, part)
            if i is not None:
                weights = jnp.exp2(score[cut, :] - peak).astype(bf16)
                prob_s[slot + (cut, slice(None))] = weights
                mixed = mixed + dg(vt_s[s, h, :, cut], weights, NN)
        if then is not None:
            next_top[...] = jnp.max(high, 0, keepdims=True)
        if i is not None:
            prob_out(i, slot).start()
            inverse = 1.0 / mixed[64:65, :]
            att_o[s, h, :, at] = (mixed[0:64, :] * inverse).astype(bf16)
            inv_o[s, h, :, at] = inverse

    def prob_out(i, slot):
        s, h, _ = place(i)
        return pltpu.make_async_copy(
            prob_s.at[slot], prob_any.at[s, h, i % per_head], prob_sem.at[slot]
        )

    outs = [
        pltpu.make_async_copy(src, dst, out_sem.at[1 + n])
        for n, (src, dst) in enumerate(((q_o, q_any), (k_o, k_any), (v_o, v_any)))
    ]
    for out in outs:
        out.start()
    turn(None, None, (0, score_a, top_a))
    turns = blocks // 2
    heads_a_turn = max(1, 2 // per_head)

    def head_outs(j):
        s, h = j // HEADS, j % HEADS
        return [
            pltpu.make_async_copy(att_o.at[s, h], att_any.at[s, h], head_sem.at[j, 0]),
            pltpu.make_async_copy(inv_o.at[s, h], inv_any.at[s, h], head_sem.at[j, 1]),
        ]

    plan = ((0, 3, 1), (3, 0, 3), (4, 1, 3), (4, 2, 2), (5, 3, 2), (10, 2, 3), (11, 3, 3))

    @pl.loop(0, turns)
    def _(j):
        for slot, c, step in plan:

            @pl.when(j == (slot * turns) // 16)
            def _():
                advance(c, step)

        odd = j % 2

        @pl.when(j > 1)
        def _():
            for k in range(2):
                prob_out(2 * j - 4 + k, (odd, k)).wait()

        turn(2 * j, (score_a, top_a, (odd, 0)), (2 * j + 1, score_b, top_b))
        then = jnp.minimum(2 * j + 2, blocks - 1)
        turn(2 * j + 1, (score_b, top_b, (odd, 1)), (then, score_a, top_a))
        for k in range(heads_a_turn):
            for out in head_outs(j * heads_a_turn + k):
                out.start()

    for c in range(chunks):
        advance(c, steps)
    for j in range(max(0, turns - 2), turns):
        for k in range(2):
            prob_out(2 * j + k, (j % 2, k)).wait()
    for out in outs + [g1_out]:
        out.wait()

    @pl.loop(0, seqs * HEADS)
    def _(j):
        for out in head_outs(j):
            out.wait()


def attend_call(count, sub, lengths, x, wq, wk, wv, wo, wu, wd, memt, ub, vecs, mem_rows):
    seqs, length, width = x.shape
    r, ff, fr = wq.shape[0], wu.shape[1], wd.shape[0]
    rows2 = r + (ff // width) * r + fr
    keys = length + KEY_PAD
    nb = count.bit_length() - 1
    cube = (2,) * nb
    way = routes(nb)[0]
    links = (len(way), most(way))
    block = min(512, length)
    pairs = HEADS // 2
    shape = jax.ShapeDtypeStruct
    vm = pl.BlockSpec(memory_space=VMEM)
    hbm = pl.BlockSpec(memory_space=pl.ANY)
    dma = pltpu.SemaphoreType.DMA
    kept = (
        shape((seqs, pairs, 128, length), bf16),
        shape((seqs, pairs, 128, keys), bf16),
        shape((seqs, pairs, keys, 128), bf16),
        shape((seqs, HEADS, HEAD_DIM, length), bf16),
        shape((seqs, HEADS, 1, length), f32),
        shape(cube + (3 * r, width), bf16),
    )
    return pl.pallas_call(
        functools.partial(attend_kernel, count, sub, mem_rows),
        out_shape=kept
        + (
            shape((seqs, HEADS, length // block, keys, block), bf16),
            shape(cube + (rows2, width), bf16),
            shape((8, width), f32),
            shape((1, ff), f32),
            shape((KEY_PAD, width), bf16),
        ),
        in_specs=[pl.BlockSpec(memory_space=pltpu.SMEM), hbm] + [vm] * 16,
        out_specs=[hbm] * 8 + [vm] * 3,
        scratch_shapes=[VMEM(x.shape, bf16)]
        + [VMEM(a.shape, a.dtype) for a in kept]
        + [
            VMEM((seqs, HEADS, 128, length), bf16),
            VMEM(cube + (16, 128), bf16),
            VMEM((seqs, HEADS, keys, 128), bf16),
            VMEM((seqs, HEADS, 80, keys), bf16),
            VMEM((keys, block), f32),
            VMEM((keys, block), f32),
            VMEM((2, 2, keys, block), bf16),
            VMEM((1, block), f32),
            VMEM((1, block), f32),
            VMEM((16, 128), f32),
            VMEM((128, 128), f32),
            dma((2 + ff // width,)),
            dma,
            dma((4,)),
            dma((seqs * HEADS, 2)),
            dma((2, 2)),
            dma((2,) + links),
            dma((2,) + links),
            dma((4,) + links),
            dma((4,) + links),
            dma(links),
            dma(links),
        ],
        compiler_params=pltpu.CompilerParams(
            collective_id=0, has_side_effects=True, vmem_limit_bytes=60 * 2**20
        ),
        name="attend",
    )(lengths, x, wq, wk, wv, wo, wu, wd, memt, ub, *vecs)


def norm_forward(value, gain, shift):
    center = value - jnp.mean(value, -1, keepdims=True)
    inverse = lax.rsqrt(jnp.mean(center * center, -1, keepdims=True) + EPSILON)
    normed = center * inverse
    return normed * gain + shift, normed, inverse


def norm_backward(grad, normed, inverse, gain):
    scaled = grad * gain
    return inverse * (
        scaled
        - jnp.mean(scaled, -1, keepdims=True)
        - normed * jnp.mean(scaled * normed, -1, keepdims=True)
    )


def feed_kernel(
    r, fr, steps,
    x_ref, att_ref, dy_ref, g2, vec, ub,
    out_o, res_o, datt_o, part_o, gvec, gub,
    act_s, slope_s, low_s, outer_s, branch_s, gwo, gwu, gwd,
):
    i = pl.program_id(0)
    rows, width = x_ref.shape[1:]
    count = g2.shape[0]
    cols = g2.shape[1] // r - 1 - fr // r
    per = width // fr

    @pl.when(i == 0)
    def _():
        for ref in (gwo, gwu, gwd, gvec, gub):
            ref[...] = jnp.zeros_like(ref)

    bo, ga, sa, bd, gb, sb = [vec[j : j + 1, :] for j in range(2, 8)]

    def wo():
        return g2[:, 0:r, :].reshape(width, width)

    def wu(c):
        return g2[:, r + c * r : r + c * r + r, :].reshape(width, width)

    def wd(c):
        return g2[c * per : (c + 1) * per, r + cols * r :, :].reshape(width, width)

    class Part:
        def __init__(self, at):
            self.at = at

        def enter(self):
            branch = dg(att_ref[0, :, self.at], wo(), TN)
            value = x_ref[0, self.at, :].astype(f32) + branch + bo
            hidden, self.normed, self.inverse = norm_forward(value, ga, sa)
            self.low = hidden.astype(bf16)
            low_s[self.at, :] = self.low
            self.outer = hidden + bd

        def forward(self, c):
            u = dg(self.low, wu(c), NN) + ub[:, c * width : (c + 1) * width]
            bend = GELU_A + GELU_B * (u * u)
            gate = 0.5 + 0.5 * jnp.tanh(u * bend)
            act = u * gate
            low = act.astype(bf16)
            act_s[c][self.at, :] = low
            slope = gate + act * (1.0 - gate) * (6.0 * bend - 4.0 * GELU_A)
            slope_s[c][self.at, :] = slope.astype(bf16)
            self.outer = self.outer + dg(low, wd(c), NN)

        def turn(self):
            out, normed, inverse = norm_forward(self.outer, gb, sb)
            out_o[0, self.at, :] = out.astype(bf16)
            dy = dy_ref[0, self.at, :].astype(f32)
            gvec[6:7, :] += col_sum(dy * normed)
            gvec[7:8, :] += col_sum(dy)
            self.d_hidden = norm_backward(dy, normed, inverse, gb)
            gvec[5:6, :] += col_sum(self.d_hidden)
            self.d_outer = self.d_hidden.astype(bf16)
            outer_s[self.at, :] = self.d_outer

        def backward(self, c):
            d_act = dg(self.d_outer, wd(c), NT)
            d_inner = d_act * slope_s[c][self.at, :].astype(f32)
            gub[:, c * width : (c + 1) * width] += col_sum(d_inner)
            low = d_inner.astype(bf16)
            slope_s[c][self.at, :] = low
            self.d_hidden = self.d_hidden + dg(low, wu(c), NT)

        def leave(self):
            gvec[3:4, :] += col_sum(self.d_hidden * self.normed)
            gvec[4:5, :] += col_sum(self.d_hidden)
            d_res1 = norm_backward(self.d_hidden, self.normed, self.inverse, ga)
            res_o[0, self.at, :] = d_res1
            gvec[2:3, :] += col_sum(d_res1)
            d_branch = d_res1.astype(bf16)
            branch_s[self.at, :] = d_branch
            d_att = dg(d_branch, wo(), NT).astype(bf16)
            for p in range(width // 128):
                datt_o[0, p, self.at, :] = d_att[:, 128 * p : 128 * p + 128]

    half = rows // 2
    a, b = Part(slice(0, half)), Part(slice(half, rows))
    a.enter()
    b.enter()
    for c in range(cols):
        a.forward(c)
    b.forward(0)
    a.turn()
    for c in range(1, cols):
        b.forward(c)
    a.backward(0)
    b.turn()
    for c in range(1, cols):
        a.backward(c)
    b.backward(0)
    a.leave()
    for c in range(1, cols):
        b.backward(c)
    for c in range(cols):
        at = slice(c * width, (c + 1) * width)
        gwd[at, :] += dg(act_s[c][...], outer_s[...], TN)
        gwu[:, at] += dg(low_s[...], slope_s[c][...], TN)
        if c == 0:
            b.leave()
    gwo[...] += dg(att_ref[0], branch_s[...], NN)

    @pl.when(i == steps - 1)
    def _():
        part_o[:, 0:r, :] = gwo[...].astype(bf16).reshape(count, r, width)
        for c in range(cols):
            part_o[:, r + c * r : r + c * r + r, :] = (
                gwu[:, c * width : (c + 1) * width].astype(bf16).reshape(count, r, width)
            )
        part_o[:, r + cols * r :, :] = gwd[...].astype(bf16).reshape(count, fr, width)


def feed_call(x, att, dy, g2, vec, ub, r, fr):
    seqs, length, width = x.shape
    ff = ub.shape[1]
    tile = min(512, length)
    tiles = length // tile
    shape = jax.ShapeDtypeStruct
    rows = pl.BlockSpec((1, tile, width), lambda i: (i // tiles, i % tiles, 0))

    def full(a):
        return pl.BlockSpec(a.shape, lambda i: (0,) * len(a.shape))

    outs = (
        shape((seqs, length, width), bf16),
        shape((seqs, length, width), f32),
        shape((seqs, width // 128, length, 128), bf16),
        shape(g2.shape, bf16),
        shape((8, width), f32),
        shape((1, ff), f32),
    )
    return pl.pallas_call(
        functools.partial(feed_kernel, r, fr, seqs * tiles),
        grid=(seqs * tiles,),
        out_shape=outs,
        in_specs=[
            rows,
            pl.BlockSpec((1, width, tile), lambda i: (i // tiles, 0, i % tiles)),
            rows,
            full(g2),
            full(vec),
            full(ub),
        ],
        out_specs=[
            rows,
            rows,
            pl.BlockSpec((1, width // 128, tile, 128), lambda i: (i // tiles, 0, i % tiles, 0)),
        ]
        + [full(a) for a in outs[3:]],
        scratch_shapes=[
            [VMEM((tile, width), bf16)] * (ff // width),
            [VMEM((tile, width), bf16)] * (ff // width),
            VMEM((tile, width), bf16),
            VMEM((tile, width), bf16),
            VMEM((tile, width), bf16),
            VMEM((width, width), f32),
            VMEM((width, ff), f32),
            VMEM((ff, width), f32),
        ],
        compiler_params=pltpu.CompilerParams(vmem_limit_bytes=60 * 2**20),
        name="feed",
    )(x, att, dy, g2, vec, ub)


def pull_kernel(
    count, sub, mem_rows, r, fr,
    x_any, mem_ref, q_any, k_any, v_any, att_any, inv_any, prob_any, da_any, res_any, g1_any, part1,
    gvec_ref, gub_ref,
    dx_any, sums_o, small_o,
    x_ref, q_ref, k_ref, v_ref, att_ref, inv_ref, da_ref, res_ref, g1, dx_o,
    prob_s, vsel, dot_s, d_a, d_b, pt_s, dt_s, dq_s, dk_s, dv_s, dqt, dkt, dvt, dkm, dvm, part2, small_s, *rest,
):
    cube = Cube(count, sub)
    nb = cube.nb
    ways = [list(reversed(route)) for route in routes(nb)]
    steps = len(ways[0])
    bufs = [rest[k * steps : (k + 1) * steps] for k in range(8)]
    send, recv, load_sem, late_sem, out_sem, prob_sem = rest[8 * steps :]
    seqs, length, width = x_ref.shape
    keys = v_ref.shape[2]
    ff = gub_ref.shape[1]
    cols = ff // width
    half = width // 2
    halves = (slice(0, half), slice(half, width))
    pairs = HEADS // 2
    quarter = width // 4

    def scatter(n, source, lo, hi, way):
        return Scatter(cube, source, slice(lo, hi), ways[way], bufs[n], send.at[n], recv.at[n])

    feeds = [scatter(k, part1, k * quarter, (k + 1) * quarter, k % 2) for k in range(4)]
    first = [scatter(4, part2, 0, half, 0)]
    last = [scatter(5 + k, part2, half + k * quarter, half + (k + 1) * quarter, k) for k in range(2)]
    smalls = scatter(7, small_s, 0, 128, 0)

    def start(group, step):
        for part in group:
            for copy in part.copies(step):
                copy.start()

    def finish(group, step):
        for part in group:
            for copy in part.copies(step):
                copy.wait()
        if step < steps - 1:
            for part in group:
                part.add(step)

    def loads(j):
        p, s = j // seqs, j % seqs
        own = ((q_any, q_ref), (k_any, k_ref), (v_any, v_ref), (da_any, da_ref))
        out = [
            pltpu.make_async_copy(a.at[s, p], b.at[s, p], load_sem.at[j, n])
            for n, (a, b) in enumerate(own)
        ]
        both = pl.ds(2 * p, 2)
        return out + [
            pltpu.make_async_copy(a.at[s, both], b.at[s, both], load_sem.at[j, 4 + n])
            for n, (a, b) in enumerate(((att_any, att_ref), (inv_any, inv_ref)))
        ]

    def prob_load(j):
        p, s = j // seqs, j % seqs
        return pltpu.make_async_copy(
            prob_any.at[s, pl.ds(2 * p, 2)], prob_s.at[j % 2], prob_sem.at[j % 2]
        )

    late = [
        pltpu.make_async_copy(a, b, late_sem.at[n])
        for n, (a, b) in enumerate(((x_any, x_ref), (g1_any, g1), (res_any, res_ref)))
    ]

    prob_load(0).start()

    @pl.loop(0, seqs * pairs)
    def _(j):
        for load in loads(j):
            load.start()

    for load in late:
        load.start()
    cube.barrier(ways)
    start(feeds, 0)

    lane = lax.broadcasted_iota(jnp.int32, (1, 128), 1)
    block = d_a.shape[1]
    per_head = length // block
    temp = (d_a, d_b)

    def pair(j):
        p, s = j // seqs, j % seqs
        at = pl.ds(pl.multiple_of(128 * p, 128), 128)
        slot = j % 2
        vp = v_ref[s, p]
        dat = da_ref[s, p].T
        for e in range(2):
            o = 64 * (1 - e)
            mine = (lane < 64) if e == 0 else (lane >= 64)
            vsel[e] = jnp.where(
                mine, vp, jnp.where((lane >= o) & (lane < o + 2), 1.0, 0.0).astype(bf16)
            )
            dt = dat[64 * e : 64 * e + 64, :].astype(f32) * inv_ref[s, 2 * p + e]
            dot_s[e, 64 * e : 64 * e + 64, :] = dt.astype(bf16)
            delta = col_sum(dt * att_ref[s, 2 * p + e].astype(f32))
            hi = delta.astype(bf16).astype(f32)
            row = lax.broadcasted_iota(jnp.int32, (64, length), 0)
            dot_s[e, o : o + 64, :] = jnp.where(
                row == 0, -hi, jnp.where(row == 1, hi - delta, 0.0)
            ).astype(bf16)

        def grads(b):
            e, c = b // per_head, b % per_head
            cut = slice(c * block, (c + 1) * block)
            grad = dg(vsel[e], dot_s[e, :, cut], NN)
            temp[b % 2][...] = (prob_s[slot, e, c].astype(f32) * grad).astype(bf16)
            pt_s[b % 2] = prob_s[slot, e, c, 0:length, :].T
            dt_s[b % 2] = temp[b % 2][0:length, :].T

        def pulls(b):
            e, c = b // per_head, b % per_head
            cut = slice(c * block, (c + 1) * block)
            own = slice(64 * e, 64 * e + 64)
            grad = temp[b % 2]
            dqt[own, cut] = dg(k_ref[s, p, own, :], grad[...], NN)
            dots, queries = dot_s[e, own, cut], q_ref[s, p, own, cut]
            prob = prob_s.at[slot, e, c]
            news = (
                (dvt, dg(dots, pt_s[b % 2], NN)),
                (dkt, dg(queries, dt_s[b % 2], NN)),
                (dvm, dg(dots, prob[length:keys, :], NT)),
                (dkm, dg(queries, grad[length:keys, :], NT)),
            )
            for ref, new in news:
                to = slice(0, new.shape[1])
                if c == 0:
                    ref[own, to] = new
                else:
                    ref[own, to] += new

        grads(0)
        for b in range(2 * per_head):
            if b + 1 < 2 * per_head:
                grads(b + 1)
            pulls(b)
        dq_s[s, :, at] = dqt[...].astype(bf16).T
        for ref, tops, mems, unit in ((dk_s, dkt, dkm, LN2), (dv_s, dvt, dvm, 1.0)):
            ref[s, 0:length, at] = (tops[...] * unit).astype(bf16).T
            ref[s, length:keys, at] = ((mems[...] * unit).T)[0 : keys - length, :].astype(bf16)

    def weight(j):
        return g1[(slice(None),) * nb + (slice(j * r, j * r + r), slice(None))].reshape(width, width)

    scale = HEAD_DIM**-0.5
    tail = slice(length, keys)

    def terms(k):
        mem = mem_ref[...]
        for j, ref in enumerate((dq_s, dk_s, dv_s)):
            total = 0.0
            for s in range(seqs):
                total = total + dg(x_ref[s], ref[s, 0:length, halves[k]], TN)
                if j:
                    total = total + dg(mem, ref[s, tail, halves[k]], TN)
            if j == 0:
                total = total * scale
            cuts = (slice(None),) * nb + (slice(j * r, j * r + r), halves[k])
            part2[cuts] = total.astype(bf16).reshape((2,) * nb + (r, half))

    turns = seqs * pairs

    @pl.loop(0, turns)
    def _(j):
        @pl.when(j + 1 < turns)
        def _():
            prob_load(j + 1).start()

        for load in loads(j) + [prob_load(j)]:
            load.wait()

        plan = ((1, feeds, 0), (3, feeds[:2], 1), (4, feeds[2:], 1), (5, feeds[:2], 2))
        plan += ((6, feeds[2:], 2), (5, first, 0), (6, first, 1), (7, first, 2))
        for slot, group, step in plan:

            @pl.when(j == (slot * turns) // 8)
            def _():
                finish(group, step)
                start(group, step + 1)

        @pl.when(j == turns // 2)
        def _():
            for load in late:
                load.wait()
            terms(0)
            start(first, 0)

        pair(j)

    terms(1)
    start(last, 0)
    bq = sum(col_sum(dq_s[s].astype(f32)) for s in range(seqs)) * scale
    bv = sum(col_sum(dv_s[s].astype(f32)) for s in range(seqs))
    gmem = sum(
        dg(dk_s[s, tail, :], weight(1), NT) + dg(dv_s[s, tail, :], weight(2), NT)
        for s in range(seqs)
    )
    vec_row = lax.broadcasted_iota(jnp.int32, (8, width), 0)
    vecs = jnp.where(vec_row == 0, bq, jnp.where(vec_row == 1, bv, gvec_ref[...]))
    flat = jnp.concatenate(
        [
            gmem[0:16, :],
            jnp.concatenate([gmem[16:20, :], vecs[0:4, :]], 0),
            jnp.concatenate([vecs[4:8, :], jnp.zeros((4, width), f32)], 0),
            jnp.zeros((96, width), f32),
        ],
        0,
    )
    small_s[...] = flat.T.reshape((2,) * nb + (16, 128))
    for i in range(count):
        at = tuple((i >> b) & 1 for b in cube.msb_first)
        off = (i * fr) % 128
        up = jnp.broadcast_to(gub_ref[:, i * fr - off : i * fr - off + 128], (8, 128))
        up = pltpu.roll(up, (64 - off) % 128, 1)
        small_s[at + (slice(0, 1), slice(64, 64 + fr))] = up[0:1, 64 : 64 + fr]
    start([smalls], 0)
    tile = 512
    tiles = length // tile

    def inputs(i):
        s, rows = i // tiles, pl.ds((i % tiles) * tile, tile)
        dx = res_ref[s, rows, :] + dg(dq_s[s, rows, :], weight(0), NT) * scale
        dx = dx + dg(dk_s[s, rows, :], weight(1), NT) + dg(dv_s[s, rows, :], weight(2), NT)
        dx_o[s, rows, :] = dx.astype(bf16)
        out = pltpu.make_async_copy(dx_o.at[s, rows], dx_any.at[s, rows], out_sem.at[i])
        out.start()
        return out

    def total(part, lo, hi):
        sums_o[lo:hi, part.lanes] = part.total(steps - 1)

    todo = list(range(seqs * tiles))
    outs = []
    group = last + [smalls]
    for step in range(steps):
        if todo:
            outs.append(inputs(todo.pop(0)))
        if step == steps - 2:
            finish(feeds + first, steps - 1)
            for part in feeds:
                total(part, 3 * r, sums_o.shape[0])
            total(first[0], 0, 3 * r)
        finish(group, step)
        if step + 1 < steps:
            start(group, step + 1)
    for i in todo:
        outs.append(inputs(i))
    for part in last:
        total(part, 0, 3 * r)
    small_o[...] = smalls.total(steps - 1)
    for out in outs:
        out.wait()


def pull_call(count, sub, mem_rows, r, fr, x, mem, q, k, v, att, inv, prob, da, res, g1, part1, gvec, gub):
    seqs, length, width = x.shape
    keys = v.shape[2]
    rows2 = part1.shape[-2]
    nb = count.bit_length() - 1
    cube = (2,) * nb
    way = list(reversed(routes(nb)[0]))
    links = (len(way), most(way))
    block = prob.shape[4]
    half, quarter = width // 2, width // 4
    turns = seqs * (HEADS // 2)
    shape = jax.ShapeDtypeStruct
    vm = pl.BlockSpec(memory_space=VMEM)
    hbm = pl.BlockSpec(memory_space=pl.ANY)
    dma = pltpu.SemaphoreType.DMA
    return pl.pallas_call(
        functools.partial(pull_kernel, count, sub, mem_rows, r, fr),
        out_shape=(
            shape((seqs, length, width), bf16),
            shape((3 * r + rows2, width), f32),
            shape((16, 128), f32),
        ),
        in_specs=[hbm, vm] + [hbm] * 9 + [vm] * 3,
        out_specs=[hbm, vm, vm],
        scratch_shapes=[VMEM(a.shape, a.dtype) for a in (x, q, k, v, att, inv, da, res, g1, x)]
        + [
            VMEM((2, 2) + prob.shape[2:], bf16),
            VMEM((2, keys, 128), bf16),
            VMEM((2, 128, length), bf16),
            VMEM((keys, block), bf16),
            VMEM((keys, block), bf16),
            VMEM((2, block, length), bf16),
            VMEM((2, block, length), bf16),
            VMEM((seqs, length, width), bf16),
            VMEM((seqs, keys, width), bf16),
            VMEM((seqs, keys, width), bf16),
            VMEM((128, length), f32),
            VMEM((128, length), f32),
            VMEM((128, length), f32),
            VMEM((128, KEY_PAD), f32),
            VMEM((128, KEY_PAD), f32),
            VMEM(cube + (3 * r, width), bf16),
            VMEM(cube + (16, 128), f32),
        ]
        + scatter_bufs(nb, way, (rows2, quarter), bf16) * 4
        + scatter_bufs(nb, way, (3 * r, half), bf16)
        + scatter_bufs(nb, way, (3 * r, quarter), bf16) * 2
        + scatter_bufs(nb, way, (16, 128), f32)
        + [dma((8,) + links)] * 2
        + [dma((turns, 6)), dma((3,)), dma((seqs * (length // 512),)), dma((2,))],
        compiler_params=pltpu.CompilerParams(
            collective_id=1, has_side_effects=True, vmem_limit_bytes=62 * 2**20
        ),
        name="pull",
    )(x, mem, q, k, v, att, inv, prob, da, res, g1, part1, gvec, gub)


def results_kernel(r, fr, mem_rows, dx_ref, sums, small, dx_o, *outs):
    outs, sem = outs[:-1], outs[-1]
    move = pltpu.make_async_copy(dx_ref, dx_o, sem)
    move.start()
    gq, gk, gv, go, gu, gd, gm, gb = outs[:8]
    vecs = outs[8:]
    width = gq.shape[1]
    cols = gu.shape[1] // width
    for n, ref in enumerate((gq, gk, gv, go)):
        ref[...] = sums[n * r : (n + 1) * r, :]
    for c in range(cols):
        gu[:, c * width : (c + 1) * width] = sums[(4 + c) * r : (5 + c) * r, :]
    gd[...] = sums[(4 + cols) * r :, :]
    value = small[...]
    gm[...] = value[0:r, 0:mem_rows]
    turned = jnp.concatenate([value, jnp.zeros((112, 128), f32)], 0).T
    for n, ref in enumerate(vecs):
        ref[...] = turned[VEC + n : VEC + n + 1, 0:r]
    gb[...] = value[0:1, 64 : 64 + fr]
    move.wait()


def results_call(r, fr, mem_rows, ff, dx, sums, small):
    width = sums.shape[1]
    shape = jax.ShapeDtypeStruct
    vm = pl.BlockSpec(memory_space=VMEM)
    hbm = pl.BlockSpec(memory_space=pl.ANY)
    mats = [(r, width)] * 4 + [(r, ff), (fr, width), (r, mem_rows), (1, fr)] + [(1, r)] * 8
    return pl.pallas_call(
        functools.partial(results_kernel, r, fr, mem_rows),
        out_shape=(shape(dx.shape, dx.dtype),) + tuple(shape(m, f32) for m in mats),
        in_specs=[vm, vm, vm],
        out_specs=[hbm] + [vm] * len(mats),
        scratch_shapes=[pltpu.SemaphoreType.DMA],
        name="results",
    )(dx, sums, small)


DIMS = (1, 0, 0, 0, 0, 0, 0, 0, 0, 0, 0, 0, 0, 0, 0, 0)


def on_device(devices, inputs, lengths, *rest):
    params, cotangent = rest[:-1], rest[-1]
    width = inputs.shape[2]
    count = min(devices, width // 16)
    sub = devices // count
    sets = [list(range(g * sub, (g + 1) * sub)) for g in range(count)]
    if sub > 1:
        params = tuple(
            lax.all_gather(a, "dp", axis=d, tiled=True, axis_index_groups=sets)
            for a, d in zip(params, DIMS, strict=True)
        )
    (memory, wq, bq, wk, wv, bv, wo, bo, ga, sa, wu, bu, wd, bd, gb, sb) = params
    r, fr = wq.shape[0], wd.shape[0]
    mem_rows = memory.shape[0]

    vecs = [a.reshape(1, r) for a in (bq, bv, bo, ga, sa, bd, gb, sb)]
    q, k, v, att, inv, g1, prob, g2, vec, ub, mem = attend_call(
        count, sub, lengths, inputs, wq, wk, wv, wo, wu, wd, memory.T, bu.reshape(1, fr), vecs, mem_rows
    )
    seqs, length = inputs.shape[:2]
    layer_out, res, datt, part1, gvec, gub = feed_call(
        inputs,
        att.reshape(seqs, width, length),
        cotangent,
        g2.reshape((count,) + g2.shape[-2:]),
        vec,
        ub,
        r,
        fr,
    )
    dx, sums, tiny = pull_call(
        count, sub, mem_rows, r, fr, inputs, mem, q, k, v, att, inv, prob, datt, res, g1,
        part1.reshape(g2.shape), gvec, gub,
    )
    dx, gwq, gwk, gwv, gwo, gwu, gwd, gmem, gbu, *vecs = results_call(
        r, fr, mem_rows, wu.shape[1], dx, sums, tiny
    )
    gmem = gmem.T
    gbu = gbu.reshape(fr)
    gbq, gbv, gbo, gga, gsa, gbd, ggb, gsb = [a.reshape(r) for a in vecs]
    grads = (gmem, gwq, gbq, gwk, gwv, gbv, gwo, gbo, gga, gsa, gwu, gbu, gwd, gbd, ggb, gsb)
    if sub > 1:
        grads = tuple(
            lax.psum_scatter(a, "dp", scatter_dimension=d, tiled=True, axis_index_groups=sets)
            for a, d in zip(grads, DIMS, strict=True)
        )
    return (layer_out, dx) + grads


def solution(mesh):
    rows, row, mem = P("dp", None), P("dp"), P(None, "dp")
    full = P("dp", None, None)
    params = (mem, rows, row, rows, rows, row, rows, row, row, row, rows, row, rows, row, row, row)
    return jax.shard_map(
        functools.partial(on_device, mesh.shape["dp"]),
        mesh=mesh,
        in_specs=(full, P("dp")) + params + (full,),
        out_specs=(full, full) + params,
        check_vma=False,
    )
```

```python
import functools

import jax
import jax.numpy as jnp
from jax import lax
from jax.experimental import pallas as pl
from jax.experimental.pallas import tpu as pltpu
from jax.sharding import PartitionSpec as P

HEADS = 8
HEAD_DIM = 64
EPSILON = 1e-05
LOG2E = 1.4426950408889634
LN2 = 0.6931471805599453
GELU_A = 0.7978845608028654
GELU_B = GELU_A * 0.044715
HIDE = -1e30
VEC = 20
KEY_PAD = 32

f32 = jnp.float32
bf16 = jnp.bfloat16
VMEM = pltpu.VMEM
MESH = pl.DeviceIdType.MESH
NN = (((1,), (0,)), ((), ()))
NT = (((1,), (1,)), ((), ()))
TN = (((0,), (0,)), ((), ()))


def dg(left, right, dims):
    return lax.dot_general(left, right, dims, preferred_element_type=f32)


def col_sum(value):
    return jnp.sum(value, 0, keepdims=True)


class Cube:
    def __init__(self, count, sub):
        self.count, self.sub = count, sub
        self.nb = count.bit_length() - 1
        device = lax.axis_index("dp")
        self.device = device
        me = device // sub
        self.bits = [(me // (2**b)) % 2 for b in range(self.nb)]
        self.msb_first = tuple(range(self.nb - 1, -1, -1))

    def partner(self, flips):
        to = self.device
        for b in flips:
            to = to + (1 - 2 * self.bits[b]) * (2**b * self.sub)
        return (to,)

    def barrier(self, routes):
        groups = sorted({flips for route in routes for group in route for flips in masks(group)})
        sem = pltpu.get_barrier_semaphore()
        for flips in groups:
            pl.semaphore_signal(sem, inc=1, device_id=self.partner(flips), device_id_type=MESH)
        pl.semaphore_wait(sem, len(groups))

    def own(self):
        return tuple(self.bits[b] for b in self.msb_first)


def masks(group):
    return [
        tuple(b for k, b in enumerate(group) if (m >> k) & 1) for m in range(1, 2 ** len(group))
    ]


def routes(nb):
    if nb >= 4:
        far = list(range(nb - 1, 2, -1))
        groups = [tuple(far[k : k + 2]) for k in range(0, len(far), 2)]
        return (groups + [(1,), (2,), (0,)], groups + [(2,), (1,), (0,)])
    return ([(b,) for b in range(nb - 1, -1, -1)],) * 2


def short(route):
    if len(route) != 4:
        return route
    return [route[0], route[1] + route[2], route[3]]


def most(route):
    return max(2 ** len(group) - 1 for group in route)


def gather_copies(cube, ref, route, step, rows, lanes, send, recv):
    done = {b for group in route[:step] for b in group}
    idx = tuple(slice(None) if c in done else cube.bits[c] for c in cube.msb_first)
    view = ref.at[idx + (rows, lanes)]
    return [
        pltpu.make_async_remote_copy(
            src_ref=view,
            dst_ref=view,
            send_sem=send.at[step, k],
            recv_sem=recv.at[step, k],
            device_id=cube.partner(flips),
            device_id_type=MESH,
        )
        for k, flips in enumerate(masks(route[step]))
    ]


class Scatter:
    def __init__(self, cube, source, lanes, route, bufs, send, recv):
        self.cube, self.source, self.lanes, self.route = cube, source, lanes, route
        self.bufs, self.send, self.recv = bufs, send, recv
        self.steps = len(route)

    def _piece(self, step, flips, rest=None):
        cube = self.cube
        gone = {b for group in self.route[:step] for b in group}
        left = [c for c in cube.msb_first if c not in gone]
        rest = iter(rest) if rest is not None else None
        idx = ()
        for c in left:
            if c in self.route[step]:
                idx += (1 - cube.bits[c] if c in flips else cube.bits[c],)
            else:
                idx += (slice(None) if rest is None else next(rest),)
        if step == 0:
            return self.source, idx + (slice(None), self.lanes)
        return self.bufs[step - 1].at[0], idx

    def copies(self, step):
        out = []
        for k, flips in enumerate(masks(self.route[step])):
            ref, idx = self._piece(step, flips)
            out.append(
                pltpu.make_async_remote_copy(
                    src_ref=ref.at[idx],
                    dst_ref=self.bufs[step].at[k],
                    send_sem=self.send.at[step, k],
                    recv_sem=self.recv.at[step, k],
                    device_id=self.cube.partner(flips),
                    device_id_type=MESH,
                )
            )
        return out

    def total(self, step, rest=None):
        ref, idx = self._piece(step, (), rest)
        value = ref[idx].astype(f32)
        for k in range(2 ** len(self.route[step]) - 1):
            value = value + self.bufs[step][(k,) + tuple(rest or ())].astype(f32)
        return value

    def add(self, step):
        free = self.cube.nb - sum(len(group) for group in self.route[: step + 1])
        into = self.bufs[step]
        for flat in range(2**free):
            rest = tuple((flat >> (free - 1 - k)) & 1 for k in range(free))
            into[(0,) + rest] = self.total(step, rest).astype(into.dtype)


def scatter_bufs(nb, route, tail, dtype):
    bufs, left = [], nb
    for group in route:
        left -= len(group)
        bufs.append(VMEM((2 ** len(group) - 1,) + (2,) * left + tail, dtype))
    return bufs


def attend_kernel(
    count, sub, mem_rows,
    len_ref, x_any, wq_ref, wk_ref, wv_ref, wo_ref, wu_ref, wd_ref, memt_ref, ub_ref, *rest,
):
    vec_refs, rest = rest[:8], rest[8:]
    (
    q_any, k_any, v_any, att_any, inv_any, g1_any, prob_any, g2, vec_o, ub_o, mem_o,
    x_ref, q_o, k_o, v_o, att_o, inv_o, g1,
    qt_o, gs, ksel, vt_s, score_a, score_b, prob_s, top_a, top_b,
    flat_s, wide_s,
    local, x_sem, out_sem, head_sem, prob_sem, send1, recv1, send2, recv2, send3, recv3,
    ) = rest
    cube = Cube(count, sub)
    nb = cube.nb
    seqs, length, width = x_ref.shape
    keys = v_o.shape[2]
    mem_pad = keys - length
    r = wq_ref.shape[0]
    ff = wu_ref.shape[1]
    cols = ff // width
    fr = wd_ref.shape[0]
    own = cube.own()
    ways = routes(nb)
    steps = len(ways[0])
    half = width // 2
    halves = (slice(0, half), slice(half, width))
    whole = (slice(None), slice(None))
    x_load = pltpu.make_async_copy(x_any, x_ref, x_sem)
    x_load.start()
    for j, ref in enumerate((wq_ref, wk_ref, wv_ref)):
        g1[own + (slice(j * r, j * r + r), slice(None))] = ref[...]
    wide_s[...] = jnp.zeros_like(wide_s)
    flat_s[...] = jnp.zeros_like(flat_s)
    for j, ref in enumerate(vec_refs):
        wide_s[VEC + j : VEC + j + 1, 0:r] = ref[...].astype(f32)
    flat_s[0:r, 0:mem_rows] = memt_ref[...].astype(f32)
    flat_s[0:1, 64 : 64 + fr] = ub_ref[...].astype(f32)
    gs[own + whole] = (flat_s[...] + wide_s[...].T[0:16, :]).astype(bf16)
    parts = [(wo_ref, slice(0, r))]
    parts += [
        (wu_ref.at[:, c * width : (c + 1) * width], slice(r + c * r, r + c * r + r))
        for c in range(cols)
    ]
    parts += [(wd_ref, slice(r + cols * r, r + cols * r + fr))]
    moves = [
        pltpu.make_async_copy(ref, g2.at[own + (rows, slice(None))], local.at[j])
        for j, (ref, rows) in enumerate(parts)
    ]
    for move in moves:
        move.start()
    cube.barrier(ways)

    every_row = slice(None)

    def first(j, step):
        rows = slice(j * r, j * r + r)
        copies = []
        for k in range(2):
            links = (send1.at[2 * j + k], recv1.at[2 * j + k])
            copies += gather_copies(cube, g1, ways[k], step, rows, halves[k], *links)
        return copies

    def tiny(step):
        return gather_copies(cube, gs, ways[0], step, every_row, slice(None), send3, recv3)

    chunks = 4
    chunk = width // chunks

    def second(c, step):
        lanes = slice(c * chunk, (c + 1) * chunk)
        return gather_copies(
            cube, g2, ways[c % 2], step, every_row, lanes, send2.at[c], recv2.at[c]
        )

    def advance(c, step):
        if step > 0:
            for copy in second(c, step - 1):
                copy.wait()
        if step < steps:
            for copy in second(c, step):
                copy.start()

    sets = [functools.partial(first, 1), tiny, functools.partial(first, 2), functools.partial(first, 0)]
    for copies in sets:
        for copy in copies(0):
            copy.start()
    for move in moves:
        move.wait()
    for step in range(1, steps):
        for copies in sets:
            for copy in copies(step - 1):
                copy.wait()
            for copy in copies(step):
                copy.start()
        if step == 1:
            for c in range(chunks):
                advance(c, 0)

    def arrived(n):
        for copy in sets[n](steps - 1):
            copy.wait()

    arrived(0)
    arrived(1)
    x_load.wait()

    lane = lax.broadcasted_iota(jnp.int32, (1, 128), 1)
    every = gs[...].astype(f32).reshape(width, 128).T
    mem_o[0:16, :] = every[0:16, :].astype(bf16)
    rest_row = lax.broadcasted_iota(jnp.int32, (16, width), 0)
    mem_o[16:32, :] = jnp.where(rest_row < mem_rows - 16, every[16:32, :], 0.0).astype(bf16)
    vec_o[...] = every[VEC : VEC + 8, :]
    ups = [jnp.zeros((16, 128), f32) for _ in range(ff // 128)]
    for i in range(count):
        at = tuple((i >> b) & 1 for b in cube.msb_first)
        to = (i * fr) % 128
        here = (lane >= to) & (lane < to + fr)
        rolled = pltpu.roll(gs[at + whole].astype(f32), (to - 64) % 128, 1)
        ups[i * fr // 128] = ups[i * fr // 128] + jnp.where(here, rolled, 0.0)
    for g in range(ff // 128):
        ub_o[:, 128 * g : 128 * g + 128] = ups[g][0:1, :]

    def weight(j):
        return g1[(slice(None),) * nb + (slice(j * r, j * r + r), slice(None))].reshape(width, width)

    bq = vec_o[0:1, :]
    bv = vec_o[1:2, :]

    def put_keys(s, rows, kk, bias):
        kb = kk.astype(bf16)
        kt = kb.T
        for p in range(HEADS // 2):
            k_o[s, p, :, rows] = kt[128 * p : 128 * p + 128, :]
        for h in range(HEADS):
            p, o = h // 2, 64 * (1 - h % 2)
            pattern = jnp.where(lane == o, bias, 0.0).astype(bf16)
            mine = (lane < 64) if h % 2 == 0 else (lane >= 64)
            ksel[s, h, rows, :] = jnp.where(mine, kb[:, 128 * p : 128 * p + 128], pattern)

    def put_values(s, rows, vv):
        vb = vv.astype(bf16)
        vt = vb.T
        for p in range(HEADS // 2):
            v_o[s, p, rows, :] = vb[:, 128 * p : 128 * p + 128]
        for h in range(HEADS):
            vt_s[s, h, 0:64, rows] = vt[64 * h : 64 * h + 64, :]

    top_row = lax.broadcasted_iota(jnp.int32, (16, keys), 0)
    ones = jnp.where(top_row == 0, 1.0, 0.0).astype(bf16)
    for s in range(seqs):
        for h in range(HEADS):
            vt_s[s, h, 64:80, :] = ones
    mem = mem_o[...]
    mem_keys = dg(mem, weight(1), NN)
    mem_row = lax.broadcasted_iota(jnp.int32, (mem_pad, 1), 0)
    mem_bias = jnp.where(mem_row < mem_rows, 0.0, HIDE)
    for s in range(seqs):
        put_keys(s, slice(length, keys), mem_keys, mem_bias)
    tile = 512
    tiles = length // tile
    aux = jnp.where(lax.broadcasted_iota(jnp.int32, (64, tile), 0) == 0, 1.0, 0.0).astype(bf16)

    def place_rows(i):
        start = pl.multiple_of((i % tiles) * tile, tile)
        return i // tiles, start, pl.ds(start, tile)

    @pl.loop(0, seqs * tiles)
    def _(i):
        s, start, rows = place_rows(i)
        row = lax.broadcasted_iota(jnp.int32, (tile, 1), 0) + start
        bias = jnp.where(row < len_ref[s], 0.0, HIDE)
        put_keys(s, rows, dg(x_ref[s, rows, :], weight(1), NN), bias)

    arrived(2)
    mem_values = dg(mem, weight(2), NN) + bv
    for s in range(seqs):
        put_values(s, slice(length, keys), mem_values)

    @pl.loop(0, seqs * tiles)
    def _(i):
        s, start, rows = place_rows(i)
        put_values(s, rows, dg(x_ref[s, rows, :], weight(2), NN) + bv)

    arrived(3)
    advance(0, 1)
    advance(1, 1)
    g1_out = pltpu.make_async_copy(g1, g1_any, out_sem.at[0])
    g1_out.start()

    @pl.loop(0, seqs * tiles)
    def _(i):
        s, start, rows = place_rows(i)
        qb = ((dg(x_ref[s, rows, :], weight(0), NN) + bq) * (LOG2E * HEAD_DIM**-0.5)).astype(bf16)
        qt = qb.T
        for p in range(HEADS // 2):
            q_o[s, p, :, rows] = qt[128 * p : 128 * p + 128, :]
        for h in range(HEADS):
            e = h % 2
            qt_o[s, h, 64 * e : 64 * e + 64, rows] = qt[64 * h : 64 * h + 64, :]
            qt_o[s, h, 64 * (1 - e) : 64 * (1 - e) + 64, rows] = aux

    block = score_a.shape[1]
    per_head = length // block
    blocks = seqs * HEADS * per_head

    def place(i):
        s = i // (HEADS * per_head)
        h = (i // per_head) % HEADS
        return s, h, pl.ds(pl.multiple_of((i % per_head) * block, block), block)

    cuts = [slice(c, c + 256) for c in range(0, length - 256, 256)] + [slice(length - 256, keys)]

    def turn(i, now, then):
        if i is not None:
            score, top, slot = now
            s, h, at = place(i)
            peak = top[...]
            mixed = 0.0
        if then is not None:
            next_i, next_score, next_top = then
            next_s, next_h, next_at = place(next_i)
            column = qt_o[next_s, next_h, :, next_at]
            high = None
        for cut in cuts:
            if then is not None:
                value = dg(ksel[next_s, next_h, cut, :], column, NN)
                next_score[cut, :] = value
                part = jnp.max(value.reshape(-1, 8, block), 0)
                high = part if high is None else jnp.maximum(high, part)
            if i is not None:
                weights = jnp.exp2(score[cut, :] - peak).astype(bf16)
                prob_s[slot + (cut, slice(None))] = weights
                mixed = mixed + dg(vt_s[s, h, :, cut], weights, NN)
        if then is not None:
            next_top[...] = jnp.max(high, 0, keepdims=True)
        if i is not None:
            prob_out(i, slot).start()
            inverse = 1.0 / mixed[64:65, :]
            att_o[s, h, :, at] = (mixed[0:64, :] * inverse).astype(bf16)
            inv_o[s, h, :, at] = inverse

    def prob_out(i, slot):
        s, h, _ = place(i)
        return pltpu.make_async_copy(
            prob_s.at[slot], prob_any.at[s, h, i % per_head], prob_sem.at[slot]
        )

    outs = [
        pltpu.make_async_copy(src, dst, out_sem.at[1 + n])
        for n, (src, dst) in enumerate(((q_o, q_any), (k_o, k_any), (v_o, v_any)))
    ]
    for out in outs:
        out.start()
    turn(None, None, (0, score_a, top_a))
    turns = blocks // 2
    heads_a_turn = max(1, 2 // per_head)

    def head_outs(j):
        s, h = j // HEADS, j % HEADS
        return [
            pltpu.make_async_copy(att_o.at[s, h], att_any.at[s, h], head_sem.at[j, 0]),
            pltpu.make_async_copy(inv_o.at[s, h], inv_any.at[s, h], head_sem.at[j, 1]),
        ]

    plan = ((2, 0, 2), (2, 1, 2), (3, 2, 1), (3, 3, 1), (9, 0, 3), (9, 1, 3), (9, 2, 2), (9, 3, 2))
    plan += ((15, 2, 3), (15, 3, 3))

    @pl.loop(0, turns)
    def _(j):
        for slot, c, step in plan:

            @pl.when(j == (slot * turns) // 16)
            def _():
                advance(c, step)

        odd = j % 2

        @pl.when(j > 1)
        def _():
            for k in range(2):
                prob_out(2 * j - 4 + k, (odd, k)).wait()

        turn(2 * j, (score_a, top_a, (odd, 0)), (2 * j + 1, score_b, top_b))
        then = jnp.minimum(2 * j + 2, blocks - 1)
        turn(2 * j + 1, (score_b, top_b, (odd, 1)), (then, score_a, top_a))
        for k in range(heads_a_turn):
            for out in head_outs(j * heads_a_turn + k):
                out.start()

    for c in range(chunks):
        advance(c, steps)
    for j in range(max(0, turns - 2), turns):
        for k in range(2):
            prob_out(2 * j + k, (j % 2, k)).wait()
    for out in outs + [g1_out]:
        out.wait()

    @pl.loop(0, seqs * HEADS)
    def _(j):
        for out in head_outs(j):
            out.wait()


def attend_call(count, sub, lengths, x, wq, wk, wv, wo, wu, wd, memt, ub, vecs, mem_rows):
    seqs, length, width = x.shape
    r, ff, fr = wq.shape[0], wu.shape[1], wd.shape[0]
    rows2 = r + (ff // width) * r + fr
    keys = length + KEY_PAD
    nb = count.bit_length() - 1
    cube = (2,) * nb
    way = routes(nb)[0]
    links = (len(way), most(way))
    block = min(512, length)
    pairs = HEADS // 2
    shape = jax.ShapeDtypeStruct
    vm = pl.BlockSpec(memory_space=VMEM)
    hbm = pl.BlockSpec(memory_space=pl.ANY)
    dma = pltpu.SemaphoreType.DMA
    kept = (
        shape((seqs, pairs, 128, length), bf16),
        shape((seqs, pairs, 128, keys), bf16),
        shape((seqs, pairs, keys, 128), bf16),
        shape((seqs, HEADS, HEAD_DIM, length), bf16),
        shape((seqs, HEADS, 1, length), f32),
        shape(cube + (3 * r, width), bf16),
    )
    return pl.pallas_call(
        functools.partial(attend_kernel, count, sub, mem_rows),
        out_shape=kept
        + (
            shape((seqs, HEADS, length // block, keys, block), bf16),
            shape(cube + (rows2, width), bf16),
            shape((8, width), f32),
            shape((1, ff), f32),
            shape((KEY_PAD, width), bf16),
        ),
        in_specs=[pl.BlockSpec(memory_space=pltpu.SMEM), hbm] + [vm] * 16,
        out_specs=[hbm] * 8 + [vm] * 3,
        scratch_shapes=[VMEM(x.shape, bf16)]
        + [VMEM(a.shape, a.dtype) for a in kept]
        + [
            VMEM((seqs, HEADS, 128, length), bf16),
            VMEM(cube + (16, 128), bf16),
            VMEM((seqs, HEADS, keys, 128), bf16),
            VMEM((seqs, HEADS, 80, keys), bf16),
            VMEM((keys, block), f32),
            VMEM((keys, block), f32),
            VMEM((2, 2, keys, block), bf16),
            VMEM((1, block), f32),
            VMEM((1, block), f32),
            VMEM((16, 128), f32),
            VMEM((128, 128), f32),
            dma((2 + ff // width,)),
            dma,
            dma((4,)),
            dma((seqs * HEADS, 2)),
            dma((2, 2)),
            dma((6,) + links),
            dma((6,) + links),
            dma((4,) + links),
            dma((4,) + links),
            dma(links),
            dma(links),
        ],
        compiler_params=pltpu.CompilerParams(
            collective_id=0, has_side_effects=True, vmem_limit_bytes=60 * 2**20
        ),
        name="attend",
    )(lengths, x, wq, wk, wv, wo, wu, wd, memt, ub, *vecs)


def norm_forward(value, gain, shift):
    center = value - jnp.mean(value, -1, keepdims=True)
    inverse = lax.rsqrt(jnp.mean(center * center, -1, keepdims=True) + EPSILON)
    normed = center * inverse
    return normed * gain + shift, normed, inverse


def norm_backward(grad, normed, inverse, gain):
    scaled = grad * gain
    return inverse * (
        scaled
        - jnp.mean(scaled, -1, keepdims=True)
        - normed * jnp.mean(scaled * normed, -1, keepdims=True)
    )


def feed_kernel(
    r, fr, steps,
    x_ref, att_ref, dy_ref, g2, vec, ub,
    out_o, res_o, datt_o, part_o, gvec, gub,
    act_s, slope_s, low_s, outer_s, branch_s, gwo, gwu, gwd,
):
    i = pl.program_id(0)
    rows, width = x_ref.shape[1:]
    count = g2.shape[0]
    cols = g2.shape[1] // r - 1 - fr // r
    per = width // fr

    @pl.when(i == 0)
    def _():
        for ref in (gwo, gwu, gwd, gvec, gub):
            ref[...] = jnp.zeros_like(ref)

    bo, ga, sa, bd, gb, sb = [vec[j : j + 1, :] for j in range(2, 8)]

    def wo():
        return g2[:, 0:r, :].reshape(width, width)

    def wu(c):
        return g2[:, r + c * r : r + c * r + r, :].reshape(width, width)

    def wd(c):
        return g2[c * per : (c + 1) * per, r + cols * r :, :].reshape(width, width)

    class Part:
        def __init__(self, at):
            self.at = at

        def enter(self):
            branch = dg(att_ref[0, :, self.at], wo(), TN)
            value = x_ref[0, self.at, :].astype(f32) + branch + bo
            hidden, self.normed, self.inverse = norm_forward(value, ga, sa)
            self.low = hidden.astype(bf16)
            low_s[self.at, :] = self.low
            self.outer = hidden + bd

        def forward(self, c):
            u = dg(self.low, wu(c), NN) + ub[:, c * width : (c + 1) * width]
            bend = GELU_A + GELU_B * (u * u)
            gate = 0.5 + 0.5 * jnp.tanh(u * bend)
            act = u * gate
            low = act.astype(bf16)
            act_s[c][self.at, :] = low
            slope = gate + act * (1.0 - gate) * (6.0 * bend - 4.0 * GELU_A)
            slope_s[c][self.at, :] = slope.astype(bf16)
            self.outer = self.outer + dg(low, wd(c), NN)

        def turn(self):
            out, normed, inverse = norm_forward(self.outer, gb, sb)
            out_o[0, self.at, :] = out.astype(bf16)
            dy = dy_ref[0, self.at, :].astype(f32)
            gvec[6:7, :] += col_sum(dy * normed)
            gvec[7:8, :] += col_sum(dy)
            self.d_hidden = norm_backward(dy, normed, inverse, gb)
            gvec[5:6, :] += col_sum(self.d_hidden)
            self.d_outer = self.d_hidden.astype(bf16)
            outer_s[self.at, :] = self.d_outer

        def backward(self, c):
            d_act = dg(self.d_outer, wd(c), NT)
            d_inner = d_act * slope_s[c][self.at, :].astype(f32)
            gub[:, c * width : (c + 1) * width] += col_sum(d_inner)
            low = d_inner.astype(bf16)
            slope_s[c][self.at, :] = low
            self.d_hidden = self.d_hidden + dg(low, wu(c), NT)

        def leave(self):
            gvec[3:4, :] += col_sum(self.d_hidden * self.normed)
            gvec[4:5, :] += col_sum(self.d_hidden)
            d_res1 = norm_backward(self.d_hidden, self.normed, self.inverse, ga)
            res_o[0, self.at, :] = d_res1
            gvec[2:3, :] += col_sum(d_res1)
            d_branch = d_res1.astype(bf16)
            branch_s[self.at, :] = d_branch
            d_att = dg(d_branch, wo(), NT).astype(bf16)
            for p in range(width // 128):
                datt_o[0, p, self.at, :] = d_att[:, 128 * p : 128 * p + 128]

    half = rows // 2
    a, b = Part(slice(0, half)), Part(slice(half, rows))
    a.enter()
    b.enter()
    for c in range(cols):
        a.forward(c)
    b.forward(0)
    a.turn()
    for c in range(1, cols):
        b.forward(c)
    a.backward(0)
    b.turn()
    for c in range(1, cols):
        a.backward(c)
    b.backward(0)
    a.leave()
    for c in range(1, cols):
        b.backward(c)
    for c in range(cols):
        at = slice(c * width, (c + 1) * width)
        gwd[at, :] += dg(act_s[c][...], outer_s[...], TN)
        gwu[:, at] += dg(low_s[...], slope_s[c][...], TN)
        if c == 0:
            b.leave()
    gwo[...] += dg(att_ref[0], branch_s[...], NN)

    @pl.when(i == steps - 1)
    def _():
        part_o[:, 0:r, :] = gwo[...].astype(bf16).reshape(count, r, width)
        for c in range(cols):
            part_o[:, r + c * r : r + c * r + r, :] = (
                gwu[:, c * width : (c + 1) * width].astype(bf16).reshape(count, r, width)
            )
        part_o[:, r + cols * r :, :] = gwd[...].astype(bf16).reshape(count, fr, width)


def feed_call(x, att, dy, g2, vec, ub, r, fr):
    seqs, length, width = x.shape
    ff = ub.shape[1]
    tile = min(512, length)
    tiles = length // tile
    shape = jax.ShapeDtypeStruct
    rows = pl.BlockSpec((1, tile, width), lambda i: (i // tiles, i % tiles, 0))

    def full(a):
        return pl.BlockSpec(a.shape, lambda i: (0,) * len(a.shape))

    outs = (
        shape((seqs, length, width), bf16),
        shape((seqs, length, width), f32),
        shape((seqs, width // 128, length, 128), bf16),
        shape(g2.shape, bf16),
        shape((8, width), f32),
        shape((1, ff), f32),
    )
    return pl.pallas_call(
        functools.partial(feed_kernel, r, fr, seqs * tiles),
        grid=(seqs * tiles,),
        out_shape=outs,
        in_specs=[
            rows,
            pl.BlockSpec((1, width, tile), lambda i: (i // tiles, 0, i % tiles)),
            rows,
            full(g2),
            full(vec),
            full(ub),
        ],
        out_specs=[
            rows,
            rows,
            pl.BlockSpec((1, width // 128, tile, 128), lambda i: (i // tiles, 0, i % tiles, 0)),
        ]
        + [full(a) for a in outs[3:]],
        scratch_shapes=[
            [VMEM((tile, width), bf16)] * (ff // width),
            [VMEM((tile, width), bf16)] * (ff // width),
            VMEM((tile, width), bf16),
            VMEM((tile, width), bf16),
            VMEM((tile, width), bf16),
            VMEM((width, width), f32),
            VMEM((width, ff), f32),
            VMEM((ff, width), f32),
        ],
        compiler_params=pltpu.CompilerParams(vmem_limit_bytes=60 * 2**20),
        name="feed",
    )(x, att, dy, g2, vec, ub)


def pull_kernel(
    count, sub, mem_rows, r, fr,
    x_any, mem_ref, q_any, k_any, v_any, att_any, inv_any, prob_any, da_any, res_any, g1_any, part1,
    gvec_ref, gub_ref,
    dx_any, sums_o, small_o,
    x_ref, q_ref, k_ref, v_ref, att_ref, inv_ref, da_ref, res_ref, g1, dx_o,
    prob_s, vsel, dot_s, d_a, d_b, pt_s, dt_s, dq_s, dk_s, dv_s, dqt, dkt, dvt, dkm, dvm, turned, terms,
    vec_s, part2, small_s, *rest,
):
    cube = Cube(count, sub)
    nb = cube.nb
    ways = [list(reversed(route)) for route in routes(nb)]
    steps = len(ways[0])
    brief = short(ways[0])
    sizes = [steps] * 7 + [len(brief)] * 2
    ends = [sum(sizes[: k + 1]) for k in range(len(sizes))]
    bufs = [rest[end - size : end] for size, end in zip(sizes, ends, strict=True)]
    send, recv, load_sem, late_sem, out_sem, prob_sem = rest[ends[-1] :]
    seqs, length, width = x_ref.shape
    keys = v_ref.shape[2]
    ff = gub_ref.shape[1]
    cols = ff // width
    half = width // 2
    halves = (slice(0, half), slice(half, width))
    pairs = HEADS // 2
    quarter = width // 4

    def scatter(n, source, lo, hi, way):
        return Scatter(cube, source, slice(lo, hi), way, bufs[n], send.at[n], recv.at[n])

    feeds = [scatter(k, part1, k * quarter, (k + 1) * quarter, ways[k % 2]) for k in range(4)]
    heads = [
        scatter(4 + p, part2, 128 * p, 128 * p + 128, ways[p % 2] if p < pairs - 1 else brief)
        for p in range(pairs)
    ]
    smalls = scatter(8, small_s, 0, 128, brief)

    def start(group, step):
        for part in group:
            for copy in part.copies(step):
                copy.start()

    def finish(group, step):
        for part in group:
            for copy in part.copies(step):
                copy.wait()
        for part in group:
            if step < part.steps - 1:
                part.add(step)

    def loads(j):
        p, s = j // seqs, j % seqs
        own = ((q_any, q_ref), (k_any, k_ref), (v_any, v_ref), (da_any, da_ref))
        out = [
            pltpu.make_async_copy(a.at[s, p], b.at[s, p], load_sem.at[j, n])
            for n, (a, b) in enumerate(own)
        ]
        both = pl.ds(2 * p, 2)
        return out + [
            pltpu.make_async_copy(a.at[s, both], b.at[s, both], load_sem.at[j, 4 + n])
            for n, (a, b) in enumerate(((att_any, att_ref), (inv_any, inv_ref)))
        ]

    def prob_load(j):
        p, s = j // seqs, j % seqs
        return pltpu.make_async_copy(
            prob_any.at[s, pl.ds(2 * p, 2)], prob_s.at[j % 2], prob_sem.at[j % 2]
        )

    late = [
        pltpu.make_async_copy(a, b, late_sem.at[n])
        for n, (a, b) in enumerate(((g1_any, g1), (res_any, res_ref)))
    ]

    def x_load(s):
        return pltpu.make_async_copy(x_any.at[s], x_ref.at[s], late_sem.at[2 + s])

    prob_load(0).start()

    @pl.loop(0, seqs * pairs)
    def _(j):
        for load in loads(j):
            load.start()

    for load in [x_load(s) for s in range(seqs)] + late:
        load.start()
    cube.barrier(ways + [brief])
    start(feeds, 0)

    lane = lax.broadcasted_iota(jnp.int32, (1, 128), 1)
    block = d_a.shape[1]
    per_head = length // block
    temp = (d_a, d_b)

    def pair(j):
        p, s = j // seqs, j % seqs
        at = pl.ds(pl.multiple_of(128 * p, 128), 128)
        slot = j % 2
        vp = v_ref[s, p]
        dat = da_ref[s, p].T
        for e in range(2):
            o = 64 * (1 - e)
            mine = (lane < 64) if e == 0 else (lane >= 64)
            vsel[e] = jnp.where(
                mine, vp, jnp.where((lane >= o) & (lane < o + 2), 1.0, 0.0).astype(bf16)
            )
            dt = dat[64 * e : 64 * e + 64, :].astype(f32) * inv_ref[s, 2 * p + e]
            dot_s[e, 64 * e : 64 * e + 64, :] = dt.astype(bf16)
            delta = col_sum(dt * att_ref[s, 2 * p + e].astype(f32))
            hi = delta.astype(bf16).astype(f32)
            row = lax.broadcasted_iota(jnp.int32, (64, length), 0)
            dot_s[e, o : o + 64, :] = jnp.where(
                row == 0, -hi, jnp.where(row == 1, hi - delta, 0.0)
            ).astype(bf16)

        def grads(b):
            e, c = b // per_head, b % per_head
            cut = slice(c * block, (c + 1) * block)
            grad = dg(vsel[e], dot_s[e, :, cut], NN)
            temp[b % 2][...] = (prob_s[slot, e, c].astype(f32) * grad).astype(bf16)
            pt_s[b % 2] = prob_s[slot, e, c, 0:length, :].T
            dt_s[b % 2] = temp[b % 2][0:length, :].T

        def pulls(b):
            e, c = b // per_head, b % per_head
            cut = slice(c * block, (c + 1) * block)
            own = slice(64 * e, 64 * e + 64)
            grad = temp[b % 2]
            dqt[own, cut] = dg(k_ref[s, p, own, :], grad[...], NN)
            dots, queries = dot_s[e, own, cut], q_ref[s, p, own, cut]
            prob = prob_s.at[slot, e, c]
            news = (
                (dvt, dg(dots, pt_s[b % 2], NN)),
                (dkt, dg(queries, dt_s[b % 2], NN)),
                (dvm, dg(dots, prob[length:keys, :], NT)),
                (dkm, dg(queries, grad[length:keys, :], NT)),
            )
            for ref, new in news:
                to = slice(0, new.shape[1])
                if c == 0:
                    ref[own, to] = new
                else:
                    ref[own, to] += new

        grads(0)
        for b in range(2 * per_head):
            if b + 1 < 2 * per_head:
                grads(b + 1)
            pulls(b)
        units = ((dq_s, dqt, None, 1.0), (dk_s, dkt, dkm, LN2), (dv_s, dvt, dvm, 1.0))
        news = []
        for n, (ref, tops, mems, unit) in enumerate(units):
            low = (tops[...] * unit).astype(bf16)
            turned[128 * n : 128 * n + 128, :] = low
            ref[s, 0:length, at] = low.T
            if mems is not None:
                low = (mems[...] * unit).astype(bf16)
                ref[s, length:keys, at] = low.T
                news.append(dg(low, mem_ref[...], NN))
        new = dg(turned[...], x_ref[s], NN)
        add = jnp.where(s == 0, 0.0, 1.0)
        terms[0:128, :] = terms[0:128, :] * add + new[0:128, :] * HEAD_DIM**-0.5
        for n in range(2):
            own = slice(128 * (n + 1), 128 * (n + 2))
            terms[own, :] = terms[own, :] * add + (new[own, :] + news[n])
        vec_s[0:1, at] = vec_s[0:1, at] * add + col_sum(dq_s[s, :, at].astype(f32)) * HEAD_DIM**-0.5
        vec_s[1:2, at] = vec_s[1:2, at] * add + col_sum(dv_s[s, :, at].astype(f32))

        @pl.when(s == seqs - 1)
        def _():
            for n in range(3):
                low = terms[128 * n : 128 * n + 128, :].astype(bf16).T
                part2[(slice(None),) * nb + (slice(n * r, n * r + r), at)] = low.reshape(
                    (2,) * nb + (r, 128)
                )

    terms[...] = jnp.zeros_like(terms)
    vec_s[...] = jnp.zeros_like(vec_s)

    def weight(j):
        return g1[(slice(None),) * nb + (slice(j * r, j * r + r), slice(None))].reshape(width, width)

    scale = HEAD_DIM**-0.5
    tail = slice(length, keys)

    turns = seqs * pairs

    @pl.loop(0, turns)
    def _(j):
        @pl.when(j + 1 < turns)
        def _():
            prob_load(j + 1).start()

        for load in loads(j) + [prob_load(j)]:
            load.wait()

        for s in range(seqs):

            @pl.when(j == s)
            def _():
                x_load(s).wait()

        plan = ((1, feeds, 0), (3, feeds[:2], 1), (4, feeds[2:], 1), (5, feeds[:2], 2))
        plan += ((6, feeds[2:], 2), (2, heads[:1], -1), (4, heads[1:2], -1), (6, heads[2:3], -1))
        plan += ((5, heads[:2], 0), (6, heads[:2], 1), (7, heads[:2], 2), (7, heads[2:3], 0))
        for slot, group, step in plan:

            @pl.when(j == (slot * turns) // 8)
            def _():
                if step >= 0:
                    finish(group, step)
                start(group, step + 1)

        pair(j)

    start(heads[3:], 0)
    for load in late:
        load.wait()
    tails = [jnp.concatenate([ref[s, tail, :] for s in range(seqs)], 0) for ref in (dk_s, dv_s)]
    both = dg(tails[0], weight(1), NT) + dg(tails[1], weight(2), NT)
    gmem = sum(both[s * (keys - length) : (s + 1) * (keys - length), :] for s in range(seqs))
    vec_row = lax.broadcasted_iota(jnp.int32, (8, width), 0)
    vecs = jnp.where(vec_row < 2, vec_s[...], gvec_ref[...])
    flat = jnp.concatenate(
        [
            gmem[0:16, :],
            jnp.concatenate([gmem[16:20, :], vecs[0:4, :]], 0),
            jnp.concatenate([vecs[4:8, :], jnp.zeros((4, width), f32)], 0),
            jnp.zeros((96, width), f32),
        ],
        0,
    )
    small_s[...] = flat.T.reshape((2,) * nb + (16, 128))
    for i in range(count):
        at = tuple((i >> b) & 1 for b in cube.msb_first)
        off = (i * fr) % 128
        up = jnp.broadcast_to(gub_ref[:, i * fr - off : i * fr - off + 128], (8, 128))
        up = pltpu.roll(up, (64 - off) % 128, 1)
        small_s[at + (slice(0, 1), slice(64, 64 + fr))] = up[0:1, 64 : 64 + fr]
    start([smalls], 0)
    tile = 512
    tiles = length // tile

    def inputs(i):
        s, rows = i // tiles, pl.ds((i % tiles) * tile, tile)
        dx = res_ref[s, rows, :] + dg(dq_s[s, rows, :], weight(0), NT) * scale
        dx = dx + dg(dk_s[s, rows, :], weight(1), NT) + dg(dv_s[s, rows, :], weight(2), NT)
        dx_o[s, rows, :] = dx.astype(bf16)
        out = pltpu.make_async_copy(dx_o.at[s, rows], dx_any.at[s, rows], out_sem.at[i])
        out.start()
        return out

    def total(part, lo, hi):
        sums_o[lo:hi, part.lanes] = part.total(part.steps - 1)

    todo = list(range(seqs * tiles))
    outs = []
    group = heads[3:] + [smalls]
    for step in range(len(brief)):
        if todo:
            outs.append(inputs(todo.pop(0)))
        finish(group, step)
        if step + 1 < len(brief):
            start(group, step + 1)
        if step == 0:
            finish(heads[2:3], 1)
            start(heads[2:3], 2)
            finish(feeds, steps - 1)
            for part in feeds:
                total(part, 3 * r, sums_o.shape[0])
        if step == 1:
            finish(heads[2:3], 2)
            start(heads[2:3], 3)
            finish(heads[:2], steps - 1)
    for i in todo:
        outs.append(inputs(i))
    finish(heads[2:3], 3)
    for part in heads:
        total(part, 0, 3 * r)
    small_o[...] = smalls.total(smalls.steps - 1)
    for out in outs:
        out.wait()


def pull_call(count, sub, mem_rows, r, fr, x, mem, q, k, v, att, inv, prob, da, res, g1, part1, gvec, gub):
    seqs, length, width = x.shape
    keys = v.shape[2]
    rows2 = part1.shape[-2]
    nb = count.bit_length() - 1
    cube = (2,) * nb
    way = list(reversed(routes(nb)[0]))
    links = (len(way), most(way))
    block = prob.shape[4]
    quarter = width // 4
    turns = seqs * (HEADS // 2)
    shape = jax.ShapeDtypeStruct
    vm = pl.BlockSpec(memory_space=VMEM)
    hbm = pl.BlockSpec(memory_space=pl.ANY)
    dma = pltpu.SemaphoreType.DMA
    return pl.pallas_call(
        functools.partial(pull_kernel, count, sub, mem_rows, r, fr),
        out_shape=(
            shape((seqs, length, width), bf16),
            shape((3 * r + rows2, width), f32),
            shape((16, 128), f32),
        ),
        in_specs=[hbm, vm] + [hbm] * 9 + [vm] * 3,
        out_specs=[hbm, vm, vm],
        scratch_shapes=[VMEM(a.shape, a.dtype) for a in (x, q, k, v, att, inv, da, res, g1, x)]
        + [
            VMEM((2, 2) + prob.shape[2:], bf16),
            VMEM((2, keys, 128), bf16),
            VMEM((2, 128, length), bf16),
            VMEM((keys, block), bf16),
            VMEM((keys, block), bf16),
            VMEM((2, block, length), bf16),
            VMEM((2, block, length), bf16),
            VMEM((seqs, length, width), bf16),
            VMEM((seqs, keys, width), bf16),
            VMEM((seqs, keys, width), bf16),
            VMEM((128, length), f32),
            VMEM((128, length), f32),
            VMEM((128, length), f32),
            VMEM((128, KEY_PAD), f32),
            VMEM((128, KEY_PAD), f32),
            VMEM((384, length), bf16),
            VMEM((384, width), f32),
            VMEM((8, width), f32),
            VMEM(cube + (3 * r, width), bf16),
            VMEM(cube + (16, 128), f32),
        ]
        + scatter_bufs(nb, way, (rows2, quarter), bf16) * 4
        + scatter_bufs(nb, way, (3 * r, 128), bf16) * 3
        + scatter_bufs(nb, short(way), (3 * r, 128), bf16)
        + scatter_bufs(nb, short(way), (16, 128), f32)
        + [dma((9,) + links)] * 2
        + [dma((turns, 6)), dma((2 + seqs,)), dma((seqs * (length // 512),)), dma((2,))],
        compiler_params=pltpu.CompilerParams(
            collective_id=1, has_side_effects=True, vmem_limit_bytes=62 * 2**20
        ),
        name="pull",
    )(x, mem, q, k, v, att, inv, prob, da, res, g1, part1, gvec, gub)


def results_kernel(r, fr, mem_rows, dx_ref, sums, small, dx_o, *outs):
    outs, sem = outs[:-1], outs[-1]
    move = pltpu.make_async_copy(dx_ref, dx_o, sem)
    move.start()
    gq, gk, gv, go, gu, gd, gm, gb = outs[:8]
    vecs = outs[8:]
    width = gq.shape[1]
    cols = gu.shape[1] // width
    for n, ref in enumerate((gq, gk, gv, go)):
        ref[...] = sums[n * r : (n + 1) * r, :]
    for c in range(cols):
        gu[:, c * width : (c + 1) * width] = sums[(4 + c) * r : (5 + c) * r, :]
    gd[...] = sums[(4 + cols) * r :, :]
    value = small[...]
    gm[...] = value[0:r, 0:mem_rows]
    turned = jnp.concatenate([value, jnp.zeros((112, 128), f32)], 0).T
    for n, ref in enumerate(vecs):
        ref[...] = turned[VEC + n : VEC + n + 1, 0:r]
    gb[...] = value[0:1, 64 : 64 + fr]
    move.wait()


def results_call(r, fr, mem_rows, ff, dx, sums, small):
    width = sums.shape[1]
    shape = jax.ShapeDtypeStruct
    vm = pl.BlockSpec(memory_space=VMEM)
    hbm = pl.BlockSpec(memory_space=pl.ANY)
    mats = [(r, width)] * 4 + [(r, ff), (fr, width), (r, mem_rows), (1, fr)] + [(1, r)] * 8
    return pl.pallas_call(
        functools.partial(results_kernel, r, fr, mem_rows),
        out_shape=(shape(dx.shape, dx.dtype),) + tuple(shape(m, f32) for m in mats),
        in_specs=[vm, vm, vm],
        out_specs=[hbm] + [vm] * len(mats),
        scratch_shapes=[pltpu.SemaphoreType.DMA],
        name="results",
    )(dx, sums, small)


DIMS = (1, 0, 0, 0, 0, 0, 0, 0, 0, 0, 0, 0, 0, 0, 0, 0)


def on_device(devices, inputs, lengths, *rest):
    params, cotangent = rest[:-1], rest[-1]
    width = inputs.shape[2]
    count = min(devices, width // 16)
    sub = devices // count
    sets = [list(range(g * sub, (g + 1) * sub)) for g in range(count)]
    if sub > 1:
        params = tuple(
            lax.all_gather(a, "dp", axis=d, tiled=True, axis_index_groups=sets)
            for a, d in zip(params, DIMS, strict=True)
        )
    (memory, wq, bq, wk, wv, bv, wo, bo, ga, sa, wu, bu, wd, bd, gb, sb) = params
    r, fr = wq.shape[0], wd.shape[0]
    mem_rows = memory.shape[0]

    vecs = [a.reshape(1, r) for a in (bq, bv, bo, ga, sa, bd, gb, sb)]
    q, k, v, att, inv, g1, prob, g2, vec, ub, mem = attend_call(
        count, sub, lengths, inputs, wq, wk, wv, wo, wu, wd, memory.T, bu.reshape(1, fr), vecs, mem_rows
    )
    seqs, length = inputs.shape[:2]
    layer_out, res, datt, part1, gvec, gub = feed_call(
        inputs,
        att.reshape(seqs, width, length),
        cotangent,
        g2.reshape((count,) + g2.shape[-2:]),
        vec,
        ub,
        r,
        fr,
    )
    dx, sums, tiny = pull_call(
        count, sub, mem_rows, r, fr, inputs, mem, q, k, v, att, inv, prob, datt, res, g1,
        part1.reshape(g2.shape), gvec, gub,
    )
    dx, gwq, gwk, gwv, gwo, gwu, gwd, gmem, gbu, *vecs = results_call(
        r, fr, mem_rows, wu.shape[1], dx, sums, tiny
    )
    gmem = gmem.T
    gbu = gbu.reshape(fr)
    gbq, gbv, gbo, gga, gsa, gbd, ggb, gsb = [a.reshape(r) for a in vecs]
    grads = (gmem, gwq, gbq, gwk, gwv, gbv, gwo, gbo, gga, gsa, gwu, gbu, gwd, gbd, ggb, gsb)
    if sub > 1:
        grads = tuple(
            lax.psum_scatter(a, "dp", scatter_dimension=d, tiled=True, axis_index_groups=sets)
            for a, d in zip(grads, DIMS, strict=True)
        )
    return (layer_out, dx) + grads


def solution(mesh):
    rows, row, mem = P("dp", None), P("dp"), P(None, "dp")
    full = P("dp", None, None)
    params = (mem, rows, row, rows, rows, row, rows, row, row, row, rows, row, rows, row, row, row)
    return jax.shard_map(
        functools.partial(on_device, mesh.shape["dp"]),
        mesh=mesh,
        in_specs=(full, P("dp")) + params + (full,),
        out_specs=(full, full) + params,
        check_vma=False,
    )
```

```python
import functools

import jax
import jax.numpy as jnp
from jax import lax
from jax.experimental import pallas as pl
from jax.experimental.pallas import tpu as pltpu
from jax.sharding import PartitionSpec as P

HEADS = 8
HEAD_DIM = 64
EPSILON = 1e-05
LOG2E = 1.4426950408889634
LN2 = 0.6931471805599453
GELU_A = 0.7978845608028654
GELU_B = GELU_A * 0.044715
HIDE = -1e30
VEC = 20
KEY_PAD = 32

f32 = jnp.float32
bf16 = jnp.bfloat16
VMEM = pltpu.VMEM
MESH = pl.DeviceIdType.MESH
NN = (((1,), (0,)), ((), ()))
NT = (((1,), (1,)), ((), ()))
TN = (((0,), (0,)), ((), ()))


def dg(left, right, dims):
    return lax.dot_general(left, right, dims, preferred_element_type=f32)


def col_sum(value):
    return jnp.sum(value, 0, keepdims=True)


class Cube:
    def __init__(self, count, sub):
        self.count, self.sub = count, sub
        self.nb = count.bit_length() - 1
        device = lax.axis_index("dp")
        self.device = device
        me = device // sub
        self.bits = [(me // (2**b)) % 2 for b in range(self.nb)]
        self.msb_first = tuple(range(self.nb - 1, -1, -1))

    def partner(self, flips):
        to = self.device
        for b in flips:
            to = to + (1 - 2 * self.bits[b]) * (2**b * self.sub)
        return (to,)

    def barrier(self, routes):
        groups = sorted({flips for route in routes for group in route for flips in masks(group)})
        sem = pltpu.get_barrier_semaphore()
        for flips in groups:
            pl.semaphore_signal(sem, inc=1, device_id=self.partner(flips), device_id_type=MESH)
        pl.semaphore_wait(sem, len(groups))

    def own(self):
        return tuple(self.bits[b] for b in self.msb_first)


def masks(group):
    return [
        tuple(b for k, b in enumerate(group) if (m >> k) & 1) for m in range(1, 2 ** len(group))
    ]


def routes(nb):
    if nb >= 4:
        far = list(range(nb - 1, 2, -1))
        groups = [tuple(far[k : k + 2]) for k in range(0, len(far), 2)]
        return (groups + [(1,), (2,), (0,)], groups + [(2,), (1,), (0,)])
    return ([(b,) for b in range(nb - 1, -1, -1)],) * 2


def short(route):
    if len(route) != 4:
        return route
    return [route[0], route[1] + route[2], route[3]]


def most(route):
    return max(2 ** len(group) - 1 for group in route)


def gather_copies(cube, ref, route, step, rows, lanes, send, recv):
    done = {b for group in route[:step] for b in group}
    idx = tuple(slice(None) if c in done else cube.bits[c] for c in cube.msb_first)
    view = ref.at[idx + (rows, lanes)]
    return [
        pltpu.make_async_remote_copy(
            src_ref=view,
            dst_ref=view,
            send_sem=send.at[step, k],
            recv_sem=recv.at[step, k],
            device_id=cube.partner(flips),
            device_id_type=MESH,
        )
        for k, flips in enumerate(masks(route[step]))
    ]


class Scatter:
    def __init__(self, cube, source, lanes, route, bufs, send, recv):
        self.cube, self.source, self.lanes, self.route = cube, source, lanes, route
        self.bufs, self.send, self.recv = bufs, send, recv
        self.steps = len(route)

    def _piece(self, step, flips, rest=None):
        cube = self.cube
        gone = {b for group in self.route[:step] for b in group}
        left = [c for c in cube.msb_first if c not in gone]
        rest = iter(rest) if rest is not None else None
        idx = ()
        for c in left:
            if c in self.route[step]:
                idx += (1 - cube.bits[c] if c in flips else cube.bits[c],)
            else:
                idx += (slice(None) if rest is None else next(rest),)
        if step == 0:
            return self.source, idx + (slice(None), self.lanes)
        return self.bufs[step - 1].at[0], idx

    def copies(self, step):
        out = []
        for k, flips in enumerate(masks(self.route[step])):
            ref, idx = self._piece(step, flips)
            out.append(
                pltpu.make_async_remote_copy(
                    src_ref=ref.at[idx],
                    dst_ref=self.bufs[step].at[k],
                    send_sem=self.send.at[step, k],
                    recv_sem=self.recv.at[step, k],
                    device_id=self.cube.partner(flips),
                    device_id_type=MESH,
                )
            )
        return out

    def total(self, step, rest=None):
        ref, idx = self._piece(step, (), rest)
        value = ref[idx].astype(f32)
        for k in range(2 ** len(self.route[step]) - 1):
            value = value + self.bufs[step][(k,) + tuple(rest or ())].astype(f32)
        return value

    def add(self, step):
        free = self.cube.nb - sum(len(group) for group in self.route[: step + 1])
        into = self.bufs[step]
        for flat in range(2**free):
            rest = tuple((flat >> (free - 1 - k)) & 1 for k in range(free))
            into[(0,) + rest] = self.total(step, rest).astype(into.dtype)


def scatter_bufs(nb, route, tail, dtype):
    bufs, left = [], nb
    for group in route:
        left -= len(group)
        bufs.append(VMEM((2 ** len(group) - 1,) + (2,) * left + tail, dtype))
    return bufs


def attend_part(
    cube, mem_rows,
    len_ref, x_any, wq_ref, wk_ref, wv_ref, wo_ref, wu_ref, wd_ref, memt_ref, ub_ref, vec_refs,
    x_ref, q_o, k_o, v_o, att_o, inv_o, g1, g2, gs, vec_o, ub_o, mem_o, prob_any,
    qt_o, ksel, vt_s, score_a, score_b, prob_s, top_a, top_b, flat_s, wide_s,
    local, x_sem, prob_sem, send1, recv1, send2, recv2, send3, recv3,
):
    nb, count = cube.nb, cube.count
    seqs, length, width = x_ref.shape
    keys = v_o.shape[2]
    mem_pad = keys - length
    r = wq_ref.shape[0]
    ff = wu_ref.shape[1]
    cols = ff // width
    fr = wd_ref.shape[0]
    own = cube.own()
    ways = routes(nb)
    steps = len(ways[0])
    half = width // 2
    halves = (slice(0, half), slice(half, width))
    whole = (slice(None), slice(None))
    x_load = pltpu.make_async_copy(x_any, x_ref, x_sem)
    x_load.start()
    for j, ref in enumerate((wq_ref, wk_ref, wv_ref)):
        g1[own + (slice(j * r, j * r + r), slice(None))] = ref[...]
    wide_s[...] = jnp.zeros_like(wide_s)
    flat_s[...] = jnp.zeros_like(flat_s)
    for j, ref in enumerate(vec_refs):
        wide_s[VEC + j : VEC + j + 1, 0:r] = ref[...].astype(f32)
    flat_s[0:r, 0:mem_rows] = memt_ref[...].astype(f32)
    flat_s[0:1, 64 : 64 + fr] = ub_ref[...].astype(f32)
    gs[own + whole] = (flat_s[...] + wide_s[...].T[0:16, :]).astype(bf16)
    parts = [(wo_ref, slice(0, r))]
    parts += [
        (wu_ref.at[:, c * width : (c + 1) * width], slice(r + c * r, r + c * r + r))
        for c in range(cols)
    ]
    parts += [(wd_ref, slice(r + cols * r, r + cols * r + fr))]
    moves = [
        pltpu.make_async_copy(ref, g2.at[own + (rows, slice(None))], local.at[j])
        for j, (ref, rows) in enumerate(parts)
    ]
    for move in moves:
        move.start()
    cube.barrier([*ways, short(list(reversed(ways[0])))])

    every_row = slice(None)

    def first(j, step):
        rows = slice(j * r, j * r + r)
        copies = []
        for k in range(2):
            links = (send1.at[2 * j + k], recv1.at[2 * j + k])
            copies += gather_copies(cube, g1, ways[k], step, rows, halves[k], *links)
        return copies

    def tiny(step):
        return gather_copies(cube, gs, ways[0], step, every_row, slice(None), send3, recv3)

    chunks = 4
    chunk = width // chunks

    def second(c, step):
        lanes = slice(c * chunk, (c + 1) * chunk)
        return gather_copies(
            cube, g2, ways[c % 2], step, every_row, lanes, send2.at[c], recv2.at[c]
        )

    def advance(c, step):
        if step > 0:
            for copy in second(c, step - 1):
                copy.wait()
        if step < steps:
            for copy in second(c, step):
                copy.start()

    sets = [functools.partial(first, 1), tiny, functools.partial(first, 2), functools.partial(first, 0)]
    for copies in sets:
        for copy in copies(0):
            copy.start()
    for move in moves:
        move.wait()
    for step in range(1, steps):
        for copies in sets:
            for copy in copies(step - 1):
                copy.wait()
            for copy in copies(step):
                copy.start()
        if step == 1:
            for c in range(chunks):
                advance(c, 0)

    def arrived(n):
        for copy in sets[n](steps - 1):
            copy.wait()

    arrived(0)
    arrived(1)
    x_load.wait()

    lane = lax.broadcasted_iota(jnp.int32, (1, 128), 1)
    every = gs[...].astype(f32).reshape(width, 128).T
    mem_o[0:16, :] = every[0:16, :].astype(bf16)
    rest_row = lax.broadcasted_iota(jnp.int32, (16, width), 0)
    mem_o[16:32, :] = jnp.where(rest_row < mem_rows - 16, every[16:32, :], 0.0).astype(bf16)
    vec_o[...] = every[VEC : VEC + 8, :]
    ups = [jnp.zeros((16, 128), f32) for _ in range(ff // 128)]
    for i in range(count):
        at = tuple((i >> b) & 1 for b in cube.msb_first)
        to = (i * fr) % 128
        here = (lane >= to) & (lane < to + fr)
        rolled = pltpu.roll(gs[at + whole].astype(f32), (to - 64) % 128, 1)
        ups[i * fr // 128] = ups[i * fr // 128] + jnp.where(here, rolled, 0.0)
    for g in range(ff // 128):
        ub_o[:, 128 * g : 128 * g + 128] = ups[g][0:1, :]

    def weight(j):
        return g1[(slice(None),) * nb + (slice(j * r, j * r + r), slice(None))].reshape(width, width)

    bq = vec_o[0:1, :]
    bv = vec_o[1:2, :]

    def put_keys(s, rows, kk, bias):
        kb = kk.astype(bf16)
        kt = kb.T
        for p in range(HEADS // 2):
            k_o[s, p, :, rows] = kt[128 * p : 128 * p + 128, :]
        for h in range(HEADS):
            p, o = h // 2, 64 * (1 - h % 2)
            pattern = jnp.where(lane == o, bias, 0.0).astype(bf16)
            mine = (lane < 64) if h % 2 == 0 else (lane >= 64)
            ksel[s, h, rows, :] = jnp.where(mine, kb[:, 128 * p : 128 * p + 128], pattern)

    def put_values(s, rows, vv):
        vb = vv.astype(bf16)
        vt = vb.T
        for p in range(HEADS // 2):
            v_o[s, p, rows, :] = vb[:, 128 * p : 128 * p + 128]
        for h in range(HEADS):
            vt_s[s, h, 0:64, rows] = vt[64 * h : 64 * h + 64, :]

    top_row = lax.broadcasted_iota(jnp.int32, (16, keys), 0)
    ones = jnp.where(top_row == 0, 1.0, 0.0).astype(bf16)
    for s in range(seqs):
        for h in range(HEADS):
            vt_s[s, h, 64:80, :] = ones
    mem = mem_o[...]
    mem_keys = dg(mem, weight(1), NN)
    mem_row = lax.broadcasted_iota(jnp.int32, (mem_pad, 1), 0)
    mem_bias = jnp.where(mem_row < mem_rows, 0.0, HIDE)
    for s in range(seqs):
        put_keys(s, slice(length, keys), mem_keys, mem_bias)
    tile = 512
    tiles = length // tile
    aux = jnp.where(lax.broadcasted_iota(jnp.int32, (64, tile), 0) == 0, 1.0, 0.0).astype(bf16)

    def place_rows(i):
        start = pl.multiple_of((i % tiles) * tile, tile)
        return i // tiles, start, pl.ds(start, tile)

    @pl.loop(0, seqs * tiles)
    def _(i):
        s, start, rows = place_rows(i)
        row = lax.broadcasted_iota(jnp.int32, (tile, 1), 0) + start
        bias = jnp.where(row < len_ref[s], 0.0, HIDE)
        put_keys(s, rows, dg(x_ref[s, rows, :], weight(1), NN), bias)

    arrived(2)
    mem_values = dg(mem, weight(2), NN) + bv
    for s in range(seqs):
        put_values(s, slice(length, keys), mem_values)

    @pl.loop(0, seqs * tiles)
    def _(i):
        s, start, rows = place_rows(i)
        put_values(s, rows, dg(x_ref[s, rows, :], weight(2), NN) + bv)

    arrived(3)
    advance(0, 1)
    advance(1, 1)

    @pl.loop(0, seqs * tiles)
    def _(i):
        s, start, rows = place_rows(i)
        qb = ((dg(x_ref[s, rows, :], weight(0), NN) + bq) * (LOG2E * HEAD_DIM**-0.5)).astype(bf16)
        qt = qb.T
        for p in range(HEADS // 2):
            q_o[s, p, :, rows] = qt[128 * p : 128 * p + 128, :]
        for h in range(HEADS):
            e = h % 2
            qt_o[s, h, 64 * e : 64 * e + 64, rows] = qt[64 * h : 64 * h + 64, :]
            qt_o[s, h, 64 * (1 - e) : 64 * (1 - e) + 64, rows] = aux

    block = score_a.shape[1]
    per_head = length // block
    blocks = seqs * HEADS * per_head

    def place(i):
        s = i // (HEADS * per_head)
        h = (i // per_head) % HEADS
        return s, h, pl.ds(pl.multiple_of((i % per_head) * block, block), block)

    cuts = [slice(c, c + 256) for c in range(0, length - 256, 256)] + [slice(length - 256, keys)]

    def turn(i, now, then):
        if i is not None:
            score, top, slot = now
            s, h, at = place(i)
            peak = top[...]
            mixed = 0.0
        if then is not None:
            next_i, next_score, next_top = then
            next_s, next_h, next_at = place(next_i)
            column = qt_o[next_s, next_h, :, next_at]
            high = None
        for cut in cuts:
            if then is not None:
                value = dg(ksel[next_s, next_h, cut, :], column, NN)
                next_score[cut, :] = value
                part = jnp.max(value.reshape(-1, 8, block), 0)
                high = part if high is None else jnp.maximum(high, part)
            if i is not None:
                weights = jnp.exp2(score[cut, :] - peak).astype(bf16)
                prob_s[slot + (cut, slice(None))] = weights
                mixed = mixed + dg(vt_s[s, h, :, cut], weights, NN)
        if then is not None:
            next_top[...] = jnp.max(high, 0, keepdims=True)
        if i is not None:
            prob_out(i, slot).start()
            inverse = 1.0 / mixed[64:65, :]
            att_o[s, h, :, at] = (mixed[0:64, :] * inverse).astype(bf16)
            inv_o[s, h, :, at] = inverse

    def prob_out(i, slot):
        s, h, _ = place(i)
        return pltpu.make_async_copy(
            prob_s.at[slot], prob_any.at[s, h, i % per_head], prob_sem.at[slot]
        )

    turn(None, None, (0, score_a, top_a))
    turns = blocks // 2
    plan = ((2, 0, 2), (2, 1, 2), (3, 2, 1), (3, 3, 1), (9, 0, 3), (9, 1, 3), (9, 2, 2), (9, 3, 2))
    plan += ((15, 2, 3), (15, 3, 3))

    @pl.loop(0, turns)
    def _(j):
        for slot, c, step in plan:

            @pl.when(j == (slot * turns) // 16)
            def _():
                advance(c, step)

        odd = j % 2

        @pl.when(j > 1)
        def _():
            for k in range(2):
                prob_out(2 * j - 4 + k, (odd, k)).wait()

        turn(2 * j, (score_a, top_a, (odd, 0)), (2 * j + 1, score_b, top_b))
        then = jnp.minimum(2 * j + 2, blocks - 1)
        turn(2 * j + 1, (score_b, top_b, (odd, 1)), (then, score_a, top_a))

    for c in range(chunks):
        advance(c, steps)
    for j in range(max(0, turns - 2), turns):
        for k in range(2):
            prob_out(2 * j + k, (j % 2, k)).wait()


def norm_forward(value, gain, shift):
    center = value - jnp.mean(value, -1, keepdims=True)
    inverse = lax.rsqrt(jnp.mean(center * center, -1, keepdims=True) + EPSILON)
    normed = center * inverse
    return normed * gain + shift, normed, inverse


def norm_backward(grad, normed, inverse, gain):
    scaled = grad * gain
    return inverse * (
        scaled
        - jnp.mean(scaled, -1, keepdims=True)
        - normed * jnp.mean(scaled * normed, -1, keepdims=True)
    )


def tile_copy(i, rows, source, target, sem):
    tiles = source.shape[1] // rows
    s, start = i // tiles, (i % tiles) * rows
    own = pl.ds(start if isinstance(i, int) else pl.multiple_of(start, rows), rows)
    return pltpu.make_async_copy(source.at[s, own], target.at[s, own], sem.at[i])


def feed_part(
    cube, r, fr,
    x_all, att_all, dy_all, g2, vec, ub, out_all, out_any, res_all, datt_all, gvec, gub,
    act_s, slope_s, low_s, outer_s, branch_s, gwo, gwu, gwd, out_sem,
):
    nb = cube.nb
    rows, width = low_s.shape
    length = x_all.shape[1]
    tiles = length // rows
    steps = x_all.shape[0] * tiles
    cols = g2.shape[-2] // r - 1 - fr // r
    high = cols.bit_length() - 1
    half = rows // 2
    every = (slice(None),) * nb

    for ref in (gwo, gwu, gwd, gvec, gub):
        ref[...] = jnp.zeros_like(ref)

    bo, ga, sa, bd, gb, sb = [vec[j : j + 1, :] for j in range(2, 8)]

    def wo():
        return g2[every + (slice(0, r), slice(None))].reshape(width, width)

    def wu(c):
        return g2[every + (slice(r + c * r, r + c * r + r), slice(None))].reshape(width, width)

    def wd(c):
        top = tuple((c >> k) & 1 for k in range(high - 1, -1, -1))
        rest = every[high:] + (slice(r + cols * r, None), slice(None))
        return g2[top + rest].reshape(width, width)

    def feed_tile(seq, base):
        tile = pl.ds(pl.multiple_of(base, rows), rows)
        class Part:
            def __init__(self, low):
                self.at = slice(low, low + half)
                self.all = pl.ds(pl.multiple_of(base + low, half), half)

            def enter(self):
                branch = dg(att_all[seq, :, :, self.all].reshape(width, half), wo(), TN)
                value = x_all[seq, self.all, :].astype(f32) + branch + bo
                hidden, self.normed, self.inverse = norm_forward(value, ga, sa)
                self.low = hidden.astype(bf16)
                low_s[self.at, :] = self.low
                self.outer = hidden + bd

            def forward(self, c):
                u = dg(self.low, wu(c), NN) + ub[:, c * width : (c + 1) * width]
                bend = GELU_A + GELU_B * (u * u)
                gate = 0.5 + 0.5 * jnp.tanh(u * bend)
                act = u * gate
                low = act.astype(bf16)
                act_s[c][self.at, :] = low
                slope = gate + act * (1.0 - gate) * (6.0 * bend - 4.0 * GELU_A)
                slope_s[c][self.at, :] = slope.astype(bf16)
                self.outer = self.outer + dg(low, wd(c), NN)

            def turn(self):
                out, normed, inverse = norm_forward(self.outer, gb, sb)
                out_all[seq, self.all, :] = out.astype(bf16)
                dy = dy_all[seq, self.all, :].astype(f32)
                gvec[6:7, :] += col_sum(dy * normed)
                gvec[7:8, :] += col_sum(dy)
                self.d_hidden = norm_backward(dy, normed, inverse, gb)
                gvec[5:6, :] += col_sum(self.d_hidden)
                self.d_outer = self.d_hidden.astype(bf16)
                outer_s[self.at, :] = self.d_outer

            def backward(self, c):
                d_act = dg(self.d_outer, wd(c), NT)
                d_inner = d_act * slope_s[c][self.at, :].astype(f32)
                gub[:, c * width : (c + 1) * width] += col_sum(d_inner)
                low = d_inner.astype(bf16)
                slope_s[c][self.at, :] = low
                self.d_hidden = self.d_hidden + dg(low, wu(c), NT)

            def leave(self):
                gvec[3:4, :] += col_sum(self.d_hidden * self.normed)
                gvec[4:5, :] += col_sum(self.d_hidden)
                d_res1 = norm_backward(self.d_hidden, self.normed, self.inverse, ga)
                res_all[seq, self.all, :] = d_res1
                gvec[2:3, :] += col_sum(d_res1)
                d_branch = d_res1.astype(bf16)
                branch_s[self.at, :] = d_branch
                d_att = dg(d_branch, wo(), NT).astype(bf16)
                for p in range(width // 128):
                    datt_all[seq, p, self.all, :] = d_att[:, 128 * p : 128 * p + 128]

        a, b = Part(0), Part(half)
        a.enter()
        b.enter()
        for c in range(cols):
            a.forward(c)
        b.forward(0)
        a.turn()
        for c in range(1, cols):
            b.forward(c)
        a.backward(0)
        b.turn()
        for c in range(1, cols):
            a.backward(c)
        b.backward(0)
        a.leave()
        for c in range(1, cols):
            b.backward(c)
        for c in range(cols):
            at = slice(c * width, (c + 1) * width)
            gwd[at, :] += dg(act_s[c][...], outer_s[...], TN)
            gwu[:, at] += dg(low_s[...], slope_s[c][...], TN)
            if c == 0:
                b.leave()
        gwo[...] += dg(att_all[seq, :, :, tile].reshape(width, rows), branch_s[...], NN)

    @pl.loop(0, steps)
    def _(i):
        feed_tile(i // tiles, (i % tiles) * rows)
        tile_copy(i, rows, out_all, out_any, out_sem).start()

    g2[every + (slice(0, r), slice(None))] = gwo[...].astype(bf16).reshape((2,) * nb + (r, width))
    for c in range(cols):
        g2[every + (slice(r + c * r, r + c * r + r), slice(None))] = (
            gwu[:, c * width : (c + 1) * width].astype(bf16).reshape((2,) * nb + (r, width))
        )
    g2[every + (slice(r + cols * r, None), slice(None))] = (
        gwd[...].astype(bf16).reshape((2,) * nb + (fr, width))
    )


def prob_load(j, seqs, prob_any, prob_s, prob_sem):
    p, s = j // seqs, j % seqs
    return pltpu.make_async_copy(
        prob_any.at[s, pl.ds(2 * p, 2)], prob_s.at[j % 2], prob_sem.at[j % 2]
    )


def pull_part(
    cube, mem_rows, r, fr,
    x_ref, mem_ref, q_ref, k_ref, v_ref, att_ref, inv_ref, prob_any, da_ref, res_ref, g1, part1,
    gvec_ref, gub_ref, dx_any, sums_o, small_o, prob_s,
    vsel, dot_s, d_a, d_b, pt_s, dt_s, dq_s, dk_s, dv_s, dqt, dkt, dvt, dkm, dvm, turned, terms,
    vec_s, part2, small_s, bufs, send, recv, out_sem, prob_sem,
):
    nb, count = cube.nb, cube.count
    ways = [list(reversed(route)) for route in routes(nb)]
    steps = len(ways[0])
    brief = short(ways[0])
    seqs, length, width = x_ref.shape
    keys = v_ref.shape[2]
    ff = gub_ref.shape[1]
    cols = ff // width
    half = width // 2
    halves = (slice(0, half), slice(half, width))
    pairs = HEADS // 2
    quarter = width // 4

    def scatter(n, source, lo, hi, way):
        return Scatter(cube, source, slice(lo, hi), way, bufs[n], send.at[n], recv.at[n])

    feeds = [scatter(k, part1, k * quarter, (k + 1) * quarter, ways[k % 2]) for k in range(4)]
    heads = [
        scatter(4 + p, part2, 128 * p, 128 * p + 128, ways[p % 2] if p < pairs - 1 else brief)
        for p in range(pairs)
    ]
    smalls = scatter(8, small_s, 0, 128, brief)

    def start(group, step):
        for part in group:
            for copy in part.copies(step):
                copy.start()

    def finish(group, step):
        for part in group:
            for copy in part.copies(step):
                copy.wait()
        for part in group:
            if step < part.steps - 1:
                part.add(step)

    def load(j):
        return prob_load(j, seqs, prob_any, prob_s, prob_sem)

    start(feeds, 0)

    lane = lax.broadcasted_iota(jnp.int32, (1, 128), 1)
    block = d_a.shape[1]
    per_head = length // block
    temp = (d_a, d_b)

    def pair(j):
        p, s = j // seqs, j % seqs
        at = pl.ds(pl.multiple_of(128 * p, 128), 128)
        slot = j % 2
        vp = v_ref[s, p]
        dat = da_ref[s, p].T
        for e in range(2):
            o = 64 * (1 - e)
            mine = (lane < 64) if e == 0 else (lane >= 64)
            vsel[e] = jnp.where(
                mine, vp, jnp.where((lane >= o) & (lane < o + 2), 1.0, 0.0).astype(bf16)
            )
            dt = dat[64 * e : 64 * e + 64, :].astype(f32) * inv_ref[s, 2 * p + e]
            dot_s[e, 64 * e : 64 * e + 64, :] = dt.astype(bf16)
            delta = col_sum(dt * att_ref[s, 2 * p + e].astype(f32))
            hi = delta.astype(bf16).astype(f32)
            row = lax.broadcasted_iota(jnp.int32, (64, length), 0)
            dot_s[e, o : o + 64, :] = jnp.where(
                row == 0, -hi, jnp.where(row == 1, hi - delta, 0.0)
            ).astype(bf16)

        def grads(b):
            e, c = b // per_head, b % per_head
            cut = slice(c * block, (c + 1) * block)
            grad = dg(vsel[e], dot_s[e, :, cut], NN)
            temp[b % 2][...] = (prob_s[slot, e, c].astype(f32) * grad).astype(bf16)
            pt_s[b % 2] = prob_s[slot, e, c, 0:length, :].T
            dt_s[b % 2] = temp[b % 2][0:length, :].T

        def pulls(b):
            e, c = b // per_head, b % per_head
            cut = slice(c * block, (c + 1) * block)
            own = slice(64 * e, 64 * e + 64)
            grad = temp[b % 2]
            dqt[own, cut] = dg(k_ref[s, p, own, :], grad[...], NN)
            dots, queries = dot_s[e, own, cut], q_ref[s, p, own, cut]
            prob = prob_s.at[slot, e, c]
            news = (
                (dvt, dg(dots, pt_s[b % 2], NN)),
                (dkt, dg(queries, dt_s[b % 2], NN)),
                (dvm, dg(dots, prob[length:keys, :], NT)),
                (dkm, dg(queries, grad[length:keys, :], NT)),
            )
            for ref, new in news:
                to = slice(0, new.shape[1])
                if c == 0:
                    ref[own, to] = new
                else:
                    ref[own, to] += new

        grads(0)
        for b in range(2 * per_head):
            if b + 1 < 2 * per_head:
                grads(b + 1)
            pulls(b)
        units = ((dq_s, dqt, None, 1.0), (dk_s, dkt, dkm, LN2), (dv_s, dvt, dvm, 1.0))
        news = []
        for n, (ref, tops, mems, unit) in enumerate(units):
            low = (tops[...] * unit).astype(bf16)
            turned[128 * n : 128 * n + 128, :] = low
            ref[s, 0:length, at] = low.T
            if mems is not None:
                low = (mems[...] * unit).astype(bf16)
                ref[s, length:keys, at] = low.T
                news.append(dg(low, mem_ref[...], NN))
        new = dg(turned[...], x_ref[s], NN)
        add = jnp.where(s == 0, 0.0, 1.0)
        terms[0:128, :] = terms[0:128, :] * add + new[0:128, :] * HEAD_DIM**-0.5
        for n in range(2):
            own = slice(128 * (n + 1), 128 * (n + 2))
            terms[own, :] = terms[own, :] * add + (new[own, :] + news[n])
        vec_s[0:1, at] = vec_s[0:1, at] * add + col_sum(dq_s[s, :, at].astype(f32)) * HEAD_DIM**-0.5
        vec_s[1:2, at] = vec_s[1:2, at] * add + col_sum(dv_s[s, :, at].astype(f32))

        @pl.when(s == seqs - 1)
        def _():
            for n in range(3):
                low = terms[128 * n : 128 * n + 128, :].astype(bf16).T
                part2[(slice(None),) * nb + (slice(n * r, n * r + r), at)] = low.reshape(
                    (2,) * nb + (r, 128)
                )

    terms[...] = jnp.zeros_like(terms)
    vec_s[...] = jnp.zeros_like(vec_s)

    def weight(j):
        return g1[(slice(None),) * nb + (slice(j * r, j * r + r), slice(None))].reshape(width, width)

    scale = HEAD_DIM**-0.5
    tail = slice(length, keys)

    turns = seqs * pairs

    @pl.loop(0, turns)
    def _(j):
        @pl.when(j + 1 < turns)
        def _():
            load(j + 1).start()

        load(j).wait()
        plan = ((1, feeds, 0), (3, feeds[:2], 1), (4, feeds[2:], 1), (5, feeds[:2], 2))
        plan += ((6, feeds[2:], 2), (2, heads[:1], -1), (4, heads[1:2], -1), (6, heads[2:3], -1))
        plan += ((5, heads[:2], 0), (6, heads[:2], 1), (7, heads[:2], 2), (7, heads[2:3], 0))
        for slot, group, step in plan:

            @pl.when(j == (slot * turns) // 8)
            def _():
                if step >= 0:
                    finish(group, step)
                start(group, step + 1)

        pair(j)

    start(heads[3:], 0)
    tails = [jnp.concatenate([ref[s, tail, :] for s in range(seqs)], 0) for ref in (dk_s, dv_s)]
    both = dg(tails[0], weight(1), NT) + dg(tails[1], weight(2), NT)
    gmem = sum(both[s * (keys - length) : (s + 1) * (keys - length), :] for s in range(seqs))
    vec_row = lax.broadcasted_iota(jnp.int32, (8, width), 0)
    vecs = jnp.where(vec_row < 2, vec_s[...], gvec_ref[...])
    flat = jnp.concatenate(
        [
            gmem[0:16, :],
            jnp.concatenate([gmem[16:20, :], vecs[0:4, :]], 0),
            jnp.concatenate([vecs[4:8, :], jnp.zeros((4, width), f32)], 0),
            jnp.zeros((96, width), f32),
        ],
        0,
    )
    small_s[...] = flat.T.reshape((2,) * nb + (16, 128))
    for i in range(count):
        at = tuple((i >> b) & 1 for b in cube.msb_first)
        off = (i * fr) % 128
        up = jnp.broadcast_to(gub_ref[:, i * fr - off : i * fr - off + 128], (8, 128))
        up = pltpu.roll(up, (64 - off) % 128, 1)
        small_s[at + (slice(0, 1), slice(64, 64 + fr))] = up[0:1, 64 : 64 + fr]
    start([smalls], 0)
    tile = 512
    tiles = length // tile

    def inputs(i):
        s, rows = i // tiles, pl.ds((i % tiles) * tile, tile)
        dx = res_ref[s, rows, :] + dg(dq_s[s, rows, :], weight(0), NT) * scale
        dx = dx + dg(dk_s[s, rows, :], weight(1), NT) + dg(dv_s[s, rows, :], weight(2), NT)
        x_ref[s, rows, :] = dx.astype(bf16)
        out = pltpu.make_async_copy(x_ref.at[s, rows], dx_any.at[s, rows], out_sem.at[i])
        out.start()
        return out

    def total(part, lo, hi):
        sums_o[lo:hi, part.lanes] = part.total(part.steps - 1)

    todo = list(range(seqs * tiles))
    outs = []
    group = heads[3:] + [smalls]
    for step in range(len(brief)):
        if todo:
            outs.append(inputs(todo.pop(0)))
        finish(group, step)
        if step + 1 < len(brief):
            start(group, step + 1)
        if step == 0:
            finish(heads[2:3], 1)
            start(heads[2:3], 2)
            finish(feeds, steps - 1)
            for part in feeds:
                total(part, 3 * r, sums_o.shape[0])
        if step == 1:
            finish(heads[2:3], 2)
            start(heads[2:3], 3)
            finish(heads[:2], steps - 1)
    for i in todo:
        outs.append(inputs(i))
    finish(heads[2:3], 3)
    for part in heads:
        total(part, 0, 3 * r)
    small_o[...] = smalls.total(smalls.steps - 1)
    for out in outs:
        out.wait()


def layer_kernel(
    count, sub, mem_rows, r, fr, layout,
    len_ref, x_any, dy_any, wq_ref, wk_ref, wv_ref, wo_ref, wu_ref, wd_ref, memt_ref, ub_ref, *rest,
):
    vec_refs, rest = rest[:8], rest[8:]
    (out_any, dx_any, sums_o, small_o, prob_any), rest = rest[:5], rest[5:]
    (x_ref, q_o, k_o, v_o, att_o, inv_o, g1, g2, gs, vec_o, ub_o, mem_o, gvec, gub), rest = rest[:14], rest[14:]
    (bufs, sems1, feed_sem, dy_sem, load_sem, sems3) = rest
    cube = Cube(count, sub)
    early, late, feed, pull = layout
    dy_load = []

    def attend(*scoped):
        attend_part(
            cube, mem_rows,
            len_ref, x_any, wq_ref, wk_ref, wv_ref, wo_ref, wu_ref, wd_ref, memt_ref, ub_ref,
            vec_refs,
            x_ref, q_o, k_o, v_o, att_o, inv_o, g1, g2, gs, vec_o, ub_o, mem_o, prob_any,
            *scoped, *sems1,
        )

    pl.run_scoped(attend, *early)

    def others(out_s, res_s, datt_s, part2, small_s, prob_s):
        seqs = x_ref.shape[0]
        prob_load(0, seqs, prob_any, prob_s, load_sem).start()

        def forward(dy_s, *scoped):
            load = pltpu.make_async_copy(dy_any, dy_s, dy_sem)
            load.start()
            load.wait()
            feed_part(
                cube, r, fr,
                x_ref, att_o, dy_s, g2, vec_o, ub_o, out_s, out_any, res_s, datt_s, gvec, gub,
                *scoped, feed_sem,
            )

        pl.run_scoped(forward, *feed)

        def backward(*scoped):
            pull_part(
                cube, mem_rows, r, fr,
                x_ref, mem_o, q_o, k_o, v_o, att_o, inv_o, prob_any, datt_s, res_s, g1, g2,
                gvec, gub, dx_any, sums_o, small_o, prob_s,
                *scoped, part2, small_s, bufs, *sems3, load_sem,
            )

        pl.run_scoped(backward, *pull)
        tile = feed[3].shape[0]
        for i in range(feed_sem.shape[0]):
            tile_copy(i, tile, out_s, out_any, feed_sem).wait()

    pl.run_scoped(others, *late)


def layer_call(count, sub, mem_rows, lengths, x, dy, wq, wk, wv, wo, wu, wd, memt, ub, vecs):
    seqs, length, width = x.shape
    r, ff, fr = wq.shape[0], wu.shape[1], wd.shape[0]
    rows2 = r + (ff // width) * r + fr
    keys = length + KEY_PAD
    nb = count.bit_length() - 1
    cube = (2,) * nb
    ways = routes(nb)
    way = list(reversed(ways[0]))
    links = (len(way), most(way))
    wide = (len(way), max(most(way), most(short(way))))
    block = min(512, length)
    tile = min(512, length)
    pairs = HEADS // 2
    quarter = width // 4
    shape = jax.ShapeDtypeStruct
    vm = pl.BlockSpec(memory_space=VMEM)
    hbm = pl.BlockSpec(memory_space=pl.ANY)
    dma = pltpu.SemaphoreType.DMA
    early = (
        VMEM((seqs, HEADS, 128, length), bf16),
        VMEM((seqs, HEADS, keys, 128), bf16),
        VMEM((seqs, HEADS, 80, keys), bf16),
        VMEM((keys, block), f32),
        VMEM((keys, block), f32),
        VMEM((2, 2, keys, block), bf16),
        VMEM((1, block), f32),
        VMEM((1, block), f32),
        VMEM((16, 128), f32),
        VMEM((128, 128), f32),
    )
    late = (
        VMEM(x.shape, bf16),
        VMEM(x.shape, f32),
        VMEM((seqs, pairs, length, 128), bf16),
        VMEM(cube + (3 * r, width), bf16),
        VMEM(cube + (16, 128), f32),
        VMEM((2, 2, length // block, keys, block), bf16),
    )
    feed = (
        VMEM(x.shape, bf16),
        [VMEM((tile, width), bf16)] * (ff // width),
        [VMEM((tile, width), bf16)] * (ff // width),
        VMEM((tile, width), bf16),
        VMEM((tile, width), bf16),
        VMEM((tile, width), bf16),
        VMEM((width, width), f32),
        VMEM((width, ff), f32),
        VMEM((ff, width), f32),
    )
    pull = (
        VMEM((2, keys, 128), bf16),
        VMEM((2, 128, length), bf16),
        VMEM((keys, block), bf16),
        VMEM((keys, block), bf16),
        VMEM((2, block, length), bf16),
        VMEM((2, block, length), bf16),
        VMEM((seqs, length, width), bf16),
        VMEM((seqs, keys, width), bf16),
        VMEM((seqs, keys, width), bf16),
        VMEM((128, length), f32),
        VMEM((128, length), f32),
        VMEM((128, length), f32),
        VMEM((128, KEY_PAD), f32),
        VMEM((128, KEY_PAD), f32),
        VMEM((384, length), bf16),
        VMEM((384, width), f32),
        VMEM((8, width), f32),
    )
    bufs = [scatter_bufs(nb, way, (rows2, quarter), bf16) for _ in range(4)]
    bufs += [scatter_bufs(nb, way, (3 * r, 128), bf16) for _ in range(3)]
    bufs += [scatter_bufs(nb, short(way), (3 * r, 128), bf16)]
    bufs += [scatter_bufs(nb, short(way), (16, 128), f32)]
    return pl.pallas_call(
        functools.partial(layer_kernel, count, sub, mem_rows, r, fr, (early, late, feed, pull)),
        out_shape=(
            shape(x.shape, bf16),
            shape(x.shape, bf16),
            shape((3 * r + rows2, width), f32),
            shape((16, 128), f32),
            shape((seqs, HEADS, length // block, keys, block), bf16),
        ),
        in_specs=[pl.BlockSpec(memory_space=pltpu.SMEM), hbm, hbm] + [vm] * 16,
        out_specs=[hbm, hbm, vm, vm, hbm],
        scratch_shapes=[
            VMEM(x.shape, bf16),
            VMEM((seqs, pairs, 128, length), bf16),
            VMEM((seqs, pairs, 128, keys), bf16),
            VMEM((seqs, pairs, keys, 128), bf16),
            VMEM((seqs, HEADS, HEAD_DIM, length), bf16),
            VMEM((seqs, HEADS, 1, length), f32),
            VMEM(cube + (3 * r, width), bf16),
            VMEM(cube + (rows2, width), bf16),
            VMEM(cube + (16, 128), bf16),
            VMEM((8, width), f32),
            VMEM((1, ff), f32),
            VMEM((KEY_PAD, width), bf16),
            VMEM((8, width), f32),
            VMEM((1, ff), f32),
            bufs,
            [
                dma((2 + ff // width,)),
                dma,
                dma((2, 2)),
                dma((6,) + links),
                dma((6,) + links),
                dma((4,) + links),
                dma((4,) + links),
                dma(links),
                dma(links),
            ],
            dma((seqs * (length // tile),)),
            dma,
            dma((2,)),
            [dma((9,) + wide), dma((9,) + wide), dma((seqs * (length // 512),))],
        ],
        compiler_params=pltpu.CompilerParams(
            collective_id=0, has_side_effects=True, vmem_limit_bytes=63 * 2**20
        ),
        name="layer",
    )(lengths, x, dy, wq, wk, wv, wo, wu, wd, memt, ub, *vecs)


def results_kernel(r, fr, mem_rows, out_any, dx_any, sums, small, out_o, dx_o, *outs):
    outs, (hold, load_sem, save_sem) = outs[:-3], outs[-3:]
    seqs, length = out_any.shape[:2]
    cut = length // 2
    jobs = []
    for n, (src, dst) in enumerate(((out_any, out_o), (dx_any, dx_o))):
        for s in range(seqs):
            for c in range(length // cut):
                at = (s, slice(c * cut, (c + 1) * cut))
                k = len(jobs)
                load = pltpu.make_async_copy(src.at[at], hold.at[k], load_sem.at[k])
                jobs.append((load, pltpu.make_async_copy(hold.at[k], dst.at[at], save_sem.at[k])))
    for load, _ in jobs:
        load.start()
    gq, gk, gv, go, gu, gd, gm, gb = outs[:8]
    vecs = outs[8:]
    width = gq.shape[1]
    cols = gu.shape[1] // width
    for n, ref in enumerate((gq, gk, gv, go)):
        ref[...] = sums[n * r : (n + 1) * r, :]
    for c in range(cols):
        gu[:, c * width : (c + 1) * width] = sums[(4 + c) * r : (5 + c) * r, :]
    gd[...] = sums[(4 + cols) * r :, :]
    value = small[...]
    gm[...] = value[0:r, 0:mem_rows]
    turned = jnp.concatenate([value, jnp.zeros((112, 128), f32)], 0).T
    for n, ref in enumerate(vecs):
        ref[...] = turned[VEC + n : VEC + n + 1, 0:r]
    gb[...] = value[0:1, 64 : 64 + fr]
    for load, save in jobs:
        load.wait()
        save.start()
    for _, save in jobs:
        save.wait()


def results_call(r, fr, mem_rows, ff, out, dx, sums, small):
    width = sums.shape[1]
    seqs, length = dx.shape[:2]
    shape = jax.ShapeDtypeStruct
    vm = pl.BlockSpec(memory_space=VMEM)
    hbm = pl.BlockSpec(memory_space=pl.ANY)
    mats = [(r, width)] * 4 + [(r, ff), (fr, width), (mem_rows, r), (1, fr)] + [(1, r)] * 8
    mats[6] = (r, mem_rows)
    jobs = 4 * seqs
    return pl.pallas_call(
        functools.partial(results_kernel, r, fr, mem_rows),
        out_shape=(shape(out.shape, out.dtype), shape(dx.shape, dx.dtype))
        + tuple(shape(m, f32) for m in mats),
        in_specs=[hbm, hbm, vm, vm],
        out_specs=[hbm, hbm] + [vm] * len(mats),
        scratch_shapes=[
            VMEM((jobs, length // 2, width), bf16),
            pltpu.SemaphoreType.DMA((jobs,)),
            pltpu.SemaphoreType.DMA((jobs,)),
        ],
        compiler_params=pltpu.CompilerParams(vmem_limit_bytes=60 * 2**20),
        name="results",
    )(out, dx, sums, small)


DIMS = (1, 0, 0, 0, 0, 0, 0, 0, 0, 0, 0, 0, 0, 0, 0, 0)


def on_device(devices, inputs, lengths, *rest):
    params, cotangent = rest[:-1], rest[-1]
    width = inputs.shape[2]
    count = min(devices, width // 16)
    sub = devices // count
    sets = [list(range(g * sub, (g + 1) * sub)) for g in range(count)]
    if sub > 1:
        params = tuple(
            lax.all_gather(a, "dp", axis=d, tiled=True, axis_index_groups=sets)
            for a, d in zip(params, DIMS, strict=True)
        )
    (memory, wq, bq, wk, wv, bv, wo, bo, ga, sa, wu, bu, wd, bd, gb, sb) = params
    r, fr = wq.shape[0], wd.shape[0]
    mem_rows = memory.shape[0]

    vecs = [a.reshape(1, r) for a in (bq, bv, bo, ga, sa, bd, gb, sb)]
    out, dx, sums, tiny, _ = layer_call(
        count, sub, mem_rows, lengths, inputs, cotangent, wq, wk, wv, wo, wu, wd, memory.T,
        bu.reshape(1, fr), vecs,
    )
    layer_out, dx, gwq, gwk, gwv, gwo, gwu, gwd, gmem, gbu, *vecs = results_call(
        r, fr, mem_rows, wu.shape[1], out, dx, sums, tiny
    )
    gmem = gmem.T
    gbu = gbu.reshape(fr)
    gbq, gbv, gbo, gga, gsa, gbd, ggb, gsb = [a.reshape(r) for a in vecs]
    grads = (gmem, gwq, gbq, gwk, gwv, gbv, gwo, gbo, gga, gsa, gwu, gbu, gwd, gbd, ggb, gsb)
    if sub > 1:
        grads = tuple(
            lax.psum_scatter(a, "dp", scatter_dimension=d, tiled=True, axis_index_groups=sets)
            for a, d in zip(grads, DIMS, strict=True)
        )
    return (layer_out, dx) + grads


def solution(mesh):
    rows, row, mem = P("dp", None), P("dp"), P(None, "dp")
    full = P("dp", None, None)
    params = (mem, rows, row, rows, rows, row, rows, row, row, row, rows, row, rows, row, row, row)
    return jax.shard_map(
        functools.partial(on_device, mesh.shape["dp"]),
        mesh=mesh,
        in_specs=(full, P("dp")) + params + (full,),
        out_specs=(full, full) + params,
        check_vma=False,
    )
```

```python
import functools

import jax
import jax.numpy as jnp
from jax import lax
from jax.experimental import pallas as pl
from jax.experimental.pallas import tpu as pltpu
from jax.sharding import PartitionSpec as P

HEADS = 8
HEAD_DIM = 64
EPSILON = 1e-05
LOG2E = 1.4426950408889634
LN2 = 0.6931471805599453
GELU_A = 0.7978845608028654
GELU_B = GELU_A * 0.044715
HIDE = -1e30
VEC = 20
KEY_PAD = 32

f32 = jnp.float32
bf16 = jnp.bfloat16
VMEM = pltpu.VMEM
MESH = pl.DeviceIdType.MESH
NN = (((1,), (0,)), ((), ()))
NT = (((1,), (1,)), ((), ()))
TN = (((0,), (0,)), ((), ()))


def dg(left, right, dims):
    return lax.dot_general(left, right, dims, preferred_element_type=f32)


def col_sum(value):
    return jnp.sum(value, 0, keepdims=True)


class Cube:
    def __init__(self, count, sub):
        self.count, self.sub = count, sub
        self.nb = count.bit_length() - 1
        device = lax.axis_index("dp")
        self.device = device
        me = device // sub
        self.bits = [(me // (2**b)) % 2 for b in range(self.nb)]
        self.msb_first = tuple(range(self.nb - 1, -1, -1))

    def partner(self, flips):
        to = self.device
        for b in flips:
            to = to + (1 - 2 * self.bits[b]) * (2**b * self.sub)
        return (to,)

    def greet(self, routes):
        groups = sorted({flips for route in routes for group in route for flips in masks(group)})
        sem = pltpu.get_barrier_semaphore()
        for flips in groups:
            pl.semaphore_signal(sem, inc=1, device_id=self.partner(flips), device_id_type=MESH)
        return len(groups)

    def own(self):
        return tuple(self.bits[b] for b in self.msb_first)


def masks(group):
    return [
        tuple(b for k, b in enumerate(group) if (m >> k) & 1) for m in range(1, 2 ** len(group))
    ]


def routes(nb):
    if nb >= 4:
        far = list(range(nb - 1, 2, -1))
        groups = [tuple(far[k : k + 2]) for k in range(0, len(far), 2)]
        return (groups + [(1,), (2,), (0,)], groups + [(2,), (1,), (0,)])
    return ([(b,) for b in range(nb - 1, -1, -1)],) * 2


def short(route):
    if len(route) != 4:
        return route
    return [route[0], route[1] + route[2], route[3]]


def most(route):
    return max(2 ** len(group) - 1 for group in route)


def gather_copies(cube, ref, route, step, rows, lanes, send, recv):
    done = {b for group in route[:step] for b in group}
    idx = tuple(slice(None) if c in done else cube.bits[c] for c in cube.msb_first)
    view = ref.at[idx + (rows, lanes)]
    return [
        pltpu.make_async_remote_copy(
            src_ref=view,
            dst_ref=view,
            send_sem=send.at[step, k],
            recv_sem=recv.at[step, k],
            device_id=cube.partner(flips),
            device_id_type=MESH,
        )
        for k, flips in enumerate(masks(route[step]))
    ]


class Scatter:
    def __init__(self, cube, source, lanes, route, bufs, send, recv):
        self.cube, self.source, self.lanes, self.route = cube, source, lanes, route
        self.bufs, self.send, self.recv = bufs, send, recv
        self.steps = len(route)

    def _piece(self, step, flips, rest=None):
        cube = self.cube
        gone = {b for group in self.route[:step] for b in group}
        left = [c for c in cube.msb_first if c not in gone]
        rest = iter(rest) if rest is not None else None
        idx = ()
        for c in left:
            if c in self.route[step]:
                idx += (1 - cube.bits[c] if c in flips else cube.bits[c],)
            else:
                idx += (slice(None) if rest is None else next(rest),)
        if step == 0:
            return self.source, idx + (slice(None), self.lanes)
        return self.bufs[step - 1].at[0], idx

    def copies(self, step):
        out = []
        for k, flips in enumerate(masks(self.route[step])):
            ref, idx = self._piece(step, flips)
            out.append(
                pltpu.make_async_remote_copy(
                    src_ref=ref.at[idx],
                    dst_ref=self.bufs[step].at[k],
                    send_sem=self.send.at[step, k],
                    recv_sem=self.recv.at[step, k],
                    device_id=self.cube.partner(flips),
                    device_id_type=MESH,
                )
            )
        return out

    def total(self, step, rest=None):
        ref, idx = self._piece(step, (), rest)
        value = ref[idx].astype(f32)
        for k in range(2 ** len(self.route[step]) - 1):
            value = value + self.bufs[step][(k,) + tuple(rest or ())].astype(f32)
        return value

    def add(self, step):
        free = self.cube.nb - sum(len(group) for group in self.route[: step + 1])
        into = self.bufs[step]
        for flat in range(2**free):
            rest = tuple((flat >> (free - 1 - k)) & 1 for k in range(free))
            into[(0,) + rest] = self.total(step, rest).astype(into.dtype)


def scatter_bufs(nb, route, tail, dtype):
    bufs, left = [], nb
    for group in route:
        left -= len(group)
        bufs.append(VMEM((2 ** len(group) - 1,) + (2,) * left + tail, dtype))
    return bufs


def attend_part(
    cube, mem_rows, greeted,
    len_ref, x_any, wq_ref, wk_ref, wv_ref, wo_ref, wu_ref, wd_ref, memt_ref, ub_ref, vec_refs,
    x_ref, q_o, k_o, v_o, att_o, inv_o, g1, g2, gs, vec_o, ub_o, mem_o, prob_any,
    qt_o, ksel, vt_s, score_a, score_b, prob_s, top_a, top_b, flat_s, wide_s,
    local, x_sem, prob_sem, send1, recv1, send2, recv2, send3, recv3,
):
    nb, count = cube.nb, cube.count
    seqs, length, width = x_ref.shape
    keys = v_o.shape[2]
    mem_pad = keys - length
    r = wq_ref.shape[0]
    ff = wu_ref.shape[1]
    cols = ff // width
    fr = wd_ref.shape[0]
    own = cube.own()
    ways = routes(nb)
    steps = len(ways[0])
    half = width // 2
    halves = (slice(0, half), slice(half, width))
    whole = (slice(None), slice(None))
    x_load = pltpu.make_async_copy(x_any, x_ref, x_sem)
    x_load.start()
    near = [
        pltpu.make_async_copy(
            ref, g1.at[own + (slice(j * r, j * r + r), slice(None))], local.at[2 + cols + j]
        )
        for j, ref in enumerate((wq_ref, wk_ref, wv_ref))
    ]
    for move in near:
        move.start()
    wide_s[...] = jnp.zeros_like(wide_s)
    flat_s[...] = jnp.zeros_like(flat_s)
    for j, ref in enumerate(vec_refs):
        wide_s[VEC + j : VEC + j + 1, 0:r] = ref[...].astype(f32)
    flat_s[0:r, 0:mem_rows] = memt_ref[...].astype(f32)
    flat_s[0:1, 64 : 64 + fr] = ub_ref[...].astype(f32)
    gs[own + whole] = (flat_s[...] + wide_s[...].T[0:16, :]).astype(bf16)
    parts = [(wo_ref, slice(0, r))]
    parts += [
        (wu_ref.at[:, c * width : (c + 1) * width], slice(r + c * r, r + c * r + r))
        for c in range(cols)
    ]
    parts += [(wd_ref, slice(r + cols * r, r + cols * r + fr))]
    moves = [
        pltpu.make_async_copy(ref, g2.at[own + (rows, slice(None))], local.at[j])
        for j, (ref, rows) in enumerate(parts)
    ]
    for move in moves:
        move.start()
    for move in near:
        move.wait()
    pl.semaphore_wait(pltpu.get_barrier_semaphore(), greeted)

    every_row = slice(None)

    def first(j, step):
        rows = slice(j * r, j * r + r)
        copies = []
        for k in range(2):
            links = (send1.at[2 * j + k], recv1.at[2 * j + k])
            copies += gather_copies(cube, g1, ways[k], step, rows, halves[k], *links)
        return copies

    def tiny(step):
        return gather_copies(cube, gs, ways[0], step, every_row, slice(None), send3, recv3)

    chunks = 4
    chunk = width // chunks

    def second(c, step):
        lanes = slice(c * chunk, (c + 1) * chunk)
        return gather_copies(
            cube, g2, ways[c % 2], step, every_row, lanes, send2.at[c], recv2.at[c]
        )

    def advance(c, step):
        if step > 0:
            for copy in second(c, step - 1):
                copy.wait()
        if step < steps:
            for copy in second(c, step):
                copy.start()

    sets = [functools.partial(first, 1), tiny, functools.partial(first, 2), functools.partial(first, 0)]
    for copies in sets:
        for copy in copies(0):
            copy.start()
    for move in moves:
        move.wait()
    def follow(n, step):
        for copy in sets[n](step - 1):
            copy.wait()
        if step < steps:
            for copy in sets[n](step):
                copy.start()

    for step in range(1, steps - 1):
        for n in range(len(sets)):
            follow(n, step)
        if step == 1:
            for c in range(chunks):
                advance(c, 0)
    for step in (steps - 1, steps):
        follow(0, step)
        follow(1, step)
    x_load.wait()

    lane = lax.broadcasted_iota(jnp.int32, (1, 128), 1)
    every = gs[...].astype(f32).reshape(width, 128).T
    mem_o[0:16, :] = every[0:16, :].astype(bf16)
    rest_row = lax.broadcasted_iota(jnp.int32, (16, width), 0)
    mem_o[16:32, :] = jnp.where(rest_row < mem_rows - 16, every[16:32, :], 0.0).astype(bf16)
    vec_o[...] = every[VEC : VEC + 8, :]
    ups = [jnp.zeros((16, 128), f32) for _ in range(ff // 128)]
    for i in range(count):
        at = tuple((i >> b) & 1 for b in cube.msb_first)
        to = (i * fr) % 128
        here = (lane >= to) & (lane < to + fr)
        rolled = pltpu.roll(gs[at + whole].astype(f32), (to - 64) % 128, 1)
        ups[i * fr // 128] = ups[i * fr // 128] + jnp.where(here, rolled, 0.0)
    for g in range(ff // 128):
        ub_o[:, 128 * g : 128 * g + 128] = ups[g][0:1, :]

    def weight(j):
        return g1[(slice(None),) * nb + (slice(j * r, j * r + r), slice(None))].reshape(width, width)

    bq = vec_o[0:1, :]
    bv = vec_o[1:2, :]

    def put_keys(s, rows, kk, bias):
        kb = kk.astype(bf16)
        kt = kb.T
        for p in range(HEADS // 2):
            k_o[s, p, :, rows] = kt[128 * p : 128 * p + 128, :]
        for h in range(HEADS):
            p, o = h // 2, 64 * (1 - h % 2)
            pattern = jnp.where(lane == o, bias, 0.0).astype(bf16)
            mine = (lane < 64) if h % 2 == 0 else (lane >= 64)
            ksel[s, h, rows, :] = jnp.where(mine, kb[:, 128 * p : 128 * p + 128], pattern)

    def put_values(s, rows, vv):
        vb = vv.astype(bf16)
        vt = vb.T
        for p in range(HEADS // 2):
            v_o[s, p, rows, :] = vb[:, 128 * p : 128 * p + 128]
        for h in range(HEADS):
            vt_s[s, h, 0:64, rows] = vt[64 * h : 64 * h + 64, :]

    top_row = lax.broadcasted_iota(jnp.int32, (16, keys), 0)
    ones = jnp.where(top_row == 0, 1.0, 0.0).astype(bf16)
    for s in range(seqs):
        for h in range(HEADS):
            vt_s[s, h, 64:80, :] = ones
    follow(2, steps - 1)
    mem = mem_o[...]
    mem_keys = dg(mem, weight(1), NN)
    mem_row = lax.broadcasted_iota(jnp.int32, (mem_pad, 1), 0)
    mem_bias = jnp.where(mem_row < mem_rows, 0.0, HIDE)
    for s in range(seqs):
        put_keys(s, slice(length, keys), mem_keys, mem_bias)
    tile = 512
    tiles = length // tile
    aux = jnp.where(lax.broadcasted_iota(jnp.int32, (64, tile), 0) == 0, 1.0, 0.0).astype(bf16)

    def place_rows(i):
        start = pl.multiple_of((i % tiles) * tile, tile)
        return i // tiles, start, pl.ds(start, tile)

    @pl.loop(0, seqs * tiles)
    def _(i):
        s, start, rows = place_rows(i)
        row = lax.broadcasted_iota(jnp.int32, (tile, 1), 0) + start
        bias = jnp.where(row < len_ref[s], 0.0, HIDE)
        put_keys(s, rows, dg(x_ref[s, rows, :], weight(1), NN), bias)

    follow(3, steps - 1)
    follow(2, steps)
    mem_values = dg(mem, weight(2), NN) + bv
    for s in range(seqs):
        put_values(s, slice(length, keys), mem_values)

    @pl.loop(0, seqs * tiles)
    def _(i):
        s, start, rows = place_rows(i)
        put_values(s, rows, dg(x_ref[s, rows, :], weight(2), NN) + bv)

    follow(3, steps)
    advance(0, 1)
    advance(1, 1)

    @pl.loop(0, seqs * tiles)
    def _(i):
        s, start, rows = place_rows(i)
        qb = ((dg(x_ref[s, rows, :], weight(0), NN) + bq) * (LOG2E * HEAD_DIM**-0.5)).astype(bf16)
        qt = qb.T
        for p in range(HEADS // 2):
            q_o[s, p, :, rows] = qt[128 * p : 128 * p + 128, :]
        for h in range(HEADS):
            e = h % 2
            qt_o[s, h, 64 * e : 64 * e + 64, rows] = qt[64 * h : 64 * h + 64, :]
            qt_o[s, h, 64 * (1 - e) : 64 * (1 - e) + 64, rows] = aux

    block = score_a.shape[1]
    per_head = length // block
    blocks = seqs * HEADS * per_head

    def place(i):
        s = i // (HEADS * per_head)
        h = (i // per_head) % HEADS
        return s, h, pl.ds(pl.multiple_of((i % per_head) * block, block), block)

    cuts = [slice(c, c + 256) for c in range(0, length - 256, 256)] + [slice(length - 256, keys)]

    def turn(i, now, then):
        if i is not None:
            score, top, slot = now
            s, h, at = place(i)
            peak = top[...]
            mixed = 0.0
        if then is not None:
            next_i, next_score, next_top = then
            next_s, next_h, next_at = place(next_i)
            column = qt_o[next_s, next_h, :, next_at]
            high = None
        for cut in cuts:
            if then is not None:
                value = dg(ksel[next_s, next_h, cut, :], column, NN)
                next_score[cut, :] = value
                part = jnp.max(value.reshape(-1, 8, block), 0)
                high = part if high is None else jnp.maximum(high, part)
            if i is not None:
                weights = jnp.exp2(score[cut, :] - peak).astype(bf16)
                prob_s[slot + (cut, slice(None))] = weights
                mixed = mixed + dg(vt_s[s, h, :, cut], weights, NN)
        if then is not None:
            next_top[...] = jnp.max(high, 0, keepdims=True)
        if i is not None:
            prob_out(i, slot).start()
            inverse = 1.0 / mixed[64:65, :]
            att_o[s, h, :, at] = (mixed[0:64, :] * inverse).astype(bf16)
            inv_o[s, h, :, at] = inverse

    def prob_out(i, slot):
        s, h, _ = place(i)
        return pltpu.make_async_copy(
            prob_s.at[slot], prob_any.at[s, h, i % per_head], prob_sem.at[slot]
        )

    turn(None, None, (0, score_a, top_a))
    turns = blocks // 2
    plan = ((2, 0, 2), (2, 1, 2), (3, 2, 1), (3, 3, 1), (9, 0, 3), (9, 1, 3), (9, 2, 2), (9, 3, 2))
    plan += ((15, 2, 3), (15, 3, 3))

    @pl.loop(0, turns)
    def _(j):
        for slot, c, step in plan:

            @pl.when(j == (slot * turns) // 16)
            def _():
                advance(c, step)

        odd = j % 2

        @pl.when(j > 1)
        def _():
            for k in range(2):
                prob_out(2 * j - 4 + k, (odd, k)).wait()

        turn(2 * j, (score_a, top_a, (odd, 0)), (2 * j + 1, score_b, top_b))
        then = jnp.minimum(2 * j + 2, blocks - 1)
        turn(2 * j + 1, (score_b, top_b, (odd, 1)), (then, score_a, top_a))

    for c in range(chunks):
        advance(c, steps)
    for j in range(max(0, turns - 2), turns):
        for k in range(2):
            prob_out(2 * j + k, (j % 2, k)).wait()


def norm_forward(value, gain, shift):
    center = value - jnp.mean(value, -1, keepdims=True)
    inverse = lax.rsqrt(jnp.mean(center * center, -1, keepdims=True) + EPSILON)
    normed = center * inverse
    return normed * gain + shift, normed, inverse


def norm_backward(grad, normed, inverse, gain):
    scaled = grad * gain
    return inverse * (
        scaled
        - jnp.mean(scaled, -1, keepdims=True)
        - normed * jnp.mean(scaled * normed, -1, keepdims=True)
    )


def tile_copy(i, rows, source, target, sem):
    tiles = source.shape[1] // rows
    s, start = i // tiles, (i % tiles) * rows
    own = pl.ds(start if isinstance(i, int) else pl.multiple_of(start, rows), rows)
    return pltpu.make_async_copy(source.at[s, own], target.at[s, own], sem.at[i])


def feed_part(
    cube, r, fr,
    x_all, att_all, both_all, g2, vec, ub, out_any, res_all, datt_all, gvec, gub,
    act_s, slope_s, low_s, outer_s, branch_s, gwo, gwu, gwd, out_sem,
):
    nb = cube.nb
    rows, width = low_s.shape
    length = x_all.shape[1]
    tiles = length // rows
    steps = x_all.shape[0] * tiles
    cols = g2.shape[-2] // r - 1 - fr // r
    high = cols.bit_length() - 1
    half = rows // 2
    every = (slice(None),) * nb

    for ref in (gwo, gwu, gwd, gvec, gub):
        ref[...] = jnp.zeros_like(ref)

    bo, ga, sa, bd, gb, sb = [vec[j : j + 1, :] for j in range(2, 8)]

    def wo():
        return g2[every + (slice(0, r), slice(None))].reshape(width, width)

    def wu(c):
        return g2[every + (slice(r + c * r, r + c * r + r), slice(None))].reshape(width, width)

    def wd(c):
        top = tuple((c >> k) & 1 for k in range(high - 1, -1, -1))
        rest = every[high:] + (slice(r + cols * r, None), slice(None))
        return g2[top + rest].reshape(width, width)

    def feed_tile(seq, base):
        tile = pl.ds(pl.multiple_of(base, rows), rows)
        class Part:
            def __init__(self, low):
                self.at = slice(low, low + half)
                self.all = pl.ds(pl.multiple_of(base + low, half), half)

            def enter(self):
                branch = dg(att_all[seq, :, :, self.all].reshape(width, half), wo(), TN)
                value = x_all[seq, self.all, :].astype(f32) + branch + bo
                hidden, self.normed, self.inverse = norm_forward(value, ga, sa)
                self.low = hidden.astype(bf16)
                low_s[self.at, :] = self.low
                self.outer = hidden + bd

            def forward(self, c):
                u = dg(self.low, wu(c), NN) + ub[:, c * width : (c + 1) * width]
                bend = GELU_A + GELU_B * (u * u)
                gate = 0.5 + 0.5 * jnp.tanh(u * bend)
                act = u * gate
                low = act.astype(bf16)
                act_s[c][self.at, :] = low
                slope = gate + act * (1.0 - gate) * (6.0 * bend - 4.0 * GELU_A)
                slope_s[c][self.at, :] = slope.astype(bf16)
                self.outer = self.outer + dg(low, wd(c), NN)

            def turn(self):
                out, normed, inverse = norm_forward(self.outer, gb, sb)
                dy = both_all[seq, self.all, :].astype(f32)
                both_all[seq, self.all, :] = out.astype(bf16)
                gvec[6:7, :] += col_sum(dy * normed)
                gvec[7:8, :] += col_sum(dy)
                self.d_hidden = norm_backward(dy, normed, inverse, gb)
                gvec[5:6, :] += col_sum(self.d_hidden)
                self.d_outer = self.d_hidden.astype(bf16)
                outer_s[self.at, :] = self.d_outer

            def backward(self, c):
                d_act = dg(self.d_outer, wd(c), NT)
                d_inner = d_act * slope_s[c][self.at, :].astype(f32)
                gub[:, c * width : (c + 1) * width] += col_sum(d_inner)
                low = d_inner.astype(bf16)
                slope_s[c][self.at, :] = low
                self.d_hidden = self.d_hidden + dg(low, wu(c), NT)

            def leave(self):
                gvec[3:4, :] += col_sum(self.d_hidden * self.normed)
                gvec[4:5, :] += col_sum(self.d_hidden)
                d_res1 = norm_backward(self.d_hidden, self.normed, self.inverse, ga)
                res_all[seq, self.all, :] = d_res1
                gvec[2:3, :] += col_sum(d_res1)
                d_branch = d_res1.astype(bf16)
                branch_s[self.at, :] = d_branch
                d_att = dg(d_branch, wo(), NT).astype(bf16)
                for p in range(width // 128):
                    datt_all[seq, p, self.all, :] = d_att[:, 128 * p : 128 * p + 128]

        a, b = Part(0), Part(half)
        a.enter()
        b.enter()
        for c in range(cols):
            a.forward(c)
        b.forward(0)
        a.turn()
        for c in range(1, cols):
            b.forward(c)
        a.backward(0)
        b.turn()
        for c in range(1, cols):
            a.backward(c)
        b.backward(0)
        a.leave()
        for c in range(1, cols):
            b.backward(c)
        for c in range(cols):
            at = slice(c * width, (c + 1) * width)
            gwd[at, :] += dg(act_s[c][...], outer_s[...], TN)
            gwu[:, at] += dg(low_s[...], slope_s[c][...], TN)
            if c == 0:
                b.leave()
        gwo[...] += dg(att_all[seq, :, :, tile].reshape(width, rows), branch_s[...], NN)

    @pl.loop(0, steps)
    def _(i):
        feed_tile(i // tiles, (i % tiles) * rows)
        tile_copy(i, rows, both_all, out_any, out_sem).start()

    g2[every + (slice(0, r), slice(None))] = gwo[...].astype(bf16).reshape((2,) * nb + (r, width))
    for c in range(cols):
        g2[every + (slice(r + c * r, r + c * r + r), slice(None))] = (
            gwu[:, c * width : (c + 1) * width].astype(bf16).reshape((2,) * nb + (r, width))
        )
    g2[every + (slice(r + cols * r, None), slice(None))] = (
        gwd[...].astype(bf16).reshape((2,) * nb + (fr, width))
    )


def prob_load(j, seqs, prob_any, prob_s, prob_sem):
    p, s = j // seqs, j % seqs
    return pltpu.make_async_copy(
        prob_any.at[s, pl.ds(2 * p, 2)], prob_s.at[j % 2], prob_sem.at[j % 2]
    )


def pull_part(
    cube, mem_rows, r, fr,
    x_ref, mem_ref, q_ref, k_ref, v_ref, att_ref, inv_ref, prob_any, da_ref, res_ref, g1, part1,
    gvec_ref, gub_ref, dx_any, sums_o, small_o, prob_s,
    vsel, dot_s, d_a, d_b, pt_s, dt_s, dq_s, dk_s, dv_s, dqt, dkt, dvt, dkm, dvm, turned, terms,
    vec_s, part2, small_s, bufs, send, recv, out_sem, prob_sem,
):
    nb, count = cube.nb, cube.count
    ways = [list(reversed(route)) for route in routes(nb)]
    steps = len(ways[0])
    brief = short(ways[0])
    seqs, length, width = x_ref.shape
    keys = v_ref.shape[2]
    ff = gub_ref.shape[1]
    cols = ff // width
    half = width // 2
    halves = (slice(0, half), slice(half, width))
    pairs = HEADS // 2
    quarter = width // 4

    def scatter(n, source, lo, hi, way):
        return Scatter(cube, source, slice(lo, hi), way, bufs[n], send.at[n], recv.at[n])

    feeds = [scatter(k, part1, k * quarter, (k + 1) * quarter, ways[k % 2]) for k in range(4)]
    heads = [
        scatter(4 + p, part2, 128 * p, 128 * p + 128, ways[p % 2] if p < pairs - 1 else brief)
        for p in range(pairs)
    ]
    smalls = scatter(8, small_s, 0, 128, brief)

    def start(group, step):
        for part in group:
            for copy in part.copies(step):
                copy.start()

    def finish(group, step):
        for part in group:
            for copy in part.copies(step):
                copy.wait()
        for part in group:
            if step < part.steps - 1:
                part.add(step)

    def load(j):
        return prob_load(j, seqs, prob_any, prob_s, prob_sem)

    start(feeds, 0)

    lane = lax.broadcasted_iota(jnp.int32, (1, 128), 1)
    block = d_a.shape[1]
    per_head = length // block
    temp = (d_a, d_b)

    def pair(j):
        p, s = j // seqs, j % seqs
        at = pl.ds(pl.multiple_of(128 * p, 128), 128)
        slot = j % 2
        vp = v_ref[s, p]
        dat = da_ref[s, p].T
        for e in range(2):
            o = 64 * (1 - e)
            mine = (lane < 64) if e == 0 else (lane >= 64)
            vsel[e] = jnp.where(
                mine, vp, jnp.where((lane >= o) & (lane < o + 2), 1.0, 0.0).astype(bf16)
            )
            dt = dat[64 * e : 64 * e + 64, :].astype(f32) * inv_ref[s, 2 * p + e]
            dot_s[e, 64 * e : 64 * e + 64, :] = dt.astype(bf16)
            delta = col_sum(dt * att_ref[s, 2 * p + e].astype(f32))
            hi = delta.astype(bf16).astype(f32)
            row = lax.broadcasted_iota(jnp.int32, (64, length), 0)
            dot_s[e, o : o + 64, :] = jnp.where(
                row == 0, -hi, jnp.where(row == 1, hi - delta, 0.0)
            ).astype(bf16)

        def grads(b):
            e, c = b // per_head, b % per_head
            cut = slice(c * block, (c + 1) * block)
            grad = dg(vsel[e], dot_s[e, :, cut], NN)
            temp[b % 2][...] = (prob_s[slot, e, c].astype(f32) * grad).astype(bf16)
            pt_s[b % 2] = prob_s[slot, e, c, 0:length, :].T
            dt_s[b % 2] = temp[b % 2][0:length, :].T

        def pulls(b):
            e, c = b // per_head, b % per_head
            cut = slice(c * block, (c + 1) * block)
            own = slice(64 * e, 64 * e + 64)
            grad = temp[b % 2]
            dqt[own, cut] = dg(k_ref[s, p, own, :], grad[...], NN)
            dots, queries = dot_s[e, own, cut], q_ref[s, p, own, cut]
            prob = prob_s.at[slot, e, c]
            news = (
                (dvt, dg(dots, pt_s[b % 2], NN)),
                (dkt, dg(queries, dt_s[b % 2], NN)),
                (dvm, dg(dots, prob[length:keys, :], NT)),
                (dkm, dg(queries, grad[length:keys, :], NT)),
            )
            for ref, new in news:
                to = slice(0, new.shape[1])
                if c == 0:
                    ref[own, to] = new
                else:
                    ref[own, to] += new

        grads(0)
        for b in range(2 * per_head):
            if b + 1 < 2 * per_head:
                grads(b + 1)
            pulls(b)
        units = ((dq_s, dqt, None, 1.0), (dk_s, dkt, dkm, LN2), (dv_s, dvt, dvm, 1.0))
        news = []
        for n, (ref, tops, mems, unit) in enumerate(units):
            low = (tops[...] * unit).astype(bf16)
            turned[128 * n : 128 * n + 128, :] = low
            ref[s, 0:length, at] = low.T
            if mems is not None:
                low = (mems[...] * unit).astype(bf16)
                ref[s, length:keys, at] = low.T
                news.append(dg(low, mem_ref[...], NN))
        new = dg(turned[...], x_ref[s], NN)
        add = jnp.where(s == 0, 0.0, 1.0)
        terms[0:128, :] = terms[0:128, :] * add + new[0:128, :] * HEAD_DIM**-0.5
        for n in range(2):
            own = slice(128 * (n + 1), 128 * (n + 2))
            terms[own, :] = terms[own, :] * add + (new[own, :] + news[n])
        vec_s[0:1, at] = vec_s[0:1, at] * add + col_sum(dq_s[s, :, at].astype(f32)) * HEAD_DIM**-0.5
        vec_s[1:2, at] = vec_s[1:2, at] * add + col_sum(dv_s[s, :, at].astype(f32))

        @pl.when(s == seqs - 1)
        def _():
            for n in range(3):
                low = terms[128 * n : 128 * n + 128, :].astype(bf16).T
                part2[(slice(None),) * nb + (slice(n * r, n * r + r), at)] = low.reshape(
                    (2,) * nb + (r, 128)
                )

    terms[...] = jnp.zeros_like(terms)
    vec_s[...] = jnp.zeros_like(vec_s)

    def weight(j):
        return g1[(slice(None),) * nb + (slice(j * r, j * r + r), slice(None))].reshape(width, width)

    scale = HEAD_DIM**-0.5
    tail = slice(length, keys)

    turns = seqs * pairs

    @pl.loop(0, turns)
    def _(j):
        @pl.when(j + 1 < turns)
        def _():
            load(j + 1).start()

        load(j).wait()
        plan = ((1, feeds, 0), (3, feeds[:2], 1), (4, feeds[2:], 1), (5, feeds[:2], 2))
        plan += ((6, feeds[2:], 2), (2, heads[:1], -1), (4, heads[1:2], -1), (6, heads[2:3], -1))
        plan += ((5, heads[:2], 0), (6, heads[:2], 1), (7, heads[:2], 2), (7, heads[2:3], 0))
        for slot, group, step in plan:

            @pl.when(j == (slot * turns) // 8)
            def _():
                if step >= 0:
                    finish(group, step)
                start(group, step + 1)

        pair(j)

    start(heads[3:], 0)
    tails = [jnp.concatenate([ref[s, tail, :] for s in range(seqs)], 0) for ref in (dk_s, dv_s)]
    both = dg(tails[0], weight(1), NT) + dg(tails[1], weight(2), NT)
    gmem = sum(both[s * (keys - length) : (s + 1) * (keys - length), :] for s in range(seqs))
    vec_row = lax.broadcasted_iota(jnp.int32, (8, width), 0)
    vecs = jnp.where(vec_row < 2, vec_s[...], gvec_ref[...])
    flat = jnp.concatenate(
        [
            gmem[0:16, :],
            jnp.concatenate([gmem[16:20, :], vecs[0:4, :]], 0),
            jnp.concatenate([vecs[4:8, :], jnp.zeros((4, width), f32)], 0),
            jnp.zeros((96, width), f32),
        ],
        0,
    )
    small_s[...] = flat.T.reshape((2,) * nb + (16, 128))
    for i in range(count):
        at = tuple((i >> b) & 1 for b in cube.msb_first)
        off = (i * fr) % 128
        up = jnp.broadcast_to(gub_ref[:, i * fr - off : i * fr - off + 128], (8, 128))
        up = pltpu.roll(up, (64 - off) % 128, 1)
        small_s[at + (slice(0, 1), slice(64, 64 + fr))] = up[0:1, 64 : 64 + fr]
    finish(heads[3:], 0)
    start(heads[3:], 1)
    start([smalls], 0)
    tile = 512
    tiles = length // tile

    def inputs(i):
        s, rows = i // tiles, pl.ds((i % tiles) * tile, tile)
        dx = res_ref[s, rows, :] + dg(dq_s[s, rows, :], weight(0), NT) * scale
        dx = dx + dg(dk_s[s, rows, :], weight(1), NT) + dg(dv_s[s, rows, :], weight(2), NT)
        x_ref[s, rows, :] = dx.astype(bf16)
        out = pltpu.make_async_copy(x_ref.at[s, rows], dx_any.at[s, rows], out_sem.at[i])
        out.start()
        return out

    def total(part, lo, hi):
        sums_o[lo:hi, part.lanes] = part.total(part.steps - 1)

    todo = list(range(seqs * tiles))
    outs = []

    def some():
        if todo:
            outs.append(inputs(todo.pop(0)))

    def follow(part, step):
        finish([part], step)
        if step + 1 < part.steps:
            start([part], step + 1)

    follow(heads[2], 1)
    some()
    follow(smalls, 0)
    finish(feeds, steps - 1)
    for part in feeds:
        total(part, 3 * r, sums_o.shape[0])
    for step in range(1, len(brief) - 1):
        follow(heads[3], step)
        some()
        follow(smalls, step)
    follow(heads[2], 2)
    some()
    finish(heads[:2], steps - 1)
    for part in heads[:2]:
        total(part, 0, 3 * r)
    for i in todo:
        outs.append(inputs(i))
    finish(heads[2:3], steps - 1)
    finish([heads[3], smalls], len(brief) - 1)
    for part in heads[2:]:
        total(part, 0, 3 * r)
    small_o[...] = smalls.total(smalls.steps - 1)
    for out in outs:
        out.wait()


def layer_kernel(
    count, sub, mem_rows, r, fr, layout,
    len_ref, x_any, dy_any, wq_ref, wk_ref, wv_ref, wo_ref, wu_ref, wd_ref, memt_ref, ub_ref, *rest,
):
    vec_refs, rest = rest[:8], rest[8:]
    (out_any, dx_any, sums_o, small_o, prob_any), rest = rest[:5], rest[5:]
    held, rest = rest[:15], rest[15:]
    (x_ref, dy_ref, q_o, k_o, v_o, att_o, inv_o, g1, g2, gs, vec_o, ub_o, mem_o, gvec, gub) = held
    (bufs, sems1, feed_sem, dy_sem, load_sem, sems3) = rest
    cube = Cube(count, sub)
    early, late, feed, pull = layout
    ways = routes(cube.nb)
    greeted = cube.greet([*ways, short(list(reversed(ways[0])))])
    dy_load = pltpu.make_async_copy(dy_any, dy_ref, dy_sem)
    dy_load.start()

    def attend(*scoped):
        attend_part(
            cube, mem_rows, greeted,
            len_ref, x_any, wq_ref, wk_ref, wv_ref, wo_ref, wu_ref, wd_ref, memt_ref, ub_ref,
            vec_refs,
            x_ref, q_o, k_o, v_o, att_o, inv_o, g1, g2, gs, vec_o, ub_o, mem_o, prob_any,
            *scoped, *sems1,
        )

    pl.run_scoped(attend, *early)

    def others(res_s, datt_s, part2, small_s, prob_s):
        seqs = x_ref.shape[0]
        prob_load(0, seqs, prob_any, prob_s, load_sem).start()

        def forward(*scoped):
            dy_load.wait()
            feed_part(
                cube, r, fr,
                x_ref, att_o, dy_ref, g2, vec_o, ub_o, out_any, res_s, datt_s, gvec, gub,
                *scoped, feed_sem,
            )

        pl.run_scoped(forward, *feed)

        def backward(*scoped):
            pull_part(
                cube, mem_rows, r, fr,
                x_ref, mem_o, q_o, k_o, v_o, att_o, inv_o, prob_any, datt_s, res_s, g1, g2,
                gvec, gub, dx_any, sums_o, small_o, prob_s,
                *scoped, part2, small_s, bufs, *sems3, load_sem,
            )

        pl.run_scoped(backward, *pull)
        tile = feed[2].shape[0]
        for i in range(feed_sem.shape[0]):
            tile_copy(i, tile, dy_ref, out_any, feed_sem).wait()

    pl.run_scoped(others, *late)


def layer_call(count, sub, mem_rows, lengths, x, dy, wq, wk, wv, wo, wu, wd, memt, ub, vecs):
    seqs, length, width = x.shape
    r, ff, fr = wq.shape[0], wu.shape[1], wd.shape[0]
    rows2 = r + (ff // width) * r + fr
    keys = length + KEY_PAD
    nb = count.bit_length() - 1
    cube = (2,) * nb
    ways = routes(nb)
    way = list(reversed(ways[0]))
    links = (len(way), most(way))
    wide = (len(way), max(most(way), most(short(way))))
    block = min(512, length)
    tile = min(512, length)
    pairs = HEADS // 2
    quarter = width // 4
    shape = jax.ShapeDtypeStruct
    vm = pl.BlockSpec(memory_space=VMEM)
    hbm = pl.BlockSpec(memory_space=pl.ANY)
    dma = pltpu.SemaphoreType.DMA
    early = (
        VMEM((seqs, HEADS, 128, length), bf16),
        VMEM((seqs, HEADS, keys, 128), bf16),
        VMEM((seqs, HEADS, 80, keys), bf16),
        VMEM((keys, block), f32),
        VMEM((keys, block), f32),
        VMEM((2, 2, keys, block), bf16),
        VMEM((1, block), f32),
        VMEM((1, block), f32),
        VMEM((16, 128), f32),
        VMEM((128, 128), f32),
    )
    late = (
        VMEM(x.shape, f32),
        VMEM((seqs, pairs, length, 128), bf16),
        VMEM(cube + (3 * r, width), bf16),
        VMEM(cube + (16, 128), f32),
        VMEM((2, 2, length // block, keys, block), bf16),
    )
    feed = (
        [VMEM((tile, width), bf16)] * (ff // width),
        [VMEM((tile, width), bf16)] * (ff // width),
        VMEM((tile, width), bf16),
        VMEM((tile, width), bf16),
        VMEM((tile, width), bf16),
        VMEM((width, width), f32),
        VMEM((width, ff), f32),
        VMEM((ff, width), f32),
    )
    pull = (
        VMEM((2, keys, 128), bf16),
        VMEM((2, 128, length), bf16),
        VMEM((keys, block), bf16),
        VMEM((keys, block), bf16),
        VMEM((2, block, length), bf16),
        VMEM((2, block, length), bf16),
        VMEM((seqs, length, width), bf16),
        VMEM((seqs, keys, width), bf16),
        VMEM((seqs, keys, width), bf16),
        VMEM((128, length), f32),
        VMEM((128, length), f32),
        VMEM((128, length), f32),
        VMEM((128, KEY_PAD), f32),
        VMEM((128, KEY_PAD), f32),
        VMEM((384, length), bf16),
        VMEM((384, width), f32),
        VMEM((8, width), f32),
    )
    bufs = [scatter_bufs(nb, way, (rows2, quarter), bf16) for _ in range(4)]
    bufs += [scatter_bufs(nb, way, (3 * r, 128), bf16) for _ in range(3)]
    bufs += [scatter_bufs(nb, short(way), (3 * r, 128), bf16)]
    bufs += [scatter_bufs(nb, short(way), (16, 128), f32)]
    return pl.pallas_call(
        functools.partial(layer_kernel, count, sub, mem_rows, r, fr, (early, late, feed, pull)),
        out_shape=(
            shape(x.shape, bf16),
            shape(x.shape, bf16),
            shape((3 * r + rows2, width), f32),
            shape((16, 128), f32),
            shape((seqs, HEADS, length // block, keys, block), bf16),
        ),
        in_specs=[pl.BlockSpec(memory_space=pltpu.SMEM)] + [hbm] * 8 + [vm] * 10,
        out_specs=[hbm, hbm, vm, vm, hbm],
        scratch_shapes=[
            VMEM(x.shape, bf16),
            VMEM(x.shape, bf16),
            VMEM((seqs, pairs, 128, length), bf16),
            VMEM((seqs, pairs, 128, keys), bf16),
            VMEM((seqs, pairs, keys, 128), bf16),
            VMEM((seqs, HEADS, HEAD_DIM, length), bf16),
            VMEM((seqs, HEADS, 1, length), f32),
            VMEM(cube + (3 * r, width), bf16),
            VMEM(cube + (rows2, width), bf16),
            VMEM(cube + (16, 128), bf16),
            VMEM((8, width), f32),
            VMEM((1, ff), f32),
            VMEM((KEY_PAD, width), bf16),
            VMEM((8, width), f32),
            VMEM((1, ff), f32),
            bufs,
            [
                dma((5 + ff // width,)),
                dma,
                dma((2, 2)),
                dma((6,) + links),
                dma((6,) + links),
                dma((4,) + links),
                dma((4,) + links),
                dma(links),
                dma(links),
            ],
            dma((seqs * (length // tile),)),
            dma,
            dma((2,)),
            [dma((9,) + wide), dma((9,) + wide), dma((seqs * (length // 512),))],
        ],
        compiler_params=pltpu.CompilerParams(
            collective_id=0, has_side_effects=True, vmem_limit_bytes=63 * 2**20
        ),
        name="layer",
    )(lengths, x, dy, wq, wk, wv, wo, wu, wd, memt, ub, *vecs)


def results_kernel(r, fr, mem_rows, out_any, dx_any, sums_any, small_any, out_o, dx_o, *rest):
    outs, (sums, small, hold, first_sem, load_sem, save_sem, *kept, kept_sem) = rest[:16], rest[16:]
    length = out_any.shape[1]
    pieces = hold.shape[0] // (2 * out_any.shape[0])
    cut = length // pieces
    firsts = [
        pltpu.make_async_copy(a, b, first_sem.at[n])
        for n, (a, b) in enumerate(((sums_any, sums), (small_any, small)))
    ]
    for move in firsts:
        move.start()
    jobs = []
    for src, dst in ((out_any, out_o), (dx_any, dx_o)):
        for s in range(out_any.shape[0]):
            for c in range(pieces):
                at = (s, slice(c * cut, (c + 1) * cut))
                k = len(jobs)
                load = pltpu.make_async_copy(src.at[at], hold.at[k], load_sem.at[k])
                jobs.append((load, pltpu.make_async_copy(hold.at[k], dst.at[at], save_sem.at[k])))
    for load, _ in jobs:
        load.start()
    for move in firsts:
        move.wait()
    gq, gk, gv, go, gu, gd, gm, gb = kept[:8]
    vecs = kept[8:]
    width = gq.shape[1]
    cols = gu.shape[1] // width
    for n, ref in enumerate((gq, gk, gv, go)):
        ref[...] = sums[n * r : (n + 1) * r, :]
    for c in range(cols):
        gu[:, c * width : (c + 1) * width] = sums[(4 + c) * r : (5 + c) * r, :]
    gd[...] = sums[(4 + cols) * r :, :]
    value = small[...]
    gm[...] = value[0:r, 0:mem_rows]
    turned = jnp.concatenate([value, jnp.zeros((112, 128), f32)], 0).T
    for n, ref in enumerate(vecs):
        ref[...] = turned[VEC + n : VEC + n + 1, 0:r]
    gb[...] = value[0:1, 64 : 64 + fr]
    saves = [
        pltpu.make_async_copy(a, b, kept_sem.at[n])
        for n, (a, b) in enumerate(zip(kept, outs, strict=True))
    ]
    for save in saves:
        save.start()
    for load, save in jobs:
        load.wait()
        save.start()
    for save in saves + [save for _, save in jobs]:
        save.wait()


def results_call(r, fr, mem_rows, ff, out, dx, sums, small):
    width = sums.shape[1]
    seqs, length = dx.shape[:2]
    shape = jax.ShapeDtypeStruct
    hbm = pl.BlockSpec(memory_space=pl.ANY)
    dma = pltpu.SemaphoreType.DMA
    mats = [(r, width)] * 4 + [(r, ff), (fr, width), (r, mem_rows), (1, fr)] + [(1, r)] * 8
    jobs = 8 * seqs
    return pl.pallas_call(
        functools.partial(results_kernel, r, fr, mem_rows),
        out_shape=(shape(out.shape, out.dtype), shape(dx.shape, dx.dtype))
        + tuple(shape(m, f32) for m in mats),
        in_specs=[hbm] * 4,
        out_specs=[hbm] * (2 + len(mats)),
        scratch_shapes=[
            VMEM(sums.shape, f32),
            VMEM(small.shape, f32),
            VMEM((jobs, 2 * seqs * length // jobs, width), bf16),
            dma((2,)),
            dma((jobs,)),
            dma((jobs,)),
            *[VMEM(m, f32) for m in mats],
            dma((len(mats),)),
        ],
        compiler_params=pltpu.CompilerParams(vmem_limit_bytes=60 * 2**20),
        name="results",
    )(out, dx, sums, small)


DIMS = (1, 0, 0, 0, 0, 0, 0, 0, 0, 0, 0, 0, 0, 0, 0, 0)


def on_device(devices, inputs, lengths, *rest):
    params, cotangent = rest[:-1], rest[-1]
    width = inputs.shape[2]
    count = min(devices, width // 16)
    sub = devices // count
    sets = [list(range(g * sub, (g + 1) * sub)) for g in range(count)]
    if sub > 1:
        params = tuple(
            lax.all_gather(a, "dp", axis=d, tiled=True, axis_index_groups=sets)
            for a, d in zip(params, DIMS, strict=True)
        )
    (memory, wq, bq, wk, wv, bv, wo, bo, ga, sa, wu, bu, wd, bd, gb, sb) = params
    r, fr = wq.shape[0], wd.shape[0]
    mem_rows = memory.shape[0]

    vecs = [a.reshape(1, r) for a in (bq, bv, bo, ga, sa, bd, gb, sb)]
    out, dx, sums, tiny, _ = layer_call(
        count, sub, mem_rows, lengths, inputs, cotangent, wq, wk, wv, wo, wu, wd, memory.T,
        bu.reshape(1, fr), vecs,
    )
    layer_out, dx, gwq, gwk, gwv, gwo, gwu, gwd, gmem, gbu, *vecs = results_call(
        r, fr, mem_rows, wu.shape[1], out, dx, sums, tiny
    )
    gmem = gmem.T
    gbu = gbu.reshape(fr)
    gbq, gbv, gbo, gga, gsa, gbd, ggb, gsb = [a.reshape(r) for a in vecs]
    grads = (gmem, gwq, gbq, gwk, gwv, gbv, gwo, gbo, gga, gsa, gwu, gbu, gwd, gbd, ggb, gsb)
    if sub > 1:
        grads = tuple(
            lax.psum_scatter(a, "dp", scatter_dimension=d, tiled=True, axis_index_groups=sets)
            for a, d in zip(grads, DIMS, strict=True)
        )
    return (layer_out, dx) + grads


def solution(mesh):
    rows, row, mem = P("dp", None), P("dp"), P(None, "dp")
    full = P("dp", None, None)
    params = (mem, rows, row, rows, rows, row, rows, row, row, row, rows, row, rows, row, row, row)
    return jax.shard_map(
        functools.partial(on_device, mesh.shape["dp"]),
        mesh=mesh,
        in_specs=(full, P("dp")) + params + (full,),
        out_specs=(full, full) + params,
        check_vma=False,
    )
```
